128 devices in a mesh: space: 32 (over z_hi, y, x), band: 4 (over z_lo, core).
Axes of the slice: x: 4, y: 4, z: 4 (z_hi: 2, z_lo: 2; z = z_hi * 2 + z_lo), core: 2. Of those that a mesh axis runs over, the one named last changes fastest.
Arguments:
- wavefunctions: float32 [256, 324000], P('band', 'space'), may hold values from -6 to 6
- stiffness: float32 [125, 125], replicated, as said below
- cell_scale: float32 [3840], P('space'), may hold values from 0.5 to 2
- cell_potential: float32 [3840], P('space'), may hold values from 0.5 to 4
- connectivity: int32 [125, 3840], P(None, 'space'), may hold values from 0 to 10124, as said below
- lower_face: int32 [64800], P('space'), may hold values from 0 to 10124, as said below
- upper_face: int32 [64800], P('space'), may hold values from 0 to 10124, as said below
Outputs:
- rotated_waves: float32 [256, 324000], P('band', 'space')
The draws below stay inside these ranges and needn't reach their ends.
Inputs may be any that keep to these rules, and one draw needn't show every extreme that they name: `connectivity`: each column of a device's block lists the 125 distinct local nodes of one cell of a structured degree-4 hexahedral grid of 1 x 20 x 6 cells whose nodes are numbered in an arbitrary order; every local node belongs to some cell. A device's lower_face lists the 2025 distinct local nodes on its face towards the device below; the lists of one device are disjoint from each other. A device's upper_face lists the 2025 distinct local nodes on its face towards the device above, entry i being the same slab node as entry i of the next device's lower_face. `stiffness`: symmetric with a dominant diagonal.
All inputs are finite; a program needn't handle non-finite values.
Results may differ from the reference program's by a relative error of at most 0.00012.
Values sent between devices are 32-bit elements; how exact they have to be, the bound alone decides.
A program may use at most 128 MiB of HBM per device.

```python
import math
import jax
import jax.numpy as jnp
from jax import lax

BANDS = 256
NODES_CELL = 125
FILTER_DEG = 4
CX = 1
CY = 20
CZ = 6
CELLS_DEV = 120
NODES_DEV = 10125
FACE = 2025
CELLS = 3840
NODES = 324000
FACES = 64800
OWNED = 261225
N_SPACE = 32
N_BAND = 4


def node_layout(key):
    device_count = CELLS // CELLS_DEV
    span_y = 4 * CY + 1
    span_z = 4 * CZ + 1

    def one_device(position):
        return jax.random.permutation(jax.random.fold_in(key, position), NODES_DEV).astype(jnp.int32)
    numbering = jax.vmap(one_device)(jnp.arange(device_count))
    corner = jnp.arange(5)
    cell_x = jnp.arange(CX)
    cell_y = jnp.arange(CY)
    cell_z = jnp.arange(CZ)
    along_x = 4 * cell_x[None, None, None, :, None, None] + corner[:, None, None, None, None, None]
    along_y = 4 * cell_y[None, None, None, None, :, None] + corner[None, :, None, None, None, None]
    along_z = 4 * cell_z[None, None, None, None, None, :] + corner[None, None, :, None, None, None]
    geometry = ((along_x * span_y + along_y) * span_z + along_z).reshape(NODES_CELL, CELLS_DEV)
    connect = jnp.take(numbering, geometry, axis=1)
    connect = connect.transpose(1, 0, 2).reshape(NODES_CELL, CELLS)
    face_ids = jnp.arange(FACE)
    lower = jnp.take(numbering, face_ids, axis=1).reshape(FACES)
    upper = jnp.take(numbering, face_ids + 4 * CX * span_y * span_z, axis=1).reshape(FACES)
    return (connect.astype(jnp.int32), lower.astype(jnp.int32), upper.astype(jnp.int32))


def draw_connectivity(key, part):
    return node_layout(key)[0]


def draw_lower_face(key, part):
    return node_layout(key)[1]


def draw_upper_face(key, part):
    return node_layout(key)[2]


def draw_stiffness(key, part):
    key = jax.random.fold_in(key, 7)
    spread = 0.015
    entries = jax.random.uniform(key, (NODES_CELL, NODES_CELL), jnp.float32, -spread, spread)
    return (entries + entries.T) * 0.5 + jnp.eye(NODES_CELL, dtype=jnp.float32)


def block_scale(stream_key, dims, split, least, largest):
    level = 1.0
    for axis_at, blocks in split:
        steps = jax.random.uniform(jax.random.fold_in(jax.random.fold_in(stream_key, 6), axis_at), (blocks,), jnp.float32, least / len(split), largest / len(split))
        level = level * jnp.repeat(jnp.exp(steps), dims[axis_at] // blocks).reshape((-1,) + (1,) * (len(dims) - 1 - axis_at))
    return level


def noise(rng, dims, scale, limit, shards=(), kind=jnp.bfloat16):
    result = jax.random.normal(rng, dims, jnp.float32) * scale
    if len(shards) > 0:
        result = block_scale(rng, dims, shards, -0.22, 0.18) * result
    return jnp.clip(result, min=-limit, max=limit).astype(kind)


def setup_inputs(seed: int = 0) -> dict:
    streams_of = jax.random.split(jax.random.key(seed), 8)
    return {
        "wavefunctions": noise(streams_of[0], (BANDS, NODES), 1.0, 6.0, ((0, 4), (1, 32)), jnp.float32),
        "stiffness": draw_stiffness(jax.random.fold_in(streams_of[7], 71), 0),
        "cell_scale": jnp.clip(jnp.exp(math.log(2.0) - 1.3862944 * jax.random.uniform(streams_of[2], (CELLS,), jnp.float32) ** block_scale(streams_of[2], (CELLS,), ((0, 32),), -0.2, 0.2)), 0.5, 2.0),
        "cell_potential": jnp.clip(jnp.exp(math.log(4.0) - 2.0794415 * jax.random.uniform(streams_of[3], (CELLS,), jnp.float32) ** block_scale(streams_of[3], (CELLS,), ((0, 32),), -0.2, 0.2)), 0.5, 4.0),
        "connectivity": draw_connectivity(jax.random.fold_in(streams_of[7], 71), 0),
        "lower_face": draw_lower_face(jax.random.fold_in(streams_of[7], 71), 0),
        "upper_face": draw_upper_face(jax.random.fold_in(streams_of[7], 71), 0),
    }


GLL_WEIGHTS = (0.1, 49.0 / 90.0, 32.0 / 45.0, 49.0 / 90.0, 0.1)
CENTER = 11.0
HALF_WIDTH = 9.0
HIGHEST = lax.Precision.HIGHEST

def lumped_mass():
    weights = jnp.array(GLL_WEIGHTS, jnp.float32)
    return (weights[:, None, None] * weights[None, :, None] * weights[None, None, :]).reshape(-1)

def cell_apply(values, connectivity, cell_scale, cell_potential, stiffness):
    gathered = jnp.take(values, connectivity, axis=1)
    stiff_part = jnp.einsum('lm,bmc->blc', stiffness, gathered, precision=HIGHEST)
    products = stiff_part * cell_scale + lumped_mass()[:, None] * cell_potential * gathered
    return jnp.zeros_like(values).at[:, connectivity].add(products)

def take_faces(values, faces):
    return values[:, faces]

def add_faces(values, faces, extra):
    return values.at[:, faces].add(extra)

def set_faces(values, faces, extra):
    return values.at[:, faces].set(extra)

def zero_faces(row_values, faces, keeping):
    return row_values.at[faces].multiply(keeping)

def shifted_up(values):
    return jnp.concatenate([jnp.zeros_like(values[:1]), values[:-1]], 0)

def shifted_down(values):
    return jnp.concatenate([values[1:], jnp.zeros_like(values[:1])], 0)

def reference(wavefunctions, stiffness, cell_scale, cell_potential, connectivity, lower_face, upper_face):
    width = BANDS // N_BAND
    waves = wavefunctions.reshape(N_BAND, width, N_SPACE, NODES_DEV).transpose(0, 2, 1, 3)
    conns = connectivity.reshape(NODES_CELL, N_SPACE, CELLS_DEV).transpose(1, 0, 2)
    scales = cell_scale.reshape(N_SPACE, CELLS_DEV)
    potentials = cell_potential.reshape(N_SPACE, CELLS_DEV)
    lowers = lower_face.reshape(N_SPACE, FACE)
    uppers = upper_face.reshape(N_SPACE, FACE)
    inner = (jnp.arange(N_SPACE) > 0)[:, None, None]

    def operate(values):
        summed = jax.vmap(cell_apply, in_axes=(0, 0, 0, 0, None))(values, conns, scales, potentials, stiffness)
        upward = jax.vmap(take_faces)(summed, uppers)
        downward = jax.vmap(take_faces)(summed, lowers)
        summed = jax.vmap(add_faces)(summed, lowers, shifted_up(upward))
        return jax.vmap(add_faces)(summed, uppers, shifted_down(downward))

    def filter_group(values):
        own_lower = jax.vmap(take_faces)(values, lowers)
        owner = shifted_up(jax.vmap(take_faces)(values, uppers))
        values = jax.vmap(set_faces)(values, lowers, jnp.where(inner, owner, own_lower))
        previous = values
        current = (operate(values) - CENTER * values) / HALF_WIDTH
        for repeat in range(FILTER_DEG - 1):
            following = 2.0 / HALF_WIDTH * (operate(current) - CENTER * current) - previous
            previous, current = (current, following)
        return current
    filtered = lax.map(filter_group, waves)
    columns = filtered.transpose(0, 2, 1, 3).reshape(BANDS, NODES)
    keeping = jnp.where(jnp.arange(N_SPACE) > 0, 0.0, 1.0).astype(jnp.float32)
    weights = jax.vmap(zero_faces)(jnp.ones((N_SPACE, NODES_DEV), jnp.float32), lowers, keeping).reshape(NODES)
    margin = jnp.einsum('an,bn->ab', columns * weights, columns, precision=HIGHEST) / OWNED
    factor = jnp.linalg.cholesky(margin)
    return lax.linalg.triangular_solve(factor, columns, left_side=True, lower=True)
```

```python
import functools

import jax
import jax.numpy as jnp
import numpy as np
from jax import lax
from jax.experimental import pallas as pl
from jax.experimental.pallas import tpu as pltpu
from jax.sharding import PartitionSpec as P

FILTER_DEG = 4
GLL_WEIGHTS = (0.1, 49.0 / 90.0, 32.0 / 45.0, 49.0 / 90.0, 0.1)
CENTER = 11.0
HALF_WIDTH = 9.0
HIGHEST = lax.Precision.HIGHEST
MESH = pl.DeviceIdType.MESH

CELLS_Y = 20
CELLS_Z = 6
CHUNKS = CELLS_Y // 2
TILES = CHUNKS * CELLS_Z
SLOTS = 2 * TILES
HALF = 64
LANES = 128
ROWS = 160
PLANE = 32
PACKED = 2 * TILES + CELLS_Z + CHUNKS + 1


def plane_rows():
    rows = {(0, 0): 0, (4, 0): 8, (0, 4): 16, (4, 4): 24}
    for k in (1, 2, 3):
        rows[(0, k)] = k
        rows[(4, k)] = 8 + k
        rows[(k, 0)] = 3 + k
        rows[(k, 4)] = 16 + 3 + k
    rows[(1, 1)] = 7
    for k in (1, 2, 3):
        rows[(2, k)] = 8 + 3 + k
        rows[(3, k)] = 16 + k
    rows[(1, 2)] = 24 + 1
    rows[(1, 3)] = 24 + 7
    return rows


def local_rows():
    rows = plane_rows()
    return [PLANE * a + rows[(b, c)] for a in range(5) for b in range(5) for c in range(5)]


LOCAL_ROWS = local_rows()


def row_selector():
    chosen = np.zeros((ROWS, 125), np.float32)
    chosen[LOCAL_ROWS, np.arange(125)] = 1.0
    return chosen


def row_mass():
    weights = np.array(GLL_WEIGHTS, np.float32)
    mass = (weights[:, None, None] * weights[None, :, None] * weights[None, None, :]).reshape(-1)
    spread = np.zeros((ROWS, LANES), np.float32)
    spread[LOCAL_ROWS, :] = mass[:, None]
    return spread


def local(a, b, c):
    return 25 * a + 5 * b + c


def exact_dot(x, y):
    return jnp.dot(x, y, precision=HIGHEST, preferred_element_type=jnp.float32)


def chain_counts(before, doublings):
    size = before.shape[0]
    eye = (
        lax.broadcasted_iota(jnp.int32, (size, size), 0) == lax.broadcasted_iota(jnp.int32, (size, size), 1)
    ).astype(jnp.float32)
    total, power = eye + before, before
    for _ in range(doublings):
        power = jnp.dot(power, power, preferred_element_type=jnp.float32)
        total = total + jnp.dot(total, power, preferred_element_type=jnp.float32)
    return jnp.sum(total, axis=0, keepdims=True) - 1.0


def layout_kernel(conn_ref, coef_ref, stiff_ref, select_ref, index_ref, scale_ref, potential_ref, stiffness_ref):
    conn = conn_ref[...].astype(jnp.float32)
    cells = conn.shape[1]
    on_rows = lax.broadcasted_iota(jnp.int32, (cells, cells), 0)
    on_lanes = lax.broadcasted_iota(jnp.int32, (cells, cells), 1)

    def as_column(row):
        return jnp.sum(jnp.where(on_rows == on_lanes, row, 0.0), axis=1, keepdims=True)

    def row_of(node):
        return conn[node : node + 1, :]

    after_z = (as_column(row_of(local(2, 2, 4))) == row_of(local(2, 2, 0))).astype(jnp.float32)
    after_y = (as_column(row_of(local(2, 4, 2))) == row_of(local(2, 0, 2))).astype(jnp.float32)
    at_z = chain_counts(after_z, 2)
    at_y = chain_counts(after_y, 4)
    upper_half = at_y >= CHUNKS
    tile = (at_y - jnp.where(upper_half, 1.0 * CHUNKS, 0.0)) * CELLS_Z + at_z
    slot = 2.0 * tile + jnp.where(upper_half, 1.0, 0.0)
    moved = (as_column(slot) == on_lanes.astype(jnp.float32)).astype(jnp.float32)
    index_ref[...] = (exact_dot(conn, moved) + 0.5).astype(jnp.int32)

    wanted = lax.broadcasted_iota(jnp.int32, (TILES, cells), 0).astype(jnp.float32)
    lane = lax.broadcasted_iota(jnp.int32, (TILES, LANES), 1)

    def spread(row):
        low, high = [
            jnp.sum(jnp.where(slot == 2.0 * wanted + half, row, 0.0), axis=1, keepdims=True) for half in (0.0, 1.0)
        ]
        return jnp.where(lane < HALF, low, high)

    scale_ref[...] = spread(coef_ref[0:1, :])
    potential_ref[...] = spread(coef_ref[1:2, :])

    select = select_ref[...]
    part = exact_dot(select, stiff_ref[...])
    stiff = lax.dot_general(
        part, select, (((1,), (1,)), ((), ())), precision=HIGHEST, preferred_element_type=jnp.float32
    )
    high = stiff.astype(jnp.bfloat16)
    low = (stiff - high.astype(jnp.float32)).astype(jnp.bfloat16)
    stiffness_ref[...] = jnp.concatenate([high, high, low], axis=1)


def make_layout(connectivity, coefficients, stiffness):
    cells = connectivity.shape[1]
    whole = pl.BlockSpec(memory_space=pltpu.VMEM)
    return pl.pallas_call(
        layout_kernel,
        out_shape=(
            jax.ShapeDtypeStruct((125, cells), jnp.int32),
            jax.ShapeDtypeStruct((TILES, LANES), jnp.float32),
            jax.ShapeDtypeStruct((TILES, LANES), jnp.float32),
            jax.ShapeDtypeStruct((ROWS, 3 * ROWS), jnp.bfloat16),
        ),
        in_specs=[whole] * 4,
        out_specs=(whole,) * 4,
        name="layout",
    )(connectivity, coefficients, stiffness, row_selector())


def gather_kernel(index_ref, waves_ref, cells_ref):
    low_half = lax.broadcasted_iota(jnp.int32, (1, LANES), 1) < HALF
    cells_ref[...] = jnp.zeros_like(cells_ref)

    def body(t, carry):
        for node, row in enumerate(LOCAL_ROWS):
            first = waves_ref[pl.ds(index_ref[node, 2 * t], 1), :]
            second = waves_ref[pl.ds(index_ref[node, 2 * t + 1], 1), :]
            cells_ref[t, row : row + 1, :] = jnp.where(low_half, first, second)
        return carry

    lax.fori_loop(0, TILES, body, 0)


def gather_cells(index, doubled):
    return pl.pallas_call(
        gather_kernel,
        out_shape=jax.ShapeDtypeStruct((TILES, ROWS, LANES), jnp.float32),
        in_specs=[pl.BlockSpec(memory_space=pltpu.SMEM), pl.BlockSpec(memory_space=pltpu.VMEM)],
        out_specs=pl.BlockSpec(memory_space=pltpu.VMEM),
        compiler_params=pltpu.CompilerParams(vmem_limit_bytes=40 * 2**20),
        name="gather_cells",
    )(index, doubled)


def scatter_kernel(index_ref, cells_ref, nodes_ref, rows_ref):
    lane = lax.broadcasted_iota(jnp.int32, (ROWS, LANES), 1)
    row_at = lax.broadcasted_iota(jnp.int32, (ROWS, LANES), 0)
    inner = lax.axis_index("space") > 0
    weight = jnp.where((lane >= HALF) & (row_at < PLANE) & inner, 0.0, 1.0)

    def body(t, carry):
        values = cells_ref[t]
        turned = pltpu.roll(values, HALF, 1)
        rows_ref[0] = jnp.where(lane < HALF, values, turned) * weight
        rows_ref[1] = jnp.where(lane < HALF, turned, values) * weight
        for node, row in enumerate(LOCAL_ROWS):
            nodes_ref[pl.ds(index_ref[node, 2 * t], 1), :] = rows_ref[0, row : row + 1, :]
            nodes_ref[pl.ds(index_ref[node, 2 * t + 1], 1), :] = rows_ref[1, row : row + 1, :]
        return carry

    lax.fori_loop(0, TILES, body, 0)


def scatter_nodes(index, cells, node_count):
    return pl.pallas_call(
        scatter_kernel,
        out_shape=jax.ShapeDtypeStruct((node_count, LANES), jnp.float32),
        in_specs=[pl.BlockSpec(memory_space=pltpu.SMEM), pl.BlockSpec(memory_space=pltpu.VMEM)],
        out_specs=pl.BlockSpec(memory_space=pltpu.VMEM),
        scratch_shapes=[pltpu.VMEM((2, ROWS, LANES), jnp.float32)],
        compiler_params=pltpu.CompilerParams(vmem_limit_bytes=40 * 2**20),
        name="scatter_nodes",
    )(index, cells)


def filter_kernel(
    start_ref, stiff_ref, mass_ref, scale_ref, potential_ref, out_ref,
    other, product, face, halves, sends, receives, send_sems, receive_sems,
):
    count = lax.axis_size("space")
    me = lax.axis_index("space")
    above, below = lax.rem(me + 1, count), lax.rem(me + count - 1, count)
    has_below, has_above = me > 0, me < count - 1

    barrier = pltpu.get_barrier_semaphore()
    for neighbour in (below, above):
        pl.semaphore_signal(barrier, inc=1, device_id={"space": neighbour}, device_id_type=MESH)
    pl.semaphore_wait(barrier, 2)

    sub = lax.broadcasted_iota(jnp.int32, (8, LANES), 0)
    lane = lax.broadcasted_iota(jnp.int32, (8, LANES), 1)
    corner = sub == 0
    along_y = sub <= 3
    along_z = corner | ((sub >= 4) & (sub <= 6))
    in_z_group = (sub >= 1) & (sub <= 3)
    in_y_group = (sub >= 4) & (sub <= 6)
    low_half = lane < HALF

    def copy(step, way):
        return pltpu.make_async_remote_copy(
            src_ref=sends.at[way],
            dst_ref=receives.at[step, way],
            send_sem=send_sems.at[step, way],
            recv_sem=receive_sems.at[step, way],
            device_id={"space": above if way == 0 else below},
            device_id_type=MESH,
        )

    def groups(ref, t, first):
        return [ref[t, first + 8 * g : first + 8 * g + 8, :] for g in range(4)]

    def pack(way, c, tiles):
        for z, (a, b, y, d) in enumerate(tiles):
            t = c * CELLS_Z + z
            sends[way, 2 * t] = a
            inside = jnp.where(in_z_group, y, jnp.where(in_y_group, b, d))
            sends[way, 2 * t + 1] = jnp.where(corner, pltpu.roll(d, 7, 0), inside)
        sends[way, 2 * TILES + CELLS_Z + c] = tiles[CELLS_Z - 1][2]

        @pl.when(c == CHUNKS - 1)
        def _():
            for z in range(CELLS_Z):
                sends[way, 2 * TILES + z] = tiles[z][1]
            sends[way, PACKED - 1] = tiles[CELLS_Z - 1][3]

    def unpack(step, way, c, z):
        t = c * CELLS_Z + z
        a = receives[step, way, 2 * t]
        inside = receives[step, way, 2 * t + 1]
        turned = pltpu.roll(inside, 1, 0)
        b = jnp.where(in_y_group, inside, receives[step, way, 2 * TILES + z])
        y = jnp.where(in_z_group, inside, receives[step, way, 2 * TILES + CELLS_Z + c])
        d = jnp.where(sub == 7, inside, jnp.where(sub == 1, turned, receives[step, way, PACKED - 1]))
        return [a, b, y, d]

    def fill(ref, first):
        def body(c, carry):
            nxt = lax.rem(c + 1, CHUNKS)
            last = c == CHUNKS - 1
            shared = jnp.logical_or(jnp.logical_not(last), low_half)

            def from_next(value):
                return jnp.where(last, pltpu.roll(value, HALF, 1), value)

            tiles = [groups(ref, c * CELLS_Z + z, first) for z in range(CELLS_Z)]
            b_new = []
            for z in range(CELLS_Z):
                ahead = from_next(ref[nxt * CELLS_Z + z, first : first + 8, :])
                b_new.append(jnp.where(along_y & shared, ahead, tiles[z][1]))
            for z in range(CELLS_Z):
                t = c * CELLS_Z + z
                ref[t, first + 8 : first + 16, :] = b_new[z]
                if z < CELLS_Z - 1:
                    ref[t, first + 16 : first + 24, :] = jnp.where(along_z, tiles[z + 1][0], tiles[z][2])
                    ref[t, first + 24 : first + 32, :] = jnp.where(corner, b_new[z + 1], tiles[z][3])
                else:
                    ahead = from_next(ref[nxt * CELLS_Z + z, first + 16 : first + 24, :])
                    ref[t, first + 24 : first + 32, :] = jnp.where(corner & shared, ahead, tiles[z][3])
            return carry

        lax.fori_loop(0, CHUNKS, body, 0)

    def assembled(c, first):
        prv = lax.rem(c + CHUNKS - 1, CHUNKS)
        is_first = c == 0

        def from_previous(value):
            return jnp.where(is_first, jnp.where(low_half, 0.0, pltpu.roll(value, HALF, 1)), value)

        tiles = [groups(product, c * CELLS_Z + z, first) for z in range(CELLS_Z)]
        for z in range(CELLS_Z):
            _, b, _, d = groups(product, prv * CELLS_Z + z, first)
            tiles[z][0] = tiles[z][0] + jnp.where(along_y, from_previous(b), 0.0)
            tiles[z][2] = tiles[z][2] + jnp.where(corner, from_previous(d), 0.0)
        for z in range(1, CELLS_Z):
            tiles[z][0] = tiles[z][0] + jnp.where(along_z, tiles[z - 1][2], 0.0)
            tiles[z][1] = tiles[z][1] + jnp.where(corner, tiles[z - 1][3], 0.0)
        return tiles

    def chunk_of(ref, c, rows):
        return jnp.concatenate([ref[c * CELLS_Z + z, rows, :] for z in range(CELLS_Z)], axis=1)

    def multiply(current, parts, split):
        stiff = jnp.concatenate([stiff_ref[part, :] for part in parts], axis=0)
        mass = jnp.concatenate([mass_ref[part, :] for part in parts], axis=0)

        def body(c, carry):
            if split:
                x = chunk_of(current, c, slice(0, ROWS))
                high = x.astype(jnp.bfloat16)
                low = (x - high.astype(jnp.float32)).astype(jnp.bfloat16)
                halves[c, 0:ROWS, :] = high
                halves[c, ROWS : 2 * ROWS, :] = low
            else:
                high = halves[c, 0:ROWS, :]
                low = halves[c, ROWS : 2 * ROWS, :]
            operand = jnp.concatenate([high, low, high], axis=0)
            result = jnp.dot(stiff, operand, preferred_element_type=jnp.float32)
            for z in range(CELLS_Z):
                t = c * CELLS_Z + z
                values = jnp.concatenate([current[t, part, :] for part in parts], axis=0)
                term = result[:, z * LANES : (z + 1) * LANES] * scale_ref[pl.ds(t, 1), :] + (
                    mass * potential_ref[pl.ds(t, 1), :] * values
                )
                at = 0
                for part in parts:
                    size = part.stop - part.start
                    product[t, part, :] = term[at : at + size]
                    at += size
            return carry

        lax.fori_loop(0, CHUNKS, body, 0)

    def advanced(step, current, previous, t, rows, total):
        value = total - CENTER * current[t, rows, :]
        if step == 0:
            return value * (1.0 / HALF_WIDTH)
        return value * (2.0 / HALF_WIDTH) - previous[t, rows, :]

    def advance_inner(step, current, previous, first):
        def body(c, carry):
            tiles = assembled(c, first)
            for z in range(CELLS_Z):
                t = c * CELLS_Z + z
                for g in range(4):
                    rows = slice(first + 8 * g, first + 8 * g + 8)
                    previous[t, rows, :] = advanced(step, current, previous, t, rows, tiles[z][g])
            return carry

        lax.fori_loop(0, CHUNKS, body, 0)
        fill(previous, first)

    def send_face(way, first):
        def body(c, carry):
            tiles = assembled(c, first)
            for z in range(CELLS_Z):
                for g in range(4):
                    face[way, c * CELLS_Z + z, 8 * g : 8 * g + 8, :] = tiles[z][g]
            pack(way, c, tiles)
            return carry

        lax.fori_loop(0, CHUNKS, body, 0)

    def advance_face(step, current, previous, way, first, valid):
        def body(c, carry):
            for z in range(CELLS_Z):
                t = c * CELLS_Z + z
                arrived = unpack(step + 1, way, c, z)
                for g in range(4):
                    rows = slice(first + 8 * g, first + 8 * g + 8)
                    total = face[1 - way, t, 8 * g : 8 * g + 8, :] + jnp.where(valid, arrived[g], 0.0)
                    previous[t, rows, :] = advanced(step, current, previous, t, rows, total)
            return carry

        lax.fori_loop(0, CHUNKS, body, 0)
        fill(previous, first)

    top = 4 * PLANE

    def pack_start(c, carry):
        pack(0, c, [groups(start_ref, c * CELLS_Z + z, top) for z in range(CELLS_Z)])
        return carry

    lax.fori_loop(0, CHUNKS, pack_start, 0)
    owner = copy(0, 0)
    owner.start()
    out_ref[...] = start_ref[...]
    owner.wait()

    def take_owner(c, carry):
        for z in range(CELLS_Z):
            t = c * CELLS_Z + z
            arrived = unpack(0, 0, c, z)
            for g in range(4):
                rows = slice(8 * g, 8 * g + 8)
                out_ref[t, rows, :] = jnp.where(has_below, arrived[g], out_ref[t, rows, :])
        return carry

    lax.fori_loop(0, CHUNKS, take_owner, 0)
    fill(out_ref, 0)

    for step in range(FILTER_DEG):
        current, previous = (out_ref, other) if step % 2 == 0 else (other, out_ref)
        multiply(current, [slice(0, PLANE), slice(top, ROWS)], True)
        copies = [copy(step + 1, 0), copy(step + 1, 1)]
        for way, first in ((0, top), (1, 0)):
            send_face(way, first)
            copies[way].start()
        multiply(current, [slice(PLANE, top)], False)
        for a in range(1, 4):
            advance_inner(step, current, previous, PLANE * a)
        copies[0].wait()
        advance_face(step, current, previous, 0, 0, has_below)
        copies[1].wait()
        advance_face(step, current, previous, 1, top, has_above)


def filter_cells(start, stiff, scale, potential):
    whole = pl.BlockSpec(memory_space=pltpu.VMEM)
    cells = (TILES, ROWS, LANES)
    rounds = FILTER_DEG + 1
    return pl.pallas_call(
        filter_kernel,
        out_shape=jax.ShapeDtypeStruct(cells, jnp.float32),
        in_specs=[whole] * 5,
        out_specs=whole,
        scratch_shapes=[
            pltpu.VMEM(cells, jnp.float32),
            pltpu.VMEM(cells, jnp.float32),
            pltpu.VMEM((2, TILES, PLANE, LANES), jnp.float32),
            pltpu.VMEM((CHUNKS, 2 * ROWS, CELLS_Z * LANES), jnp.bfloat16),
            pltpu.VMEM((2, PACKED, 8, LANES), jnp.float32),
            pltpu.VMEM((rounds, 2, PACKED, 8, LANES), jnp.float32),
            pltpu.SemaphoreType.DMA((rounds, 2)),
            pltpu.SemaphoreType.DMA((rounds, 2)),
        ],
        compiler_params=pltpu.CompilerParams(
            collective_id=0, has_side_effects=True, vmem_limit_bytes=56 * 2**20
        ),
        name="filter_cells",
    )(start, stiff, row_mass(), scale, potential)


def inverse_factor(margin, order):
    factor = jnp.linalg.cholesky(margin)
    return lax.linalg.triangular_solve(
        factor, jnp.eye(order, dtype=margin.dtype), left_side=True, lower=True
    )


def shards(
    wavefunctions, stiffness, cell_scale, cell_potential, connectivity, lower_face, upper_face
):
    width, node_count = wavefunctions.shape
    face_count = lower_face.shape[0]
    space_count = lax.axis_size("space")
    band_count = lax.axis_size("band")
    total_bands = width * band_count
    owned_count = node_count * space_count - face_count * (space_count - 1)

    coefficients = jnp.stack([cell_scale, cell_potential])
    index, scale, potential, stiff = make_layout(connectivity, coefficients, stiffness)
    doubled = jnp.concatenate([wavefunctions, wavefunctions], axis=0).T
    cells = gather_cells(index, doubled)
    cells = filter_cells(cells, stiff, scale, potential)
    nodes = scatter_nodes(index, cells, node_count)
    current, weighted = nodes[:, :width].T, nodes[:, width:].T

    everything = lax.all_gather(current, "band", axis=0, tiled=True)
    blocks = jnp.einsum("bn,kn->bk", weighted, everything, precision=HIGHEST)
    row_panel = lax.psum(blocks, "space")
    margin = lax.all_gather(row_panel, "band", axis=0, tiled=True) / owned_count
    inverse = inverse_factor(margin, total_bands)
    my_panel = lax.dynamic_slice_in_dim(inverse, lax.axis_index("band") * width, width, 0)
    return jnp.dot(my_panel, everything, precision=HIGHEST)


def solution(mesh):
    placed = (
        P("band", "space"),
        P(),
        P("space"),
        P("space"),
        P(None, "space"),
        P("space"),
        P("space"),
    )
    return jax.shard_map(
        shards, mesh=mesh, in_specs=placed, out_specs=P("band", "space"), check_vma=False
    )
```

```python
import functools

import jax
import jax.numpy as jnp
import numpy as np
from jax import lax
from jax.experimental import pallas as pl
from jax.experimental.pallas import tpu as pltpu
from jax.sharding import PartitionSpec as P

FILTER_DEG = 4
GLL_WEIGHTS = (0.1, 49.0 / 90.0, 32.0 / 45.0, 49.0 / 90.0, 0.1)
CENTER = 11.0
HALF_WIDTH = 9.0
HIGHEST = lax.Precision.HIGHEST
MESH = pl.DeviceIdType.MESH

CELLS_Y = 20
CELLS_Z = 6
CHUNKS = CELLS_Y // 2
TILES = CHUNKS * CELLS_Z
SLOTS = 2 * TILES
HALF = 64
LANES = 128
ROWS = 160
PLANE = 32
PACKED = 2 * TILES + CELLS_Z + CHUNKS + 1

NODES = 10125
PAIRS = 5120
BLOCK = 256
BANDS_DEV = 64
N_BAND = 4


def plane_rows():
    rows = {(0, 0): 0, (4, 0): 8, (0, 4): 16, (4, 4): 24}
    for k in (1, 2, 3):
        rows[(0, k)] = k
        rows[(4, k)] = 8 + k
        rows[(k, 0)] = 3 + k
        rows[(k, 4)] = 16 + 3 + k
    rows[(1, 1)] = 7
    for k in (1, 2, 3):
        rows[(2, k)] = 8 + 3 + k
        rows[(3, k)] = 16 + k
    rows[(1, 2)] = 24 + 1
    rows[(1, 3)] = 24 + 7
    return rows


def local_rows():
    rows = plane_rows()
    return [PLANE * a + rows[(b, c)] for a in range(5) for b in range(5) for c in range(5)]


LOCAL_ROWS = local_rows()


def row_selector():
    chosen = np.zeros((ROWS, 125), np.float32)
    chosen[LOCAL_ROWS, np.arange(125)] = 1.0
    return chosen


def row_mass():
    weights = np.array(GLL_WEIGHTS, np.float32)
    mass = (weights[:, None, None] * weights[None, :, None] * weights[None, None, :]).reshape(-1)
    spread = np.zeros((ROWS, LANES), np.float32)
    spread[LOCAL_ROWS, :] = mass[:, None]
    return spread


def local(a, b, c):
    return 25 * a + 5 * b + c


def exact_dot(x, y):
    return jnp.dot(x, y, precision=HIGHEST, preferred_element_type=jnp.float32)


def chain_counts(before, doublings):
    size = before.shape[0]
    eye = (
        lax.broadcasted_iota(jnp.int32, (size, size), 0) == lax.broadcasted_iota(jnp.int32, (size, size), 1)
    ).astype(jnp.float32)
    total, power = eye + before, before
    for _ in range(doublings):
        power = jnp.dot(power, power, preferred_element_type=jnp.float32)
        total = total + jnp.dot(total, power, preferred_element_type=jnp.float32)
    return jnp.sum(total, axis=0, keepdims=True) - 1.0


def layout_kernel(conn_ref, coef_ref, stiff_ref, select_ref, index_ref, scale_ref, potential_ref, stiffness_ref):
    conn = conn_ref[...].astype(jnp.float32)
    cells = conn.shape[1]
    on_rows = lax.broadcasted_iota(jnp.int32, (cells, cells), 0)
    on_lanes = lax.broadcasted_iota(jnp.int32, (cells, cells), 1)

    def as_column(row):
        return jnp.sum(jnp.where(on_rows == on_lanes, row, 0.0), axis=1, keepdims=True)

    def row_of(node):
        return conn[node : node + 1, :]

    after_z = (as_column(row_of(local(2, 2, 4))) == row_of(local(2, 2, 0))).astype(jnp.float32)
    after_y = (as_column(row_of(local(2, 4, 2))) == row_of(local(2, 0, 2))).astype(jnp.float32)
    at_z = chain_counts(after_z, 2)
    at_y = chain_counts(after_y, 4)
    upper_half = at_y >= CHUNKS
    tile = (at_y - jnp.where(upper_half, 1.0 * CHUNKS, 0.0)) * CELLS_Z + at_z
    slot = 2.0 * tile + jnp.where(upper_half, 1.0, 0.0)
    moved = (as_column(slot) == on_lanes.astype(jnp.float32)).astype(jnp.float32)
    index_ref[...] = (exact_dot(conn, moved) + 0.5).astype(jnp.int32)

    wanted = lax.broadcasted_iota(jnp.int32, (TILES, cells), 0).astype(jnp.float32)
    lane = lax.broadcasted_iota(jnp.int32, (TILES, LANES), 1)

    def spread(row):
        low, high = [
            jnp.sum(jnp.where(slot == 2.0 * wanted + half, row, 0.0), axis=1, keepdims=True) for half in (0.0, 1.0)
        ]
        return jnp.where(lane < HALF, low, high)

    scale_ref[...] = spread(coef_ref[0:1, :])
    potential_ref[...] = spread(coef_ref[1:2, :])

    select = select_ref[...]
    part = exact_dot(select, stiff_ref[...])
    stiff = lax.dot_general(
        part, select, (((1,), (1,)), ((), ())), precision=HIGHEST, preferred_element_type=jnp.float32
    )
    high = stiff.astype(jnp.bfloat16)
    low = (stiff - high.astype(jnp.float32)).astype(jnp.bfloat16)
    stiffness_ref[...] = jnp.concatenate([high, high, low], axis=1)


def make_layout(connectivity, coefficients, stiffness):
    cells = connectivity.shape[1]
    whole = pl.BlockSpec(memory_space=pltpu.VMEM)
    return pl.pallas_call(
        layout_kernel,
        out_shape=(
            jax.ShapeDtypeStruct((125, cells), jnp.int32),
            jax.ShapeDtypeStruct((TILES, LANES), jnp.float32),
            jax.ShapeDtypeStruct((TILES, LANES), jnp.float32),
            jax.ShapeDtypeStruct((ROWS, 3 * ROWS), jnp.bfloat16),
        ),
        in_specs=[whole] * 4,
        out_specs=(whole,) * 4,
        name="layout",
    )(connectivity, coefficients, stiffness, row_selector())


def gather_kernel(index_ref, waves_ref, cells_ref):
    low_half = lax.broadcasted_iota(jnp.int32, (1, LANES), 1) < HALF
    cells_ref[...] = jnp.zeros_like(cells_ref)

    def body(t, carry):
        for node, row in enumerate(LOCAL_ROWS):
            first = waves_ref[pl.ds(index_ref[node, 2 * t], 1), :]
            second = waves_ref[pl.ds(index_ref[node, 2 * t + 1], 1), :]
            cells_ref[t, row : row + 1, :] = jnp.where(low_half, first, second)
        return carry

    lax.fori_loop(0, TILES, body, 0)


def gather_cells(index, doubled):
    return pl.pallas_call(
        gather_kernel,
        out_shape=jax.ShapeDtypeStruct((TILES, ROWS, LANES), jnp.float32),
        in_specs=[pl.BlockSpec(memory_space=pltpu.SMEM), pl.BlockSpec(memory_space=pltpu.VMEM)],
        out_specs=pl.BlockSpec(memory_space=pltpu.VMEM),
        compiler_params=pltpu.CompilerParams(vmem_limit_bytes=40 * 2**20),
        name="gather_cells",
    )(index, doubled)


def scatter_kernel(index_ref, cells_ref, packed_ref, weight_ref, nodes_ref, rows_ref):
    lane = lax.broadcasted_iota(jnp.int32, (ROWS, LANES), 1)
    row_at = lax.broadcasted_iota(jnp.int32, (ROWS, LANES), 0)
    inner = lax.axis_index("space") > 0
    weight = jnp.where((row_at < PLANE) & inner, 0.0, 1.0)
    nodes_ref[NODES - NODES % 8 :, :] = jnp.zeros((2 * PAIRS - NODES + NODES % 8, LANES), jnp.float32)

    def body(t, carry):
        values = cells_ref[t]
        turned = pltpu.roll(values, HALF, 1)
        rows_ref[0] = jnp.where(lane < HALF, values, weight)
        rows_ref[1] = jnp.where(lane < HALF, turned, weight)
        for node, row in enumerate(LOCAL_ROWS):
            nodes_ref[pl.ds(index_ref[node, 2 * t], 1), :] = rows_ref[0, row : row + 1, :]
            nodes_ref[pl.ds(index_ref[node, 2 * t + 1], 1), :] = rows_ref[1, row : row + 1, :]
        return carry

    lax.fori_loop(0, TILES, body, 0)
    low_half = lax.broadcasted_iota(jnp.int32, (BLOCK, LANES), 1) < HALF

    def pack(i, carry):
        first = nodes_ref[pl.ds(pl.multiple_of(i * BLOCK, BLOCK), BLOCK), :]
        second = nodes_ref[pl.ds(pl.multiple_of(PAIRS + i * BLOCK, BLOCK), BLOCK), :]
        rows = pl.ds(pl.multiple_of(i * BLOCK, BLOCK), BLOCK)
        packed_ref[rows, :] = jnp.where(low_half, first, pltpu.roll(second, HALF, 1))
        weight_ref[rows, :] = jnp.where(low_half, pltpu.roll(first, HALF, 1), second)
        return carry

    lax.fori_loop(0, PAIRS // BLOCK, pack, 0)


def scatter_nodes(index, cells):
    whole = pl.BlockSpec(memory_space=pltpu.VMEM)
    packed = jax.ShapeDtypeStruct((PAIRS, LANES), jnp.float32)
    return pl.pallas_call(
        scatter_kernel,
        out_shape=(packed, packed),
        in_specs=[pl.BlockSpec(memory_space=pltpu.SMEM), whole],
        out_specs=(whole, whole),
        scratch_shapes=[
            pltpu.VMEM((2 * PAIRS, LANES), jnp.float32),
            pltpu.VMEM((2, ROWS, LANES), jnp.float32),
        ],
        compiler_params=pltpu.CompilerParams(vmem_limit_bytes=40 * 2**20),
        name="scatter_nodes",
    )(index, cells)


def filter_kernel(
    start_ref, stiff_ref, mass_ref, scale_ref, potential_ref, out_ref,
    other, product, face, halves, sends, receives, send_sems, receive_sems,
):
    count = lax.axis_size("space")
    me = lax.axis_index("space")
    above, below = lax.rem(me + 1, count), lax.rem(me + count - 1, count)
    has_below, has_above = me > 0, me < count - 1

    barrier = pltpu.get_barrier_semaphore()
    for neighbour in (below, above):
        pl.semaphore_signal(barrier, inc=1, device_id={"space": neighbour}, device_id_type=MESH)
    pl.semaphore_wait(barrier, 2)

    sub = lax.broadcasted_iota(jnp.int32, (8, LANES), 0)
    lane = lax.broadcasted_iota(jnp.int32, (8, LANES), 1)
    corner = sub == 0
    along_y = sub <= 3
    along_z = corner | ((sub >= 4) & (sub <= 6))
    in_z_group = (sub >= 1) & (sub <= 3)
    in_y_group = (sub >= 4) & (sub <= 6)
    low_half = lane < HALF

    def copy(step, way):
        return pltpu.make_async_remote_copy(
            src_ref=sends.at[way],
            dst_ref=receives.at[step, way],
            send_sem=send_sems.at[step, way],
            recv_sem=receive_sems.at[step, way],
            device_id={"space": above if way == 0 else below},
            device_id_type=MESH,
        )

    def groups(ref, t, first):
        return [ref[t, first + 8 * g : first + 8 * g + 8, :] for g in range(4)]

    def pack(way, c, tiles):
        for z, (a, b, y, d) in enumerate(tiles):
            t = c * CELLS_Z + z
            sends[way, 2 * t] = a
            inside = jnp.where(in_z_group, y, jnp.where(in_y_group, b, d))
            sends[way, 2 * t + 1] = jnp.where(corner, pltpu.roll(d, 7, 0), inside)
        sends[way, 2 * TILES + CELLS_Z + c] = tiles[CELLS_Z - 1][2]

        @pl.when(c == CHUNKS - 1)
        def _():
            for z in range(CELLS_Z):
                sends[way, 2 * TILES + z] = tiles[z][1]
            sends[way, PACKED - 1] = tiles[CELLS_Z - 1][3]

    def unpack(step, way, c, z):
        t = c * CELLS_Z + z
        a = receives[step, way, 2 * t]
        inside = receives[step, way, 2 * t + 1]
        turned = pltpu.roll(inside, 1, 0)
        b = jnp.where(in_y_group, inside, receives[step, way, 2 * TILES + z])
        y = jnp.where(in_z_group, inside, receives[step, way, 2 * TILES + CELLS_Z + c])
        d = jnp.where(sub == 7, inside, jnp.where(sub == 1, turned, receives[step, way, PACKED - 1]))
        return [a, b, y, d]

    def fill(ref, first):
        def body(c, carry):
            nxt = lax.rem(c + 1, CHUNKS)
            last = c == CHUNKS - 1
            shared = jnp.logical_or(jnp.logical_not(last), low_half)

            def from_next(value):
                return jnp.where(last, pltpu.roll(value, HALF, 1), value)

            tiles = [groups(ref, c * CELLS_Z + z, first) for z in range(CELLS_Z)]
            b_new = []
            for z in range(CELLS_Z):
                ahead = from_next(ref[nxt * CELLS_Z + z, first : first + 8, :])
                b_new.append(jnp.where(along_y & shared, ahead, tiles[z][1]))
            for z in range(CELLS_Z):
                t = c * CELLS_Z + z
                ref[t, first + 8 : first + 16, :] = b_new[z]
                if z < CELLS_Z - 1:
                    ref[t, first + 16 : first + 24, :] = jnp.where(along_z, tiles[z + 1][0], tiles[z][2])
                    ref[t, first + 24 : first + 32, :] = jnp.where(corner, b_new[z + 1], tiles[z][3])
                else:
                    ahead = from_next(ref[nxt * CELLS_Z + z, first + 16 : first + 24, :])
                    ref[t, first + 24 : first + 32, :] = jnp.where(corner & shared, ahead, tiles[z][3])
            return carry

        lax.fori_loop(0, CHUNKS, body, 0)

    def assembled(c, first):
        prv = lax.rem(c + CHUNKS - 1, CHUNKS)
        is_first = c == 0

        def from_previous(value):
            return jnp.where(is_first, jnp.where(low_half, 0.0, pltpu.roll(value, HALF, 1)), value)

        tiles = [groups(product, c * CELLS_Z + z, first) for z in range(CELLS_Z)]
        for z in range(CELLS_Z):
            _, b, _, d = groups(product, prv * CELLS_Z + z, first)
            tiles[z][0] = tiles[z][0] + jnp.where(along_y, from_previous(b), 0.0)
            tiles[z][2] = tiles[z][2] + jnp.where(corner, from_previous(d), 0.0)
        for z in range(1, CELLS_Z):
            tiles[z][0] = tiles[z][0] + jnp.where(along_z, tiles[z - 1][2], 0.0)
            tiles[z][1] = tiles[z][1] + jnp.where(corner, tiles[z - 1][3], 0.0)
        return tiles

    def chunk_of(ref, c, rows):
        return jnp.concatenate([ref[c * CELLS_Z + z, rows, :] for z in range(CELLS_Z)], axis=1)

    def multiply(current, parts, split):
        stiff = jnp.concatenate([stiff_ref[part, :] for part in parts], axis=0)
        mass = jnp.concatenate([mass_ref[part, :] for part in parts], axis=0)

        def body(c, carry):
            if split:
                x = chunk_of(current, c, slice(0, ROWS))
                high = x.astype(jnp.bfloat16)
                low = (x - high.astype(jnp.float32)).astype(jnp.bfloat16)
                halves[c, 0:ROWS, :] = high
                halves[c, ROWS : 2 * ROWS, :] = low
            else:
                high = halves[c, 0:ROWS, :]
                low = halves[c, ROWS : 2 * ROWS, :]
            operand = jnp.concatenate([high, low, high], axis=0)
            result = jnp.dot(stiff, operand, preferred_element_type=jnp.float32)
            for z in range(CELLS_Z):
                t = c * CELLS_Z + z
                values = jnp.concatenate([current[t, part, :] for part in parts], axis=0)
                term = result[:, z * LANES : (z + 1) * LANES] * scale_ref[pl.ds(t, 1), :] + (
                    mass * potential_ref[pl.ds(t, 1), :] * values
                )
                at = 0
                for part in parts:
                    size = part.stop - part.start
                    product[t, part, :] = term[at : at + size]
                    at += size
            return carry

        lax.fori_loop(0, CHUNKS, body, 0)

    def advanced(step, current, previous, t, rows, total):
        value = total - CENTER * current[t, rows, :]
        if step == 0:
            return value * (1.0 / HALF_WIDTH)
        return value * (2.0 / HALF_WIDTH) - previous[t, rows, :]

    def advance_inner(step, current, previous, first):
        def body(c, carry):
            tiles = assembled(c, first)
            for z in range(CELLS_Z):
                t = c * CELLS_Z + z
                for g in range(4):
                    rows = slice(first + 8 * g, first + 8 * g + 8)
                    previous[t, rows, :] = advanced(step, current, previous, t, rows, tiles[z][g])
            return carry

        lax.fori_loop(0, CHUNKS, body, 0)
        fill(previous, first)

    def send_face(way, first):
        def body(c, carry):
            tiles = assembled(c, first)
            for z in range(CELLS_Z):
                for g in range(4):
                    face[way, c * CELLS_Z + z, 8 * g : 8 * g + 8, :] = tiles[z][g]
            pack(way, c, tiles)
            return carry

        lax.fori_loop(0, CHUNKS, body, 0)

    def advance_face(step, current, previous, way, first, valid):
        def body(c, carry):
            for z in range(CELLS_Z):
                t = c * CELLS_Z + z
                arrived = unpack(step + 1, way, c, z)
                for g in range(4):
                    rows = slice(first + 8 * g, first + 8 * g + 8)
                    total = face[1 - way, t, 8 * g : 8 * g + 8, :] + jnp.where(valid, arrived[g], 0.0)
                    previous[t, rows, :] = advanced(step, current, previous, t, rows, total)
            return carry

        lax.fori_loop(0, CHUNKS, body, 0)
        fill(previous, first)

    top = 4 * PLANE

    def pack_start(c, carry):
        pack(0, c, [groups(start_ref, c * CELLS_Z + z, top) for z in range(CELLS_Z)])
        return carry

    lax.fori_loop(0, CHUNKS, pack_start, 0)
    owner = copy(0, 0)
    owner.start()
    out_ref[...] = start_ref[...]
    owner.wait()

    def take_owner(c, carry):
        for z in range(CELLS_Z):
            t = c * CELLS_Z + z
            arrived = unpack(0, 0, c, z)
            for g in range(4):
                rows = slice(8 * g, 8 * g + 8)
                out_ref[t, rows, :] = jnp.where(has_below, arrived[g], out_ref[t, rows, :])
        return carry

    lax.fori_loop(0, CHUNKS, take_owner, 0)
    fill(out_ref, 0)

    for step in range(FILTER_DEG):
        current, previous = (out_ref, other) if step % 2 == 0 else (other, out_ref)
        multiply(current, [slice(0, PLANE), slice(top, ROWS)], True)
        copies = [copy(step + 1, 0), copy(step + 1, 1)]
        for way, first in ((0, top), (1, 0)):
            send_face(way, first)
            copies[way].start()
        multiply(current, [slice(PLANE, top)], False)
        for a in range(1, 4):
            advance_inner(step, current, previous, PLANE * a)
        copies[0].wait()
        advance_face(step, current, previous, 0, 0, has_below)
        copies[1].wait()
        advance_face(step, current, previous, 1, top, has_above)


def filter_cells(start, stiff, scale, potential):
    whole = pl.BlockSpec(memory_space=pltpu.VMEM)
    cells = (TILES, ROWS, LANES)
    rounds = FILTER_DEG + 1
    return pl.pallas_call(
        filter_kernel,
        out_shape=jax.ShapeDtypeStruct(cells, jnp.float32),
        in_specs=[whole] * 5,
        out_specs=whole,
        scratch_shapes=[
            pltpu.VMEM(cells, jnp.float32),
            pltpu.VMEM(cells, jnp.float32),
            pltpu.VMEM((2, TILES, PLANE, LANES), jnp.float32),
            pltpu.VMEM((CHUNKS, 2 * ROWS, CELLS_Z * LANES), jnp.bfloat16),
            pltpu.VMEM((2, PACKED, 8, LANES), jnp.float32),
            pltpu.VMEM((rounds, 2, PACKED, 8, LANES), jnp.float32),
            pltpu.SemaphoreType.DMA((rounds, 2)),
            pltpu.SemaphoreType.DMA((rounds, 2)),
        ],
        compiler_params=pltpu.CompilerParams(
            collective_id=0, has_side_effects=True, vmem_limit_bytes=56 * 2**20
        ),
        name="filter_cells",
    )(start, stiff, row_mass(), scale, potential)


def split(x):
    high = x.astype(jnp.bfloat16)
    return high, (x - high.astype(jnp.float32)).astype(jnp.bfloat16)


def exact_dot_t(x, y):
    return lax.dot_general(
        x, y, (((1,), (1,)), ((), ())), precision=HIGHEST, preferred_element_type=jnp.float32
    )


def inverse_of_block(block):
    size = BANDS_DEV
    row_at = lax.broadcasted_iota(jnp.int32, (size, LANES), 0)
    lane = lax.broadcasted_iota(jnp.int32, (size, LANES), 1)
    wide = jnp.concatenate([block, jnp.zeros((size, LANES - size), jnp.float32)], axis=1)
    wide = jnp.where(lane == row_at + size, 1.0, wide)
    tiles = [wide[8 * g : 8 * g + 8] for g in range(size // 8)]
    sub = lax.broadcasted_iota(jnp.int32, (8, LANES), 0)
    for j in range(size):
        home, at = divmod(j, 8)
        columns = [jnp.broadcast_to(tile[:, j : j + 1], (8, LANES)) for tile in tiles[home:]]
        row = tiles[home][at : at + 1, :]
        ratio = row * (1.0 / columns[0][at : at + 1, :])
        for g in range(home, size // 8):
            factor = columns[g - home]
            if g == home:
                factor = jnp.where(sub > at, factor, 0.0)
            tiles[g] = tiles[g] - factor * ratio
    wide = jnp.concatenate(tiles, axis=0)
    pivots = jnp.sum(jnp.where(lane == row_at, wide, 0.0), axis=1, keepdims=True)
    return wide[:, size:] * (1.0 / jnp.sqrt(pivots))


def finish_kernel(
    owned, own, weight, out, partner, cross, partner_cross, sums, by_x, by_y, line, piece, by_z, reduced, everyone,
    inverse, pair_sems, cross_sems, forward_sems, x_sems, y_sems, z_sems, y_back_sems, x_back_sems, band_sems,
):
    space, band = lax.axis_index("space"), lax.axis_index("band")
    at_x = lax.rem(space, 4)
    at_y = lax.rem(space // 4, 4)
    core = lax.rem(band, 2)
    chip = band // 2
    mate = band + 1 - 2 * core
    across = lax.rem(band + 2, N_BAND)
    across_mate = lax.rem(mate + 2, N_BAND)

    def x_peer(k):
        return {"space": space - at_x + lax.rem(at_x + k, 4)}

    def y_peer(k):
        return {"space": space - 4 * at_y + 4 * lax.rem(at_y + k, 4)}

    z_peer = {"space": lax.rem(space + 16, 32)}

    peers = [x_peer(k) for k in (1, 2, 3)] + [y_peer(k) for k in (1, 2, 3)] + [z_peer]
    peers += [{"band": lax.rem(band + k, N_BAND)} for k in (1, 2, 3)]
    barrier = pltpu.get_barrier_semaphore()
    for peer in peers:
        pl.semaphore_signal(barrier, inc=1, device_id=peer, device_id_type=MESH)
    pl.semaphore_wait(barrier, len(peers))

    def send(source, target, sems, slot, peer):
        return pltpu.make_async_remote_copy(
            src_ref=source,
            dst_ref=target,
            send_sem=sems.at[0, slot],
            recv_sem=sems.at[1, slot],
            device_id=peer,
            device_id_type=MESH,
        )

    half = PAIRS // 2
    mine_first = pl.ds(pl.multiple_of(chip * half, half), half)
    mine_second = pl.ds(pl.multiple_of((1 - chip) * half, half), half)
    to_mate, to_across = {"band": mate}, {"band": across}
    pair = send(own, partner, pair_sems, 0, to_mate)
    first = send(own.at[mine_first], cross.at[mine_first], cross_sems, 0, to_across)
    second = send(own.at[mine_second], cross.at[mine_second], cross_sems, 1, to_across)
    forward_first = send(cross.at[mine_second], partner_cross.at[mine_second], forward_sems, 0, to_mate)
    forward_second = send(cross.at[mine_first], partner_cross.at[mine_first], forward_sems, 1, to_mate)
    first.start()
    pair.start()
    pair.wait()

    def products(left, right):
        left_high, left_low = split(left)
        right_high, right_low = split(right)
        return lax.dot_general(
            jnp.concatenate([left_high, left_high, left_low], axis=0),
            jnp.concatenate([right_high, right_low, right_high], axis=0),
            (((0,), (0,)), ((), ())),
            preferred_element_type=jnp.float32,
        )

    def block_rows(i):
        return pl.ds(pl.multiple_of(i * BLOCK, BLOCK), BLOCK)

    def own_terms(i, total):
        rows = block_rows(i)
        mine = own[rows, :]
        return total + products(mine * weight[rows, :], jnp.concatenate([mine, partner[rows, :]], axis=1))

    def cross_terms(i, total):
        rows = block_rows(i + (1 - chip) * (half // BLOCK))
        scale = weight[rows, :]
        return total + products(
            cross[rows, :], jnp.concatenate([own[rows, :] * scale, partner[rows, :] * scale], axis=1)
        )

    low_half = lax.broadcasted_iota(jnp.int32, (BANDS_DEV, LANES), 1) < HALF

    def fold(total):
        size = BANDS_DEV
        left = total[:size, :LANES] + pltpu.roll(total[size:, :LANES], HALF, 1)
        right = pltpu.roll(total[:size, LANES:], HALF, 1) + total[size:, LANES:]
        return jnp.where(low_half, left, right)

    zero = jnp.zeros((LANES, 2 * LANES), jnp.float32)
    sums[0:BANDS_DEV, :] = fold(lax.fori_loop(0, PAIRS // BLOCK, own_terms, zero))
    first.wait()
    second.start()
    forward_first.start()
    sums[BANDS_DEV : 2 * BANDS_DEV, :] = fold(lax.fori_loop(0, half // BLOCK, cross_terms, zero))

    def rows_of(at, size):
        return pl.ds(pl.multiple_of(at, size), size)

    to_x = [
        send(sums.at[rows_of(32 * lax.rem(at_x + k, 4), 32)], by_x.at[k - 1], x_sems, k - 1, x_peer(k)) for k in (1, 2, 3)
    ]
    for step in to_x:
        step.start()
    for step in to_x:
        step.wait()
    line[...] = sums[rows_of(32 * at_x, 32), :] + by_x[0] + by_x[1] + by_x[2]
    to_y = [
        send(line.at[rows_of(8 * lax.rem(at_y + k, 4), 8)], by_y.at[k - 1], y_sems, k - 1, y_peer(k)) for k in (1, 2, 3)
    ]
    for step in to_y:
        step.start()
    for step in to_y:
        step.wait()
    piece[...] = line[rows_of(8 * at_y, 8), :] + by_y[0] + by_y[1] + by_y[2]
    to_z = send(piece, by_z, z_sems, 0, z_peer)
    to_z.start()
    to_z.wait()
    small = rows_of(32 * at_x + 8 * at_y, 8)
    reduced[small, :] = piece[...] + by_z[...]
    back_y = [send(reduced.at[small], reduced.at[small], y_back_sems, k - 1, y_peer(k)) for k in (1, 2, 3)]
    for step in back_y:
        step.start()
    for step in back_y:
        step.wait()
    large = rows_of(32 * at_x, 32)
    back_x = [send(reduced.at[large], reduced.at[large], x_back_sems, k - 1, x_peer(k)) for k in (1, 2, 3)]
    for step in back_x:
        step.start()
    for step in back_x:
        step.wait()
    to_band = [
        send(reduced, everyone.at[band], band_sems, k - 1, {"band": lax.rem(band + k, N_BAND)}) for k in (1, 2, 3)
    ]
    for step in to_band:
        step.start()
    everyone[band] = reduced[...]
    for step in to_band:
        step.wait()

    def part(b, r, c):
        size = BANDS_DEV
        return everyone[b, r * size : (r + 1) * size, c * size : (c + 1) * size] * (1.0 / owned)

    margin = {(b, b): part(b, 0, 0) for b in range(N_BAND)}
    margin[1, 0], margin[3, 2] = part(1, 0, 1), part(3, 0, 1)
    margin[2, 0] = part(0, 1, 0) + part(2, 1, 0).T
    margin[2, 1] = part(0, 1, 1) + part(3, 1, 1).T
    margin[3, 0] = part(1, 1, 1) + part(2, 1, 1).T
    margin[3, 1] = part(1, 1, 0) + part(3, 1, 0).T

    inverses, factor, whole = [], {}, {}
    for k in range(N_BAND):
        diagonal = inverse_of_block(margin[k, k])
        inverses.append(diagonal)
        for i in range(k + 1, N_BAND):
            factor[i, k] = exact_dot_t(margin[i, k], diagonal)
        for i in range(k + 1, N_BAND):
            for j in range(k + 1, i + 1):
                margin[i, j] = margin[i, j] - exact_dot_t(factor[i, k], factor[j, k])
        whole[k, k] = diagonal
        for j in range(k):
            total = exact_dot(factor[k, j], whole[j, j])
            for m in range(j + 1, k):
                total = total + exact_dot(factor[k, m], whole[m, j])
            whole[k, j] = -exact_dot(diagonal, total)
        if k == 2:
            second.wait()
            forward_second.start()
    padding = jnp.zeros((BANDS_DEV, LANES - BANDS_DEV), jnp.float32)
    for i in range(N_BAND):
        for j in range(N_BAND):
            if j <= i:
                inverse[i, j] = jnp.concatenate([whole[i, j], padding], axis=1)
            else:
                inverse[i, j] = jnp.zeros((BANDS_DEV, LANES), jnp.float32)
    forward_first.wait()
    forward_second.wait()

    panels = [inverse[band, source] for source in (band, mate, across, across_mate)]
    left = jnp.concatenate(
        [
            jnp.concatenate(panels, axis=1),
            jnp.concatenate([pltpu.roll(panel, HALF, 1) for panel in panels], axis=1),
        ],
        axis=0,
    )
    left_high, left_low = split(left)
    left = jnp.concatenate([left_high, left_high, left_low], axis=1)

    def rotate(i, carry):
        rows = block_rows(i)
        right = jnp.concatenate([ref[rows, :] for ref in (own, partner, cross, partner_cross)], axis=1)
        right_high, right_low = split(right)
        rotated = lax.dot_general(
            left,
            jnp.concatenate([right_high, right_low, right_high], axis=1),
            (((1,), (1,)), ((), ())),
            preferred_element_type=jnp.float32,
        )
        out[:, rows] = rotated[:BANDS_DEV]
        out[:, pl.ds(pl.multiple_of(PAIRS + i * BLOCK, BLOCK), BLOCK)] = rotated[BANDS_DEV:]
        return carry

    lax.fori_loop(0, PAIRS // BLOCK, rotate, 0)


def finish(packed, weight, owned_count):
    whole = pl.BlockSpec(memory_space=pltpu.VMEM)
    nodes = pltpu.VMEM((PAIRS, LANES), jnp.float32)

    def small(*shape):
        return pltpu.VMEM(shape, jnp.float32)

    def sems(slots):
        return pltpu.SemaphoreType.DMA((2, slots))

    return pl.pallas_call(
        functools.partial(finish_kernel, owned_count),
        out_shape=jax.ShapeDtypeStruct((BANDS_DEV, 2 * PAIRS), jnp.float32),
        in_specs=[whole, whole],
        out_specs=whole,
        scratch_shapes=[
            nodes, nodes, nodes,
            small(LANES, LANES), small(3, 32, LANES), small(3, 8, LANES), small(32, LANES), small(8, LANES),
            small(8, LANES), small(LANES, LANES), small(N_BAND, LANES, LANES),
            small(N_BAND, N_BAND, BANDS_DEV, LANES),
            sems(1), sems(2), sems(2), sems(3), sems(3), sems(1), sems(3), sems(3), sems(3),
        ],
        compiler_params=pltpu.CompilerParams(
            collective_id=1, has_side_effects=True, vmem_limit_bytes=48 * 2**20
        ),
        name="finish",
    )(packed, weight)


def shards(
    wavefunctions, stiffness, cell_scale, cell_potential, connectivity, lower_face, upper_face
):
    node_count = wavefunctions.shape[1]
    face_count = lower_face.shape[0]
    space_count = lax.axis_size("space")
    owned_count = node_count * space_count - face_count * (space_count - 1)

    coefficients = jnp.stack([cell_scale, cell_potential])
    index, scale, potential, stiff = make_layout(connectivity, coefficients, stiffness)
    doubled = jnp.concatenate([wavefunctions, wavefunctions], axis=0).T
    cells = gather_cells(index, doubled)
    cells = filter_cells(cells, stiff, scale, potential)
    packed, weight = scatter_nodes(index, cells)
    return finish(packed, weight, owned_count)[:, :node_count]


def solution(mesh):
    placed = (
        P("band", "space"),
        P(),
        P("space"),
        P("space"),
        P(None, "space"),
        P("space"),
        P("space"),
    )
    return jax.shard_map(
        shards, mesh=mesh, in_specs=placed, out_specs=P("band", "space"), check_vma=False
    )
```

```python
import functools

import jax
import jax.numpy as jnp
import numpy as np
from jax import lax
from jax.experimental import pallas as pl
from jax.experimental.pallas import tpu as pltpu
from jax.sharding import PartitionSpec as P

FILTER_DEG = 4
GLL_WEIGHTS = (0.1, 49.0 / 90.0, 32.0 / 45.0, 49.0 / 90.0, 0.1)
CENTER = 11.0
HALF_WIDTH = 9.0
HIGHEST = lax.Precision.HIGHEST
MESH = pl.DeviceIdType.MESH

CELLS_Y = 20
CELLS_Z = 6
CHUNKS = CELLS_Y // 2
TILES = CHUNKS * CELLS_Z
SLOTS = 2 * TILES
HALF = 64
LANES = 128
ROWS = 128
PLANE = 24
CORNERS = 5 * PLANE
PACKED = 2 * TILES + CELLS_Z + CHUNKS + 1

NODES = 10125
PAIRS = 5120
BLOCK = 256
BANDS_DEV = 64
N_BAND = 4


def row_of_node(a, b, c):
    if (b, c) == (4, 4):
        return CORNERS + a
    rows = {(0, 0): 0, (4, 0): 8, (0, 4): 16, (1, 1): 7, (1, 2): 15, (1, 3): 23}
    for k in (1, 2, 3):
        rows[(0, k)] = k
        rows[(4, k)] = 8 + k
        rows[(k, 0)] = 3 + k
        rows[(k, 4)] = 16 + 3 + k
        rows[(2, k)] = 8 + 3 + k
        rows[(3, k)] = 16 + k
    return PLANE * a + rows[(b, c)]


def node_rows(planes, chosen):
    return [
        (25 * a + 5 * b + c, row_of_node(a, b, c))
        for a in planes for b in range(5) for c in range(5) if chosen(b, c)
    ]


LOCAL_ROWS = [row for _, row in node_rows(range(5), lambda b, c: True)]


def row_selector():
    chosen = np.zeros((ROWS, 125), np.float32)
    chosen[LOCAL_ROWS, np.arange(125)] = 1.0
    return chosen


def row_mass():
    weights = np.array(GLL_WEIGHTS, np.float32)
    mass = (weights[:, None, None] * weights[None, :, None] * weights[None, None, :]).reshape(-1)
    spread = np.zeros((ROWS, LANES), np.float32)
    spread[LOCAL_ROWS, :] = mass[:, None]
    return spread


def local(a, b, c):
    return 25 * a + 5 * b + c


def exact_dot(x, y):
    return jnp.dot(x, y, precision=HIGHEST, preferred_element_type=jnp.float32)


def chain_counts(before, doublings):
    size = before.shape[0]
    eye = (
        lax.broadcasted_iota(jnp.int32, (size, size), 0) == lax.broadcasted_iota(jnp.int32, (size, size), 1)
    ).astype(jnp.float32)
    total, power = eye + before, before
    for _ in range(doublings):
        power = jnp.dot(power, power, preferred_element_type=jnp.float32)
        total = total + jnp.dot(total, power, preferred_element_type=jnp.float32)
    return jnp.sum(total, axis=0, keepdims=True) - 1.0


def layout_kernel(conn_ref, coef_ref, stiff_ref, select_ref, index_ref, scale_ref, potential_ref, stiffness_ref):
    conn = conn_ref[...].astype(jnp.float32)
    cells = conn.shape[1]
    on_rows = lax.broadcasted_iota(jnp.int32, (cells, cells), 0)
    on_lanes = lax.broadcasted_iota(jnp.int32, (cells, cells), 1)

    def as_column(row):
        return jnp.sum(jnp.where(on_rows == on_lanes, row, 0.0), axis=1, keepdims=True)

    def row_of(node):
        return conn[node : node + 1, :]

    after_z = (as_column(row_of(local(2, 2, 4))) == row_of(local(2, 2, 0))).astype(jnp.float32)
    after_y = (as_column(row_of(local(2, 4, 2))) == row_of(local(2, 0, 2))).astype(jnp.float32)
    at_z = chain_counts(after_z, 2)
    at_y = chain_counts(after_y, 4)
    upper_half = at_y >= CHUNKS
    tile = (at_y - jnp.where(upper_half, 1.0 * CHUNKS, 0.0)) * CELLS_Z + at_z
    slot = 2.0 * tile + jnp.where(upper_half, 1.0, 0.0)
    moved = (as_column(slot) == on_lanes.astype(jnp.float32)).astype(jnp.float32)
    index_ref[...] = (exact_dot(conn, moved) + 0.5).astype(jnp.int32)

    wanted = lax.broadcasted_iota(jnp.int32, (TILES, cells), 0).astype(jnp.float32)
    lane = lax.broadcasted_iota(jnp.int32, (TILES, LANES), 1)

    def spread(row):
        low, high = [
            jnp.sum(jnp.where(slot == 2.0 * wanted + half, row, 0.0), axis=1, keepdims=True) for half in (0.0, 1.0)
        ]
        return jnp.where(lane < HALF, low, high)

    scale_ref[...] = spread(coef_ref[0:1, :])
    potential_ref[...] = spread(coef_ref[1:2, :])

    select = select_ref[...]
    part = exact_dot(select, stiff_ref[...])
    stiff = lax.dot_general(
        part, select, (((1,), (1,)), ((), ())), precision=HIGHEST, preferred_element_type=jnp.float32
    )
    high = stiff.astype(jnp.bfloat16)
    low = (stiff - high.astype(jnp.float32)).astype(jnp.bfloat16)
    stiffness_ref[...] = jnp.concatenate(
        [jnp.concatenate([high, high], axis=1), jnp.concatenate([low, low], axis=1)], axis=0
    )


def make_layout(connectivity, coefficients, stiffness):
    cells = connectivity.shape[1]
    whole = pl.BlockSpec(memory_space=pltpu.VMEM)
    return pl.pallas_call(
        layout_kernel,
        out_shape=(
            jax.ShapeDtypeStruct((125, cells), jnp.int32),
            jax.ShapeDtypeStruct((TILES, LANES), jnp.float32),
            jax.ShapeDtypeStruct((TILES, LANES), jnp.float32),
            jax.ShapeDtypeStruct((2 * ROWS, 2 * ROWS), jnp.bfloat16),
        ),
        in_specs=[whole] * 4,
        out_specs=(whole,) * 4,
        name="layout",
    )(connectivity, coefficients, stiffness, row_selector())


def each_node_once(planes, visit):
    def loop(count, tile_of, nodes):
        def body(i, carry):
            visit(tile_of(i), nodes)
            return carry

        lax.fori_loop(0, count, body, 0)

    loop(TILES, lambda i: i, node_rows(planes, lambda b, c: b < 4 and c < 4))
    loop(CELLS_Z, lambda i: TILES - CELLS_Z + i, node_rows(planes, lambda b, c: b == 4))
    loop(CHUNKS, lambda i: i * CELLS_Z + CELLS_Z - 1, node_rows(planes, lambda b, c: b < 4 and c == 4))


def scatter_kernel(index_ref, cells_ref, packed_ref, weight_ref, nodes_ref, rows_ref):
    lane = lax.broadcasted_iota(jnp.int32, (ROWS, LANES), 1)
    row_at = lax.broadcasted_iota(jnp.int32, (ROWS, LANES), 0)
    inner = lax.axis_index("space") > 0
    weight = jnp.where(((row_at < PLANE) | (row_at == CORNERS)) & inner, 0.0, 1.0)
    nodes_ref[NODES - NODES % 8 :, :] = jnp.zeros((2 * PAIRS - NODES + NODES % 8, LANES), jnp.float32)

    def visit(t, nodes):
        values = cells_ref[t]
        turned = pltpu.roll(values, HALF, 1)
        rows_ref[0] = jnp.where(lane < HALF, values, weight)
        rows_ref[1] = jnp.where(lane < HALF, turned, weight)
        for node, row in nodes:
            nodes_ref[pl.ds(index_ref[node, 2 * t], 1), :] = rows_ref[0, row : row + 1, :]
            nodes_ref[pl.ds(index_ref[node, 2 * t + 1], 1), :] = rows_ref[1, row : row + 1, :]

    each_node_once(range(5), visit)
    low_half = lax.broadcasted_iota(jnp.int32, (BLOCK, LANES), 1) < HALF

    def pack(i, carry):
        first = nodes_ref[pl.ds(pl.multiple_of(i * BLOCK, BLOCK), BLOCK), :]
        second = nodes_ref[pl.ds(pl.multiple_of(PAIRS + i * BLOCK, BLOCK), BLOCK), :]
        rows = pl.ds(pl.multiple_of(i * BLOCK, BLOCK), BLOCK)
        packed_ref[rows, :] = jnp.where(low_half, first, pltpu.roll(second, HALF, 1))
        weight_ref[rows, :] = jnp.where(low_half, pltpu.roll(first, HALF, 1), second)
        return carry

    lax.fori_loop(0, PAIRS // BLOCK, pack, 0)


def scatter_nodes(index, cells):
    whole = pl.BlockSpec(memory_space=pltpu.VMEM)
    packed = jax.ShapeDtypeStruct((PAIRS, LANES), jnp.float32)
    return pl.pallas_call(
        scatter_kernel,
        out_shape=(packed, packed),
        in_specs=[pl.BlockSpec(memory_space=pltpu.SMEM), whole],
        out_specs=(whole, whole),
        scratch_shapes=[
            pltpu.VMEM((2 * PAIRS, LANES), jnp.float32),
            pltpu.VMEM((2, ROWS, LANES), jnp.float32),
        ],
        compiler_params=pltpu.CompilerParams(vmem_limit_bytes=40 * 2**20),
        name="scatter_nodes",
    )(index, cells)


def filter_kernel(
    index_ref, waves_ref, stiff_ref, mass_ref, scale_ref, potential_ref, out_ref,
    other, product, face, doubled, sends, receives, send_sems, receive_sems,
):
    count = lax.axis_size("space")
    me = lax.axis_index("space")
    above, below = lax.rem(me + 1, count), lax.rem(me + count - 1, count)
    has_below, has_above = me > 0, me < count - 1

    barrier = pltpu.get_barrier_semaphore()
    for neighbour in (below, above):
        pl.semaphore_signal(barrier, inc=1, device_id={"space": neighbour}, device_id_type=MESH)
    pl.semaphore_wait(barrier, 2)

    sub = lax.broadcasted_iota(jnp.int32, (8, LANES), 0)
    lane = lax.broadcasted_iota(jnp.int32, (8, LANES), 1)
    corner = sub == 0
    along_y = sub <= 3
    along_z = corner | ((sub >= 4) & (sub <= 6))
    in_y_group = (sub >= 4) & (sub <= 6)
    in_z_group = ((sub >= 1) & (sub <= 3)) | (sub == 7)
    low_half = lane < HALF
    corners = slice(CORNERS, CORNERS + 8)
    last_tile = TILES - 1
    bottom, top = 0, 4
    inner = (1, 2, 3)

    def group(a, g):
        return slice(PLANE * a + 8 * g, PLANE * a + 8 * g + 8)

    def turn(value, by):
        return pltpu.roll(value, by % 8, 0) if by % 8 else value

    def over_chunks(body):
        def step(c, carry):
            body(c)
            return carry

        lax.fori_loop(0, CHUNKS, step, 0)

    def copy(step, way):
        return pltpu.make_async_remote_copy(
            src_ref=sends.at[way],
            dst_ref=receives.at[step, way],
            send_sem=send_sems.at[step, way],
            recv_sem=receive_sems.at[step, way],
            device_id={"space": above if way == 0 else below},
            device_id_type=MESH,
        )

    def pack(way, c, tiles):
        for z, (own, y, d) in enumerate(tiles):
            t = c * CELLS_Z + z
            sends[way, 2 * t] = own
            sends[way, 2 * t + 1] = jnp.where(corner, turn(y, 1), jnp.where(in_y_group, y, d))
        sends[way, 2 * TILES + CELLS_Z + c] = tiles[CELLS_Z - 1][2]

        @pl.when(c == CHUNKS - 1)
        def _():
            for z in range(CELLS_Z):
                sends[way, 2 * TILES + z] = tiles[z][1]

    def unpack(step, way, c, z):
        t = c * CELLS_Z + z
        inside = receives[step, way, 2 * t + 1]
        edge = receives[step, way, 2 * TILES + z]
        y = jnp.where(in_y_group, inside, jnp.where(sub == 7, turn(inside, 7), edge))
        d = jnp.where(in_z_group, inside, receives[step, way, 2 * TILES + CELLS_Z + c])
        return [receives[step, way, 2 * t], y, d]

    def unpack_corner(step, way):
        return turn(receives[step, way, PACKED - 1], 4)

    def fill(ref, planes):
        end = ref[last_tile, corners, :]
        for a in planes:
            for z in range(CELLS_Z):
                ref[TILES + z, group(a, 0), :] = jnp.where(
                    low_half, pltpu.roll(ref[z, group(a, 0), :], HALF, 1), ref[TILES - CELLS_Z + z, group(a, 1), :]
                )
            ref[TILES + CELLS_Z - 1, group(a, 2), :] = jnp.where(
                low_half, pltpu.roll(ref[CELLS_Z - 1, group(a, 2), :], HALF, 1), turn(end, -a)
            )

        def body(c):
            first = c * CELLS_Z
            ends = [ref[first + z, corners, :] for z in range(CELLS_Z)]
            for a in planes:
                y_new = [
                    jnp.where(along_y, ref[first + CELLS_Z + z, group(a, 0), :], ref[first + z, group(a, 1), :])
                    for z in range(CELLS_Z)
                ]
                for z in range(CELLS_Z):
                    ref[first + z, group(a, 1), :] = y_new[z]
                    if z < CELLS_Z - 1:
                        ref[first + z, group(a, 2), :] = jnp.where(
                            along_z, ref[first + z + 1, group(a, 0), :], ref[first + z, group(a, 2), :]
                        )
                        ahead = y_new[z + 1]
                    else:
                        ahead = ref[first + CELLS_Z + z, group(a, 2), :]
                    ends[z] = jnp.where(sub == a, turn(ahead, a), ends[z])
            for z in range(CELLS_Z):
                ref[first + z, corners, :] = ends[z]

        over_chunks(body)

    def assembled(c, a):
        tiles, corner_terms = [], []
        for z in range(CELLS_Z):
            t = c * CELLS_Z + z
            own, y, d = [product[t + CELLS_Z, group(a, g), :] for g in range(3)]
            own = own + jnp.where(along_y, product[t, group(a, 1), :], 0.0)
            d = d + jnp.where(corner, turn(product[t, corners, :], -a), 0.0)
            tiles.append([own, y, d])
            corner_terms.append(turn(product[t + CELLS_Z, corners, :], -a))
        for z in range(1, CELLS_Z):
            tiles[z][0] = tiles[z][0] + jnp.where(along_z, tiles[z - 1][2], 0.0)
            tiles[z][1] = tiles[z][1] + jnp.where(corner, corner_terms[z - 1], 0.0)
        return tiles

    def multiply(current):
        mass = mass_ref[...]
        stiff = stiff_ref[...]

        def body(c):
            for pair in range(CELLS_Z // 2):
                t = c * CELLS_Z + 2 * pair
                values = [current[t], current[t + 1]]
                high, low = split(jnp.concatenate(values, axis=1))
                result = jnp.dot(
                    stiff, jnp.concatenate([high, low], axis=0), preferred_element_type=jnp.float32
                )
                result = result[:ROWS] + result[ROWS:]
                for k in range(2):
                    product[t + CELLS_Z + k] = result[:, k * LANES : (k + 1) * LANES] * scale_ref[
                        pl.ds(t + k, 1), :
                    ] + mass * potential_ref[pl.ds(t + k, 1), :] * values[k]

        over_chunks(body)
        for z in range(CELLS_Z):
            for rows in [group(a, 1) for a in range(5)] + [corners]:
                turned = pltpu.roll(product[TILES + z, rows, :], HALF, 1)
                product[z, rows, :] = jnp.where(low_half, 0.0, turned)

    def advance(step, current, previous, t, rows, total):
        value = total - CENTER * current[t, rows, :]
        if step == 0:
            previous[t, rows, :] = value * (1.0 / HALF_WIDTH)
        else:
            previous[t, rows, :] = value * (2.0 / HALF_WIDTH) - previous[t, rows, :]

    def advance_inner(step, current, previous):
        def body(c):
            for a in inner:
                tiles = assembled(c, a)
                for z in range(CELLS_Z):
                    for g in range(3):
                        advance(step, current, previous, c * CELLS_Z + z, group(a, g), tiles[z][g])

        over_chunks(body)

    def send_face(way, a):
        def body(c):
            tiles = assembled(c, a)
            for z in range(CELLS_Z):
                for g in range(3):
                    face[way, c * CELLS_Z + z, 8 * g : 8 * g + 8, :] = tiles[z][g]
            pack(way, c, tiles)

        over_chunks(body)
        sends[way, PACKED - 1] = product[TILES + CELLS_Z - 1, corners, :]

    def advance_face(step, current, previous, way, a, valid):
        def body(c):
            for z in range(CELLS_Z):
                t = c * CELLS_Z + z
                arrived = unpack(step + 1, way, c, z)
                for g in range(3):
                    total = face[1 - way, t, 8 * g : 8 * g + 8, :] + jnp.where(valid, arrived[g], 0.0)
                    advance(step, current, previous, t, group(a, g), total)

        over_chunks(body)

    def advance_corner(step, current, previous):
        total = product[TILES + CELLS_Z - 1, corners, :]
        total = total + jnp.where((sub == bottom) & has_below, unpack_corner(step + 1, 0), 0.0)
        total = total + jnp.where((sub == top) & has_above, unpack_corner(step + 1, 1), 0.0)
        advance(step, current, previous, last_tile, corners, total)

    node_count = waves_ref.shape[1]
    whole_blocks = node_count // LANES

    def transpose(i, carry):
        at = pl.ds(pl.multiple_of(i * LANES, LANES), LANES)
        block = waves_ref[:, at]
        doubled[at, :] = jnp.concatenate([block, block], axis=0).T
        return carry

    lax.fori_loop(0, whole_blocks, transpose, 0)
    rest = node_count - whole_blocks * LANES
    block = jnp.concatenate(
        [waves_ref[:, whole_blocks * LANES :], jnp.zeros((HALF, LANES - rest), jnp.float32)], axis=1
    )
    doubled[whole_blocks * LANES : (whole_blocks + 1) * LANES, :] = jnp.concatenate([block, block], axis=0).T

    out_ref[...] = jnp.zeros_like(out_ref)
    low_row = lax.broadcasted_iota(jnp.int32, (1, LANES), 1) < HALF

    def gather(t, nodes):
        for node, row in nodes:
            first = doubled[pl.ds(index_ref[node, 2 * t], 1), :]
            second = doubled[pl.ds(index_ref[node, 2 * t + 1], 1), :]
            out_ref[t, row : row + 1, :] = jnp.where(low_row, first, second)

    each_node_once((top,), gather)
    over_chunks(
        lambda c: pack(0, c, [[out_ref[c * CELLS_Z + z, group(top, g), :] for g in range(3)] for z in range(CELLS_Z)])
    )
    sends[0, PACKED - 1] = out_ref[last_tile, corners, :]
    owner = copy(0, 0)
    owner.start()
    each_node_once((0, 1, 2, 3), gather)
    owner.wait()

    def take_owner(c):
        for z in range(CELLS_Z):
            t = c * CELLS_Z + z
            arrived = unpack(0, 0, c, z)
            for g in range(3):
                out_ref[t, group(bottom, g), :] = jnp.where(has_below, arrived[g], out_ref[t, group(bottom, g), :])

    over_chunks(take_owner)
    out_ref[last_tile, corners, :] = jnp.where(
        (sub == bottom) & has_below, unpack_corner(0, 0), out_ref[last_tile, corners, :]
    )
    fill(out_ref, range(5))

    for step in range(FILTER_DEG):
        current, previous = (out_ref, other) if step % 2 == 0 else (other, out_ref)
        if step == 0:
            other[...] = jnp.zeros_like(other)
        multiply(current)
        copies = [copy(step + 1, 0), copy(step + 1, 1)]
        for way, a in ((0, top), (1, bottom)):
            send_face(way, a)
            copies[way].start()
        advance_inner(step, current, previous)
        copies[0].wait()
        advance_face(step, current, previous, 0, bottom, has_below)
        copies[1].wait()
        advance_face(step, current, previous, 1, top, has_above)
        advance_corner(step, current, previous)
        fill(previous, range(5))


def filter_cells(index, wavefunctions, stiff, scale, potential):
    whole = pl.BlockSpec(memory_space=pltpu.VMEM)
    cells = (TILES + CELLS_Z, ROWS, LANES)
    rounds = FILTER_DEG + 1
    blocks = wavefunctions.shape[1] // LANES + 1
    return pl.pallas_call(
        filter_kernel,
        out_shape=jax.ShapeDtypeStruct(cells, jnp.float32),
        in_specs=[pl.BlockSpec(memory_space=pltpu.SMEM)] + [whole] * 5,
        out_specs=whole,
        scratch_shapes=[
            pltpu.VMEM(cells, jnp.float32),
            pltpu.VMEM(cells, jnp.float32),
            pltpu.VMEM((2, TILES, PLANE, LANES), jnp.float32),
            pltpu.VMEM((blocks * LANES, LANES), jnp.float32),
            pltpu.VMEM((2, PACKED, 8, LANES), jnp.float32),
            pltpu.VMEM((rounds, 2, PACKED, 8, LANES), jnp.float32),
            pltpu.SemaphoreType.DMA((rounds, 2)),
            pltpu.SemaphoreType.DMA((rounds, 2)),
        ],
        compiler_params=pltpu.CompilerParams(
            collective_id=0, has_side_effects=True, vmem_limit_bytes=56 * 2**20
        ),
        name="filter_cells",
    )(index, wavefunctions, stiff, row_mass(), scale, potential)


def split(x):
    high = x.astype(jnp.bfloat16)
    return high, (x - high.astype(jnp.float32)).astype(jnp.bfloat16)


def exact_dot_t(x, y):
    return lax.dot_general(
        x, y, (((1,), (1,)), ((), ())), precision=HIGHEST, preferred_element_type=jnp.float32
    )


def inverse_of_block(block):
    size = BANDS_DEV
    row_at = lax.broadcasted_iota(jnp.int32, (size, LANES), 0)
    lane = lax.broadcasted_iota(jnp.int32, (size, LANES), 1)
    wide = jnp.concatenate([block, jnp.zeros((size, LANES - size), jnp.float32)], axis=1)
    wide = jnp.where(lane == row_at + size, 1.0, wide)
    tiles = [wide[8 * g : 8 * g + 8] for g in range(size // 8)]
    sub = lax.broadcasted_iota(jnp.int32, (8, LANES), 0)
    for home in range(size // 8):
        live = range(home, size // 8)
        columns = {
            (g, n): jnp.broadcast_to(tiles[g][:, 8 * home + n : 8 * home + n + 1], (8, LANES))
            for g in live for n in range(8)
        }
        for at in range(8):
            scale = 1.0 / columns[home, at][at : at + 1, :]
            ratio = tiles[home][at : at + 1, :] * scale
            ahead = {n: columns[home, n][at : at + 1, :] * scale for n in range(at + 1, 8)}
            for g in live:
                factor = columns[g, at]
                if g == home:
                    factor = jnp.where(sub > at, factor, 0.0)
                for n in range(at + 1, 8):
                    columns[g, n] = columns[g, n] - factor * ahead[n]
                tiles[g] = tiles[g] - factor * ratio
    wide = jnp.concatenate(tiles, axis=0)
    pivots = jnp.sum(jnp.where(lane == row_at, wide, 0.0), axis=1, keepdims=True)
    return wide[:, size:] * (1.0 / jnp.sqrt(pivots))


def finish_kernel(
    owned, own, weight, out, partner, cross, partner_cross, sums, by_x, by_y, line, piece, by_z, reduced, everyone,
    inverse, pair_sems, cross_sems, forward_sems, x_sems, y_sems, z_sems, y_back_sems, x_back_sems, band_sems,
):
    space, band = lax.axis_index("space"), lax.axis_index("band")
    at_x = lax.rem(space, 4)
    at_y = lax.rem(space // 4, 4)
    core = lax.rem(band, 2)
    chip = band // 2
    mate = band + 1 - 2 * core
    across = lax.rem(band + 2, N_BAND)
    across_mate = lax.rem(mate + 2, N_BAND)

    def x_peer(k):
        return {"space": space - at_x + lax.rem(at_x + k, 4)}

    def y_peer(k):
        return {"space": space - 4 * at_y + 4 * lax.rem(at_y + k, 4)}

    z_peer = {"space": lax.rem(space + 16, 32)}

    peers = [x_peer(k) for k in (1, 2, 3)] + [y_peer(k) for k in (1, 2, 3)] + [z_peer]
    peers += [{"band": lax.rem(band + k, N_BAND)} for k in (1, 2, 3)]
    barrier = pltpu.get_barrier_semaphore()
    for peer in peers:
        pl.semaphore_signal(barrier, inc=1, device_id=peer, device_id_type=MESH)
    pl.semaphore_wait(barrier, len(peers))

    def send(source, target, sems, slot, peer):
        return pltpu.make_async_remote_copy(
            src_ref=source,
            dst_ref=target,
            send_sem=sems.at[0, slot],
            recv_sem=sems.at[1, slot],
            device_id=peer,
            device_id_type=MESH,
        )

    half = PAIRS // 2
    mine_first = pl.ds(pl.multiple_of(chip * half, half), half)
    mine_second = pl.ds(pl.multiple_of((1 - chip) * half, half), half)
    to_mate, to_across = {"band": mate}, {"band": across}
    pair = send(own, partner, pair_sems, 0, to_mate)
    first = send(own.at[mine_first], cross.at[mine_first], cross_sems, 0, to_across)
    second = send(own.at[mine_second], cross.at[mine_second], cross_sems, 1, to_across)
    forward_first = send(cross.at[mine_second], partner_cross.at[mine_second], forward_sems, 0, to_mate)
    forward_second = send(cross.at[mine_first], partner_cross.at[mine_first], forward_sems, 1, to_mate)
    first.start()
    pair.start()
    pair.wait()

    def products(left, right):
        left_high, left_low = split(left)
        right_high, right_low = split(right)
        return lax.dot_general(
            jnp.concatenate([left_high, left_high, left_low], axis=0),
            jnp.concatenate([right_high, right_low, right_high], axis=0),
            (((0,), (0,)), ((), ())),
            preferred_element_type=jnp.float32,
        )

    def block_rows(i):
        return pl.ds(pl.multiple_of(i * BLOCK, BLOCK), BLOCK)

    def own_terms(i, total):
        rows = block_rows(i)
        mine = own[rows, :]
        return total + products(mine * weight[rows, :], jnp.concatenate([mine, partner[rows, :]], axis=1))

    def cross_terms(i, total):
        rows = block_rows(i + (1 - chip) * (half // BLOCK))
        scale = weight[rows, :]
        return total + products(
            cross[rows, :], jnp.concatenate([own[rows, :] * scale, partner[rows, :] * scale], axis=1)
        )

    low_half = lax.broadcasted_iota(jnp.int32, (BANDS_DEV, LANES), 1) < HALF

    def fold(total):
        size = BANDS_DEV
        left = total[:size, :LANES] + pltpu.roll(total[size:, :LANES], HALF, 1)
        right = pltpu.roll(total[:size, LANES:], HALF, 1) + total[size:, LANES:]
        return jnp.where(low_half, left, right)

    zero = jnp.zeros((LANES, 2 * LANES), jnp.float32)
    sums[0:BANDS_DEV, :] = fold(lax.fori_loop(0, PAIRS // BLOCK, own_terms, zero))
    first.wait()
    second.start()
    forward_first.start()
    sums[BANDS_DEV : 2 * BANDS_DEV, :] = fold(lax.fori_loop(0, half // BLOCK, cross_terms, zero))

    def rows_of(at, size):
        return pl.ds(pl.multiple_of(at, size), size)

    to_x = [
        send(sums.at[rows_of(32 * lax.rem(at_x + k, 4), 32)], by_x.at[k - 1], x_sems, k - 1, x_peer(k)) for k in (1, 2, 3)
    ]
    for step in to_x:
        step.start()
    for step in to_x:
        step.wait()
    line[...] = sums[rows_of(32 * at_x, 32), :] + by_x[0] + by_x[1] + by_x[2]
    to_y = [
        send(line.at[rows_of(8 * lax.rem(at_y + k, 4), 8)], by_y.at[k - 1], y_sems, k - 1, y_peer(k)) for k in (1, 2, 3)
    ]
    for step in to_y:
        step.start()
    for step in to_y:
        step.wait()
    piece[...] = line[rows_of(8 * at_y, 8), :] + by_y[0] + by_y[1] + by_y[2]
    to_z = send(piece, by_z, z_sems, 0, z_peer)
    to_z.start()
    to_z.wait()
    small = rows_of(32 * at_x + 8 * at_y, 8)
    reduced[small, :] = piece[...] + by_z[...]
    back_y = [send(reduced.at[small], reduced.at[small], y_back_sems, k - 1, y_peer(k)) for k in (1, 2, 3)]
    for step in back_y:
        step.start()
    for step in back_y:
        step.wait()
    large = rows_of(32 * at_x, 32)
    back_x = [send(reduced.at[large], reduced.at[large], x_back_sems, k - 1, x_peer(k)) for k in (1, 2, 3)]
    for step in back_x:
        step.start()
    for step in back_x:
        step.wait()
    to_band = [
        send(reduced, everyone.at[band], band_sems, k - 1, {"band": lax.rem(band + k, N_BAND)}) for k in (1, 2, 3)
    ]
    for step in to_band:
        step.start()
    everyone[band] = reduced[...]
    for step in to_band:
        step.wait()

    def part(b, r, c):
        size = BANDS_DEV
        return everyone[b, r * size : (r + 1) * size, c * size : (c + 1) * size] * (1.0 / owned)

    margin = {(b, b): part(b, 0, 0) for b in range(N_BAND)}
    margin[1, 0], margin[3, 2] = part(1, 0, 1), part(3, 0, 1)
    margin[2, 0] = part(0, 1, 0) + part(2, 1, 0).T
    margin[2, 1] = part(0, 1, 1) + part(3, 1, 1).T
    margin[3, 0] = part(1, 1, 1) + part(2, 1, 1).T
    margin[3, 1] = part(1, 1, 0) + part(3, 1, 0).T

    inverses, factor, whole = [], {}, {}
    for k in range(N_BAND):
        diagonal = inverse_of_block(margin[k, k])
        inverses.append(diagonal)
        for i in range(k + 1, N_BAND):
            factor[i, k] = exact_dot_t(margin[i, k], diagonal)
        for i in range(k + 1, N_BAND):
            for j in range(k + 1, i + 1):
                margin[i, j] = margin[i, j] - exact_dot_t(factor[i, k], factor[j, k])
        whole[k, k] = diagonal
        for j in range(k):
            total = exact_dot(factor[k, j], whole[j, j])
            for m in range(j + 1, k):
                total = total + exact_dot(factor[k, m], whole[m, j])
            whole[k, j] = -exact_dot(diagonal, total)
        if k == 2:
            second.wait()
            forward_second.start()
    padding = jnp.zeros((BANDS_DEV, LANES - BANDS_DEV), jnp.float32)
    for i in range(N_BAND):
        for j in range(N_BAND):
            if j <= i:
                inverse[i, j] = jnp.concatenate([whole[i, j], padding], axis=1)
            else:
                inverse[i, j] = jnp.zeros((BANDS_DEV, LANES), jnp.float32)
    forward_first.wait()
    forward_second.wait()

    panels = [inverse[band, source] for source in (band, mate, across, across_mate)]
    left = jnp.concatenate(
        [
            jnp.concatenate(panels, axis=1),
            jnp.concatenate([pltpu.roll(panel, HALF, 1) for panel in panels], axis=1),
        ],
        axis=0,
    )
    left_high, left_low = split(left)
    left = jnp.concatenate([left_high, left_high, left_low], axis=1)

    def rotate(i, carry):
        rows = block_rows(i)
        right = jnp.concatenate([ref[rows, :] for ref in (own, partner, cross, partner_cross)], axis=1)
        right_high, right_low = split(right)
        rotated = lax.dot_general(
            left,
            jnp.concatenate([right_high, right_low, right_high], axis=1),
            (((1,), (1,)), ((), ())),
            preferred_element_type=jnp.float32,
        )
        out[:, rows] = rotated[:BANDS_DEV]
        out[:, pl.ds(pl.multiple_of(PAIRS + i * BLOCK, BLOCK), BLOCK)] = rotated[BANDS_DEV:]
        return carry

    lax.fori_loop(0, PAIRS // BLOCK, rotate, 0)


def finish(packed, weight, owned_count):
    whole = pl.BlockSpec(memory_space=pltpu.VMEM)
    nodes = pltpu.VMEM((PAIRS, LANES), jnp.float32)

    def small(*shape):
        return pltpu.VMEM(shape, jnp.float32)

    def sems(slots):
        return pltpu.SemaphoreType.DMA((2, slots))

    return pl.pallas_call(
        functools.partial(finish_kernel, owned_count),
        out_shape=jax.ShapeDtypeStruct((BANDS_DEV, 2 * PAIRS), jnp.float32),
        in_specs=[whole, whole],
        out_specs=whole,
        scratch_shapes=[
            nodes, nodes, nodes,
            small(LANES, LANES), small(3, 32, LANES), small(3, 8, LANES), small(32, LANES), small(8, LANES),
            small(8, LANES), small(LANES, LANES), small(N_BAND, LANES, LANES),
            small(N_BAND, N_BAND, BANDS_DEV, LANES),
            sems(1), sems(2), sems(2), sems(3), sems(3), sems(1), sems(3), sems(3), sems(3),
        ],
        compiler_params=pltpu.CompilerParams(
            collective_id=1, has_side_effects=True, vmem_limit_bytes=48 * 2**20
        ),
        name="finish",
    )(packed, weight)


def shards(
    wavefunctions, stiffness, cell_scale, cell_potential, connectivity, lower_face, upper_face
):
    node_count = wavefunctions.shape[1]
    face_count = lower_face.shape[0]
    space_count = lax.axis_size("space")
    owned_count = node_count * space_count - face_count * (space_count - 1)

    coefficients = jnp.stack([cell_scale, cell_potential])
    index, scale, potential, stiff = make_layout(connectivity, coefficients, stiffness)
    cells = filter_cells(index, wavefunctions, stiff, scale, potential)
    packed, weight = scatter_nodes(index, cells)
    return finish(packed, weight, owned_count)[:, :node_count]


def solution(mesh):
    placed = (
        P("band", "space"),
        P(),
        P("space"),
        P("space"),
        P(None, "space"),
        P("space"),
        P("space"),
    )
    return jax.shard_map(
        shards, mesh=mesh, in_specs=placed, out_specs=P("band", "space"), check_vma=False
    )
```

```python
import functools

import jax
import jax.numpy as jnp
import numpy as np
from jax import lax
from jax.experimental import pallas as pl
from jax.experimental.pallas import tpu as pltpu
from jax.sharding import PartitionSpec as P

FILTER_DEG = 4
GLL_WEIGHTS = (0.1, 49.0 / 90.0, 32.0 / 45.0, 49.0 / 90.0, 0.1)
CENTER = 11.0
HALF_WIDTH = 9.0
HIGHEST = lax.Precision.HIGHEST
MESH = pl.DeviceIdType.MESH

CELLS_Y = 20
CELLS_Z = 6
CHUNKS = CELLS_Y // 2
TILES = CHUNKS * CELLS_Z
SLOTS = 2 * TILES
HALF = 64
LANES = 128
ROWS = 128
PLANE = 24
CORNERS = 5 * PLANE
MESSAGE = 2 * CELLS_Z + 1
EDGE = CELLS_Z + 1

NODES = 10125
PAIRS = 5120
BLOCK = 256
BANDS_DEV = 64
N_BAND = 4


def row_of_node(a, b, c):
    if (b, c) == (4, 4):
        return CORNERS + a
    rows = {(0, 0): 0, (4, 0): 8, (0, 4): 16, (1, 1): 7, (1, 2): 15, (1, 3): 23}
    for k in (1, 2, 3):
        rows[(0, k)] = k
        rows[(4, k)] = 8 + k
        rows[(k, 0)] = 3 + k
        rows[(k, 4)] = 16 + 3 + k
        rows[(2, k)] = 8 + 3 + k
        rows[(3, k)] = 16 + k
    return PLANE * a + rows[(b, c)]


def node_rows(planes, chosen):
    return [
        (25 * a + 5 * b + c, row_of_node(a, b, c))
        for a in planes for b in range(5) for c in range(5) if chosen(b, c)
    ]


LOCAL_ROWS = [row for _, row in node_rows(range(5), lambda b, c: True)]


def row_selector():
    chosen = np.zeros((ROWS, 125), np.float32)
    chosen[LOCAL_ROWS, np.arange(125)] = 1.0
    return chosen


def row_mass():
    weights = np.array(GLL_WEIGHTS, np.float32)
    mass = (weights[:, None, None] * weights[None, :, None] * weights[None, None, :]).reshape(-1)
    spread = np.zeros((ROWS, LANES), np.float32)
    spread[LOCAL_ROWS, :] = mass[:, None]
    return spread


def local(a, b, c):
    return 25 * a + 5 * b + c


def exact_dot(x, y):
    return jnp.dot(x, y, precision=HIGHEST, preferred_element_type=jnp.float32)


def chain_counts(before, doublings):
    size = before.shape[0]
    eye = (
        lax.broadcasted_iota(jnp.int32, (size, size), 0) == lax.broadcasted_iota(jnp.int32, (size, size), 1)
    ).astype(jnp.float32)
    total, power = eye + before, before
    for _ in range(doublings):
        power = jnp.dot(power, power, preferred_element_type=jnp.float32)
        total = total + jnp.dot(total, power, preferred_element_type=jnp.float32)
    return jnp.sum(total, axis=0, keepdims=True) - 1.0


def layout_kernel(conn_ref, coef_ref, stiff_ref, select_ref, index_ref, scale_ref, potential_ref, stiffness_ref):
    conn = conn_ref[...].astype(jnp.float32)
    cells = conn.shape[1]
    on_rows = lax.broadcasted_iota(jnp.int32, (cells, cells), 0)
    on_lanes = lax.broadcasted_iota(jnp.int32, (cells, cells), 1)

    def as_column(row):
        return jnp.sum(jnp.where(on_rows == on_lanes, row, 0.0), axis=1, keepdims=True)

    def row_of(node):
        return conn[node : node + 1, :]

    after_z = (as_column(row_of(local(2, 2, 4))) == row_of(local(2, 2, 0))).astype(jnp.float32)
    after_y = (as_column(row_of(local(2, 4, 2))) == row_of(local(2, 0, 2))).astype(jnp.float32)
    at_z = chain_counts(after_z, 2)
    at_y = chain_counts(after_y, 4)
    upper_half = at_y >= CHUNKS
    tile = (at_y - jnp.where(upper_half, 1.0 * CHUNKS, 0.0)) * CELLS_Z + at_z
    slot = 2.0 * tile + jnp.where(upper_half, 1.0, 0.0)
    moved = (as_column(slot) == on_lanes.astype(jnp.float32)).astype(jnp.float32)
    index_ref[...] = (exact_dot(conn, moved) + 0.5).astype(jnp.int32)

    wanted = lax.broadcasted_iota(jnp.int32, (TILES, cells), 0).astype(jnp.float32)
    lane = lax.broadcasted_iota(jnp.int32, (TILES, LANES), 1)

    def spread(row):
        low, high = [
            jnp.sum(jnp.where(slot == 2.0 * wanted + half, row, 0.0), axis=1, keepdims=True) for half in (0.0, 1.0)
        ]
        return jnp.where(lane < HALF, low, high)

    scale_ref[...] = spread(coef_ref[0:1, :])
    potential_ref[...] = spread(coef_ref[1:2, :])

    select = select_ref[...]
    part = exact_dot(select, stiff_ref[...])
    stiff = lax.dot_general(
        part, select, (((1,), (1,)), ((), ())), precision=HIGHEST, preferred_element_type=jnp.float32
    )
    high = stiff.astype(jnp.bfloat16)
    low = (stiff - high.astype(jnp.float32)).astype(jnp.bfloat16)
    stiffness_ref[...] = jnp.concatenate(
        [jnp.concatenate([high, high], axis=1), jnp.concatenate([low, low], axis=1)], axis=0
    )


def make_layout(connectivity, coefficients, stiffness):
    cells = connectivity.shape[1]
    whole = pl.BlockSpec(memory_space=pltpu.VMEM)
    return pl.pallas_call(
        layout_kernel,
        out_shape=(
            jax.ShapeDtypeStruct((125, cells), jnp.int32),
            jax.ShapeDtypeStruct((TILES, LANES), jnp.float32),
            jax.ShapeDtypeStruct((TILES, LANES), jnp.float32),
            jax.ShapeDtypeStruct((2 * ROWS, 2 * ROWS), jnp.bfloat16),
        ),
        in_specs=[whole] * 4,
        out_specs=(whole,) * 4,
        name="layout",
    )(connectivity, coefficients, stiffness, row_selector())


def each_node_once(planes, visit):
    def loop(count, tile_of, nodes, halves=(0, 1)):
        def body(i, carry):
            visit(tile_of(i), nodes, halves)
            return carry

        lax.fori_loop(0, count, body, 0)

    loop(TILES, lambda i: i, node_rows(planes, lambda b, c: b < 4 and c < 4))
    loop(CELLS_Z, lambda i: TILES - CELLS_Z + i, node_rows(planes, lambda b, c: b == 4 and c < 4), (1,))
    loop(1, lambda i: TILES - 1, node_rows(planes, lambda b, c: b == 4 and c == 4), (1,))
    loop(CHUNKS, lambda i: i * CELLS_Z + CELLS_Z - 1, node_rows(planes, lambda b, c: b < 4 and c == 4))


def scatter_kernel(index_ref, cells_ref, packed_ref, weight_ref, nodes_ref, rows_ref):
    lane = lax.broadcasted_iota(jnp.int32, (ROWS, LANES), 1)
    row_at = lax.broadcasted_iota(jnp.int32, (ROWS, LANES), 0)
    inner = lax.axis_index("space") > 0
    weight = jnp.where(((row_at < PLANE) | (row_at == CORNERS)) & inner, 0.0, 1.0)
    nodes_ref[NODES - NODES % 8 :, :] = jnp.zeros((2 * PAIRS - NODES + NODES % 8, LANES), jnp.float32)

    def visit(t, nodes, halves):
        values = cells_ref[t]
        turned = pltpu.roll(values, HALF, 1)
        rows_ref[0] = jnp.where(lane < HALF, values, weight)
        rows_ref[1] = jnp.where(lane < HALF, turned, weight)
        for node, row in nodes:
            for half in halves:
                nodes_ref[pl.ds(index_ref[node, 2 * t + half], 1), :] = rows_ref[half, row : row + 1, :]

    each_node_once(range(5), visit)
    low_half = lax.broadcasted_iota(jnp.int32, (BLOCK, LANES), 1) < HALF

    def pack(i, carry):
        first = nodes_ref[pl.ds(pl.multiple_of(i * BLOCK, BLOCK), BLOCK), :]
        second = nodes_ref[pl.ds(pl.multiple_of(PAIRS + i * BLOCK, BLOCK), BLOCK), :]
        rows = pl.ds(pl.multiple_of(i * BLOCK, BLOCK), BLOCK)
        packed_ref[rows, :] = jnp.where(low_half, first, pltpu.roll(second, HALF, 1))
        weight_ref[rows, :] = jnp.where(low_half, pltpu.roll(first, HALF, 1), second)
        return carry

    lax.fori_loop(0, PAIRS // BLOCK, pack, 0)


def scatter_nodes(index, cells):
    whole = pl.BlockSpec(memory_space=pltpu.VMEM)
    packed = jax.ShapeDtypeStruct((PAIRS, LANES), jnp.float32)
    return pl.pallas_call(
        scatter_kernel,
        out_shape=(packed, packed),
        in_specs=[pl.BlockSpec(memory_space=pltpu.SMEM), whole],
        out_specs=(whole, whole),
        scratch_shapes=[
            pltpu.VMEM((2 * PAIRS, LANES), jnp.float32),
            pltpu.VMEM((2, ROWS, LANES), jnp.float32),
        ],
        compiler_params=pltpu.CompilerParams(vmem_limit_bytes=40 * 2**20),
        name="scatter_nodes",
    )(index, cells)


def filter_kernel(
    index_ref, waves_ref, stiff_ref, mass_ref, scale_ref, potential_ref, out_ref,
    other, product, face, doubled, sends, edge_sends, receives, edge_receives,
    send_sems, receive_sems, edge_send_sems, edge_receive_sems,
):
    count = lax.axis_size("space")
    me = lax.axis_index("space")
    above, below = lax.rem(me + 1, count), lax.rem(me + count - 1, count)
    has_below, has_above = me > 0, me < count - 1

    barrier = pltpu.get_barrier_semaphore()
    for neighbour in (below, above):
        pl.semaphore_signal(barrier, inc=1, device_id={"space": neighbour}, device_id_type=MESH)
    pl.semaphore_wait(barrier, 2)

    sub = lax.broadcasted_iota(jnp.int32, (8, LANES), 0)
    lane = lax.broadcasted_iota(jnp.int32, (8, LANES), 1)
    corner = sub == 0
    along_y = sub <= 3
    along_z = corner | ((sub >= 4) & (sub <= 6))
    in_y_group = (sub >= 4) & (sub <= 6)
    in_z_group = ((sub >= 1) & (sub <= 3)) | (sub == 7)
    low_half = lane < HALF
    corners = slice(CORNERS, CORNERS + 8)
    last_tile = TILES - 1
    bottom, top = 0, 4
    inner = (1, 2, 3)

    def group(a, g):
        return slice(PLANE * a + 8 * g, PLANE * a + 8 * g + 8)

    def turn(value, by):
        return pltpu.roll(value, by % 8, 0) if by % 8 else value

    def over_chunks(body):
        def step(c, carry):
            body(c)
            return carry

        lax.fori_loop(0, CHUNKS, step, 0)

    def message(step, way, c):
        return pltpu.make_async_remote_copy(
            src_ref=sends.at[way, c],
            dst_ref=receives.at[step, way, c],
            send_sem=send_sems.at[step, way, c],
            recv_sem=receive_sems.at[step, way, c],
            device_id={"space": above if way == 0 else below},
            device_id_type=MESH,
        )

    def edge_message(step, way):
        return pltpu.make_async_remote_copy(
            src_ref=edge_sends.at[way],
            dst_ref=edge_receives.at[step, way],
            send_sem=edge_send_sems.at[step, way],
            recv_sem=edge_receive_sems.at[step, way],
            device_id={"space": above if way == 0 else below},
            device_id_type=MESH,
        )

    def start(copy, way):
        @pl.when(has_above if way == 0 else has_below)
        def _():
            copy.start()

    def finish_copy(copy, way):
        @pl.when(has_above if way == 0 else has_below)
        def _():
            copy.wait_send()

        @pl.when(has_below if way == 0 else has_above)
        def _():
            copy.wait_recv()

    def send_chunk(step, way, c, tiles, ends):
        for z, (own, y, d) in enumerate(tiles):
            sends[way, c, 2 * z] = own
            sends[way, c, 2 * z + 1] = jnp.where(corner, turn(y, 1), jnp.where(in_y_group, y, d))
        sends[way, c, MESSAGE - 1] = tiles[CELLS_Z - 1][2]
        start(message(step, way, c), way)

        @pl.when(c == CHUNKS - 1)
        def _():
            for z in range(CELLS_Z):
                edge_sends[way, z] = tiles[z][1]
            edge_sends[way, EDGE - 1] = ends
            start(edge_message(step, way), way)

    def unpack(step, way, c, z):
        inside = receives[step, way, c, 2 * z + 1]
        y = jnp.where(in_y_group, inside, jnp.where(sub == 7, turn(inside, 7), 0.0))
        d = jnp.where(in_z_group, inside, receives[step, way, c, MESSAGE - 1])
        return [receives[step, way, c, 2 * z], y, d]

    def unpack_corner(step, way):
        return turn(edge_receives[step, way, EDGE - 1], 4)

    def fill(ref, c):
        @pl.when(c == CHUNKS - 1)
        def _():
            end = ref[last_tile, corners, :]
            for a in range(5):
                for z in range(CELLS_Z):
                    ref[TILES + z, group(a, 0), :] = jnp.where(
                        low_half, pltpu.roll(ref[z, group(a, 0), :], HALF, 1), ref[TILES - CELLS_Z + z, group(a, 1), :]
                    )
                ref[TILES + CELLS_Z - 1, group(a, 2), :] = jnp.where(
                    low_half, pltpu.roll(ref[CELLS_Z - 1, group(a, 2), :], HALF, 1), turn(end, -a)
                )

        first = c * CELLS_Z
        ends = [ref[first + z, corners, :] for z in range(CELLS_Z)]
        for a in range(5):
            y_new = [
                jnp.where(along_y, ref[first + CELLS_Z + z, group(a, 0), :], ref[first + z, group(a, 1), :])
                for z in range(CELLS_Z)
            ]
            for z in range(CELLS_Z):
                ref[first + z, group(a, 1), :] = y_new[z]
                if z < CELLS_Z - 1:
                    ref[first + z, group(a, 2), :] = jnp.where(
                        along_z, ref[first + z + 1, group(a, 0), :], ref[first + z, group(a, 2), :]
                    )
                    ahead = y_new[z + 1]
                else:
                    ahead = ref[first + CELLS_Z + z, group(a, 2), :]
                ends[z] = jnp.where(sub == a, turn(ahead, a), ends[z])
        for z in range(CELLS_Z):
            ref[first + z, corners, :] = ends[z]

    def assembled(c, a):
        tiles, corner_terms = [], []
        for z in range(CELLS_Z):
            t = c * CELLS_Z + z
            own, y, d = [product[t + CELLS_Z, group(a, g), :] for g in range(3)]
            own = own + jnp.where(along_y, product[t, group(a, 1), :], 0.0)
            d = d + jnp.where(corner, turn(product[t, corners, :], -a), 0.0)
            tiles.append([own, y, d])
            corner_terms.append(turn(product[t + CELLS_Z, corners, :], -a))
        for z in range(1, CELLS_Z):
            tiles[z][0] = tiles[z][0] + jnp.where(along_z, tiles[z - 1][2], 0.0)
            tiles[z][1] = tiles[z][1] + jnp.where(corner, corner_terms[z - 1], 0.0)
        return tiles

    def multiply(current, c):
        mass = mass_ref[...]
        for pair in range(CELLS_Z // 2):
            t = c * CELLS_Z + 2 * pair
            values = [current[t], current[t + 1]]
            high, low = split(jnp.concatenate(values, axis=1))
            result = jnp.dot(
                stiff_ref[...], jnp.concatenate([high, low], axis=0), preferred_element_type=jnp.float32
            )
            result = result[:ROWS] + result[ROWS:]
            for k in range(2):
                product[t + CELLS_Z + k] = result[:, k * LANES : (k + 1) * LANES] * scale_ref[
                    pl.ds(t + k, 1), :
                ] + mass * potential_ref[pl.ds(t + k, 1), :] * values[k]

        @pl.when(c == CHUNKS - 1)
        def _():
            for z in range(CELLS_Z):
                for rows in [group(a, 1) for a in range(5)] + [corners]:
                    turned = pltpu.roll(product[TILES + z, rows, :], HALF, 1)
                    product[z, rows, :] = jnp.where(low_half, 0.0, turned)

    def buffers(step):
        return (out_ref, other) if step % 2 == 0 else (other, out_ref)

    def factor(step):
        return (1.0 if step == 0 else 2.0) / HALF_WIDTH

    def advance(step, t, rows, total):
        current, previous = buffers(step)
        value = (total - CENTER * current[t, rows, :]) * factor(step)
        previous[t, rows, :] = value if step == 0 else value - previous[t, rows, :]

    def assemble(step, c):
        ends = product[TILES + CELLS_Z - 1, corners, :]
        for way, a in ((0, top), (1, bottom)):
            tiles = assembled(c, a)
            for z in range(CELLS_Z):
                for g in range(3):
                    face[way, c * CELLS_Z + z, 8 * g : 8 * g + 8, :] = tiles[z][g]
            send_chunk(step + 1, way, c, tiles, ends)
        for a in inner:
            tiles = assembled(c, a)
            for z in range(CELLS_Z):
                for g in range(3):
                    advance(step, c * CELLS_Z + z, group(a, g), tiles[z][g])

    def advance_faces(step, c):
        for way, a, valid in ((0, bottom, has_below), (1, top, has_above)):
            finish_copy(message(step + 1, way, c), way)
            for z in range(CELLS_Z):
                t = c * CELLS_Z + z
                arrived = unpack(step + 1, way, c, z)
                for g in range(3):
                    total = face[1 - way, t, 8 * g : 8 * g + 8, :] + jnp.where(valid, arrived[g], 0.0)
                    advance(step, t, group(a, g), total)

        @pl.when(c == CHUNKS - 1)
        def _():
            previous = buffers(step)[1]
            ends = product[TILES + CELLS_Z - 1, corners, :]
            for way, a, valid in ((0, bottom, has_below), (1, top, has_above)):
                finish_copy(edge_message(step + 1, way), way)
                for z in range(CELLS_Z):
                    rows = group(a, 1)
                    edge = jnp.where(along_y & valid, edge_receives[step + 1, way, z], 0.0)
                    previous[TILES - CELLS_Z + z, rows, :] = previous[TILES - CELLS_Z + z, rows, :] + factor(step) * edge
                ends = ends + jnp.where((sub == a) & valid, unpack_corner(step + 1, way), 0.0)
            advance(step, last_tile, corners, ends)

    node_count = waves_ref.shape[1]
    whole_blocks = node_count // LANES

    def transpose(i, carry):
        at = pl.ds(pl.multiple_of(i * LANES, LANES), LANES)
        block = waves_ref[:, at]
        doubled[at, :] = jnp.concatenate([block, block], axis=0).T
        return carry

    lax.fori_loop(0, whole_blocks, transpose, 0)
    rest = node_count - whole_blocks * LANES
    block = jnp.concatenate(
        [waves_ref[:, whole_blocks * LANES :], jnp.zeros((HALF, LANES - rest), jnp.float32)], axis=1
    )
    doubled[whole_blocks * LANES : (whole_blocks + 1) * LANES, :] = jnp.concatenate([block, block], axis=0).T

    out_ref[...] = jnp.zeros_like(out_ref)
    low_row = lax.broadcasted_iota(jnp.int32, (1, LANES), 1) < HALF

    def gather(t, nodes, halves):
        for node, row in nodes:
            first = doubled[pl.ds(index_ref[node, 2 * t], 1), :]
            second = doubled[pl.ds(index_ref[node, 2 * t + 1], 1), :]
            out_ref[t, row : row + 1, :] = jnp.where(low_row, first, second)

    each_node_once((top,), gather)

    def send_owner(c):
        tiles = [[out_ref[c * CELLS_Z + z, group(top, g), :] for g in range(3)] for z in range(CELLS_Z)]
        send_chunk(0, 0, c, tiles, out_ref[last_tile, corners, :])

    over_chunks(send_owner)
    each_node_once((0, 1, 2, 3), gather)
    other[...] = jnp.zeros_like(other)

    def take_owner(c):
        finish_copy(message(0, 0, c), 0)
        for z in range(CELLS_Z):
            t = c * CELLS_Z + z
            arrived = unpack(0, 0, c, z)
            for g in range(3):
                out_ref[t, group(bottom, g), :] = jnp.where(has_below, arrived[g], out_ref[t, group(bottom, g), :])

    over_chunks(take_owner)
    finish_copy(edge_message(0, 0), 0)
    for z in range(CELLS_Z):
        t = TILES - CELLS_Z + z
        out_ref[t, group(bottom, 1), :] = jnp.where(
            along_y & has_below, edge_receives[0, 0, z], out_ref[t, group(bottom, 1), :]
        )
    out_ref[last_tile, corners, :] = jnp.where(
        (sub == bottom) & has_below, unpack_corner(0, 0), out_ref[last_tile, corners, :]
    )
    over_chunks(lambda c: fill(out_ref, c))

    multiply(out_ref, CHUNKS - 1)

    def first_step(c):
        multiply(out_ref, c)
        assemble(0, c)

    lax.fori_loop(0, CHUNKS - 1, lambda c, carry: (first_step(c), carry)[1], 0)
    assemble(0, CHUNKS - 1)

    for step in range(1, FILTER_DEG):
        base = step - 1
        current = buffers(step)[0]

        def refresh(c):
            fill(current, c)
            multiply(current, c)

        def next_chunk(i, carry):
            advance_faces(step - 1, lax.rem(base + i, CHUNKS))
            c = lax.rem(base + i - 1, CHUNKS)
            refresh(c)
            assemble(step, c)
            return carry

        advance_faces(step - 1, base)
        advance_faces(step - 1, base + 1)
        refresh(base)
        lax.fori_loop(2, CHUNKS, next_chunk, 0)
        refresh((base + CHUNKS - 1) % CHUNKS)
        assemble(step, (base + CHUNKS - 1) % CHUNKS)
        assemble(step, base)

    last = FILTER_DEG - 1
    lax.fori_loop(
        0, CHUNKS, lambda i, carry: (advance_faces(last, lax.rem(last + i, CHUNKS)), carry)[1], 0
    )


def filter_cells(index, wavefunctions, stiff, scale, potential):
    whole = pl.BlockSpec(memory_space=pltpu.VMEM)
    cells = (TILES + CELLS_Z, ROWS, LANES)
    rounds = FILTER_DEG + 1
    blocks = wavefunctions.shape[1] // LANES + 1
    return pl.pallas_call(
        filter_kernel,
        out_shape=jax.ShapeDtypeStruct(cells, jnp.float32),
        in_specs=[pl.BlockSpec(memory_space=pltpu.SMEM)] + [whole] * 5,
        out_specs=whole,
        scratch_shapes=[
            pltpu.VMEM(cells, jnp.float32),
            pltpu.VMEM(cells, jnp.float32),
            pltpu.VMEM((2, TILES, PLANE, LANES), jnp.float32),
            pltpu.VMEM((blocks * LANES, LANES), jnp.float32),
            pltpu.VMEM((2, CHUNKS, MESSAGE, 8, LANES), jnp.float32),
            pltpu.VMEM((2, EDGE, 8, LANES), jnp.float32),
            pltpu.VMEM((rounds, 2, CHUNKS, MESSAGE, 8, LANES), jnp.float32),
            pltpu.VMEM((rounds, 2, EDGE, 8, LANES), jnp.float32),
            pltpu.SemaphoreType.DMA((rounds, 2, CHUNKS)),
            pltpu.SemaphoreType.DMA((rounds, 2, CHUNKS)),
            pltpu.SemaphoreType.DMA((rounds, 2)),
            pltpu.SemaphoreType.DMA((rounds, 2)),
        ],
        compiler_params=pltpu.CompilerParams(
            collective_id=0, has_side_effects=True, vmem_limit_bytes=56 * 2**20
        ),
        name="filter_cells",
    )(index, wavefunctions, stiff, row_mass(), scale, potential)


def split(x):
    high = x.astype(jnp.bfloat16)
    return high, (x - high.astype(jnp.float32)).astype(jnp.bfloat16)


def exact_dot_t(x, y):
    return lax.dot_general(
        x, y, (((1,), (1,)), ((), ())), precision=HIGHEST, preferred_element_type=jnp.float32
    )


def inverse_of_block(block):
    size = BANDS_DEV
    row_at = lax.broadcasted_iota(jnp.int32, (size, LANES), 0)
    lane = lax.broadcasted_iota(jnp.int32, (size, LANES), 1)
    wide = jnp.concatenate([block, jnp.zeros((size, LANES - size), jnp.float32)], axis=1)
    wide = jnp.where(lane == row_at + size, 1.0, wide)
    tiles = [wide[8 * g : 8 * g + 8] for g in range(size // 8)]
    sub = lax.broadcasted_iota(jnp.int32, (8, LANES), 0)
    for home in range(size // 8):
        live = range(home, size // 8)
        columns = {
            (g, n): jnp.broadcast_to(tiles[g][:, 8 * home + n : 8 * home + n + 1], (8, LANES))
            for g in live for n in range(8)
        }
        for at in range(8):
            scale = 1.0 / columns[home, at][at : at + 1, :]
            ratio = tiles[home][at : at + 1, :] * scale
            ahead = {n: columns[home, n][at : at + 1, :] * scale for n in range(at + 1, 8)}
            for g in live:
                factor = columns[g, at]
                if g == home:
                    factor = jnp.where(sub > at, factor, 0.0)
                for n in range(at + 1, 8):
                    columns[g, n] = columns[g, n] - factor * ahead[n]
                tiles[g] = tiles[g] - factor * ratio
    wide = jnp.concatenate(tiles, axis=0)
    pivots = jnp.sum(jnp.where(lane == row_at, wide, 0.0), axis=1, keepdims=True)
    return wide[:, size:] * (1.0 / jnp.sqrt(pivots))


def finish_kernel(
    owned, own, weight, out, partner, cross, partner_cross, sums, by_x, by_y, line, piece, by_z, reduced, everyone,
    inverse, pair_sems, cross_sems, forward_sems, x_sems, y_sems, z_sems, y_back_sems, x_back_sems, band_sems,
):
    space, band = lax.axis_index("space"), lax.axis_index("band")
    at_x = lax.rem(space, 4)
    at_y = lax.rem(space // 4, 4)
    core = lax.rem(band, 2)
    chip = band // 2
    mate = band + 1 - 2 * core
    across = lax.rem(band + 2, N_BAND)
    across_mate = lax.rem(mate + 2, N_BAND)

    def x_peer(k):
        return {"space": space - at_x + lax.rem(at_x + k, 4)}

    def y_peer(k):
        return {"space": space - 4 * at_y + 4 * lax.rem(at_y + k, 4)}

    z_peer = {"space": lax.rem(space + 16, 32)}

    peers = [x_peer(k) for k in (1, 2, 3)] + [y_peer(k) for k in (1, 2, 3)] + [z_peer]
    peers += [{"band": lax.rem(band + k, N_BAND)} for k in (1, 2, 3)]
    barrier = pltpu.get_barrier_semaphore()
    for peer in peers:
        pl.semaphore_signal(barrier, inc=1, device_id=peer, device_id_type=MESH)
    pl.semaphore_wait(barrier, len(peers))

    def send(source, target, sems, slot, peer):
        return pltpu.make_async_remote_copy(
            src_ref=source,
            dst_ref=target,
            send_sem=sems.at[0, slot],
            recv_sem=sems.at[1, slot],
            device_id=peer,
            device_id_type=MESH,
        )

    half = PAIRS // 2
    mine_first = pl.ds(pl.multiple_of(chip * half, half), half)
    mine_second = pl.ds(pl.multiple_of((1 - chip) * half, half), half)
    to_mate, to_across = {"band": mate}, {"band": across}
    pair = send(own, partner, pair_sems, 0, to_mate)
    first = send(own.at[mine_first], cross.at[mine_first], cross_sems, 0, to_across)
    second = send(own.at[mine_second], cross.at[mine_second], cross_sems, 1, to_across)
    forward_first = send(cross.at[mine_second], partner_cross.at[mine_second], forward_sems, 0, to_mate)
    forward_second = send(cross.at[mine_first], partner_cross.at[mine_first], forward_sems, 1, to_mate)
    first.start()
    pair.start()
    pair.wait()

    def products(left, right):
        left_high, left_low = split(left)
        right_high, right_low = split(right)
        return lax.dot_general(
            jnp.concatenate([left_high, left_high, left_low], axis=0),
            jnp.concatenate([right_high, right_low, right_high], axis=0),
            (((0,), (0,)), ((), ())),
            preferred_element_type=jnp.float32,
        )

    def block_rows(i):
        return pl.ds(pl.multiple_of(i * BLOCK, BLOCK), BLOCK)

    def own_terms(i, total):
        rows = block_rows(i)
        mine = own[rows, :]
        return total + products(mine * weight[rows, :], jnp.concatenate([mine, partner[rows, :]], axis=1))

    def cross_terms(i, total):
        rows = block_rows(i + (1 - chip) * (half // BLOCK))
        scale = weight[rows, :]
        return total + products(
            cross[rows, :], jnp.concatenate([own[rows, :] * scale, partner[rows, :] * scale], axis=1)
        )

    low_half = lax.broadcasted_iota(jnp.int32, (BANDS_DEV, LANES), 1) < HALF

    def fold(total):
        size = BANDS_DEV
        left = total[:size, :LANES] + pltpu.roll(total[size:, :LANES], HALF, 1)
        right = pltpu.roll(total[:size, LANES:], HALF, 1) + total[size:, LANES:]
        return jnp.where(low_half, left, right)

    zero = jnp.zeros((LANES, 2 * LANES), jnp.float32)
    sums[0:BANDS_DEV, :] = fold(lax.fori_loop(0, PAIRS // BLOCK, own_terms, zero))
    first.wait()
    second.start()
    forward_first.start()
    sums[BANDS_DEV : 2 * BANDS_DEV, :] = fold(lax.fori_loop(0, half // BLOCK, cross_terms, zero))

    def rows_of(at, size):
        return pl.ds(pl.multiple_of(at, size), size)

    to_x = [
        send(sums.at[rows_of(32 * lax.rem(at_x + k, 4), 32)], by_x.at[k - 1], x_sems, k - 1, x_peer(k)) for k in (1, 2, 3)
    ]
    for step in to_x:
        step.start()
    for step in to_x:
        step.wait()
    line[...] = sums[rows_of(32 * at_x, 32), :] + by_x[0] + by_x[1] + by_x[2]
    to_y = [
        send(line.at[rows_of(8 * lax.rem(at_y + k, 4), 8)], by_y.at[k - 1], y_sems, k - 1, y_peer(k)) for k in (1, 2, 3)
    ]
    for step in to_y:
        step.start()
    for step in to_y:
        step.wait()
    piece[...] = line[rows_of(8 * at_y, 8), :] + by_y[0] + by_y[1] + by_y[2]
    to_z = send(piece, by_z, z_sems, 0, z_peer)
    to_z.start()
    to_z.wait()
    small = rows_of(32 * at_x + 8 * at_y, 8)
    reduced[small, :] = piece[...] + by_z[...]
    back_y = [send(reduced.at[small], reduced.at[small], y_back_sems, k - 1, y_peer(k)) for k in (1, 2, 3)]
    for step in back_y:
        step.start()
    for step in back_y:
        step.wait()
    large = rows_of(32 * at_x, 32)
    back_x = [send(reduced.at[large], reduced.at[large], x_back_sems, k - 1, x_peer(k)) for k in (1, 2, 3)]
    for step in back_x:
        step.start()
    for step in back_x:
        step.wait()
    to_band = [
        send(reduced, everyone.at[band], band_sems, k - 1, {"band": lax.rem(band + k, N_BAND)}) for k in (1, 2, 3)
    ]
    for step in to_band:
        step.start()
    everyone[band] = reduced[...]
    for step in to_band:
        step.wait()

    def part(b, r, c):
        size = BANDS_DEV
        return everyone[b, r * size : (r + 1) * size, c * size : (c + 1) * size] * (1.0 / owned)

    margin = {(b, b): part(b, 0, 0) for b in range(N_BAND)}
    margin[1, 0], margin[3, 2] = part(1, 0, 1), part(3, 0, 1)
    margin[2, 0] = part(0, 1, 0) + part(2, 1, 0).T
    margin[2, 1] = part(0, 1, 1) + part(3, 1, 1).T
    margin[3, 0] = part(1, 1, 1) + part(2, 1, 1).T
    margin[3, 1] = part(1, 1, 0) + part(3, 1, 0).T

    inverses, factor, whole = [], {}, {}
    for k in range(N_BAND):
        diagonal = inverse_of_block(margin[k, k])
        inverses.append(diagonal)
        for i in range(k + 1, N_BAND):
            factor[i, k] = exact_dot_t(margin[i, k], diagonal)
        for i in range(k + 1, N_BAND):
            for j in range(k + 1, i + 1):
                margin[i, j] = margin[i, j] - exact_dot_t(factor[i, k], factor[j, k])
        whole[k, k] = diagonal
        for j in range(k):
            total = exact_dot(factor[k, j], whole[j, j])
            for m in range(j + 1, k):
                total = total + exact_dot(factor[k, m], whole[m, j])
            whole[k, j] = -exact_dot(diagonal, total)
        if k == 2:
            second.wait()
            forward_second.start()
    padding = jnp.zeros((BANDS_DEV, LANES - BANDS_DEV), jnp.float32)
    for i in range(N_BAND):
        for j in range(N_BAND):
            if j <= i:
                inverse[i, j] = jnp.concatenate([whole[i, j], padding], axis=1)
            else:
                inverse[i, j] = jnp.zeros((BANDS_DEV, LANES), jnp.float32)
    forward_first.wait()
    forward_second.wait()

    panels = [inverse[band, source] for source in (band, mate, across, across_mate)]
    left = jnp.concatenate(
        [
            jnp.concatenate(panels, axis=1),
            jnp.concatenate([pltpu.roll(panel, HALF, 1) for panel in panels], axis=1),
        ],
        axis=0,
    )
    left_high, left_low = split(left)
    left = jnp.concatenate([left_high, left_high, left_low], axis=1)

    def rotate(i, carry):
        rows = block_rows(i)
        right = jnp.concatenate([ref[rows, :] for ref in (own, partner, cross, partner_cross)], axis=1)
        right_high, right_low = split(right)
        rotated = lax.dot_general(
            left,
            jnp.concatenate([right_high, right_low, right_high], axis=1),
            (((1,), (1,)), ((), ())),
            preferred_element_type=jnp.float32,
        )
        out[:, rows] = rotated[:BANDS_DEV]
        out[:, pl.ds(pl.multiple_of(PAIRS + i * BLOCK, BLOCK), BLOCK)] = rotated[BANDS_DEV:]
        return carry

    lax.fori_loop(0, PAIRS // BLOCK, rotate, 0)


def finish(packed, weight, owned_count):
    whole = pl.BlockSpec(memory_space=pltpu.VMEM)
    nodes = pltpu.VMEM((PAIRS, LANES), jnp.float32)

    def small(*shape):
        return pltpu.VMEM(shape, jnp.float32)

    def sems(slots):
        return pltpu.SemaphoreType.DMA((2, slots))

    return pl.pallas_call(
        functools.partial(finish_kernel, owned_count),
        out_shape=jax.ShapeDtypeStruct((BANDS_DEV, 2 * PAIRS), jnp.float32),
        in_specs=[whole, whole],
        out_specs=whole,
        scratch_shapes=[
            nodes, nodes, nodes,
            small(LANES, LANES), small(3, 32, LANES), small(3, 8, LANES), small(32, LANES), small(8, LANES),
            small(8, LANES), small(LANES, LANES), small(N_BAND, LANES, LANES),
            small(N_BAND, N_BAND, BANDS_DEV, LANES),
            sems(1), sems(2), sems(2), sems(3), sems(3), sems(1), sems(3), sems(3), sems(3),
        ],
        compiler_params=pltpu.CompilerParams(
            collective_id=1, has_side_effects=True, vmem_limit_bytes=48 * 2**20
        ),
        name="finish",
    )(packed, weight)


def shards(
    wavefunctions, stiffness, cell_scale, cell_potential, connectivity, lower_face, upper_face
):
    node_count = wavefunctions.shape[1]
    face_count = lower_face.shape[0]
    space_count = lax.axis_size("space")
    owned_count = node_count * space_count - face_count * (space_count - 1)

    coefficients = jnp.stack([cell_scale, cell_potential])
    index, scale, potential, stiff = make_layout(connectivity, coefficients, stiffness)
    cells = filter_cells(index, wavefunctions, stiff, scale, potential)
    packed, weight = scatter_nodes(index, cells)
    return finish(packed, weight, owned_count)[:, :node_count]


def solution(mesh):
    placed = (
        P("band", "space"),
        P(),
        P("space"),
        P("space"),
        P(None, "space"),
        P("space"),
        P("space"),
    )
    return jax.shard_map(
        shards, mesh=mesh, in_specs=placed, out_specs=P("band", "space"), check_vma=False
    )
```

```python
import functools

import jax
import jax.numpy as jnp
import numpy as np
from jax import lax
from jax.experimental import pallas as pl
from jax.experimental.pallas import tpu as pltpu
from jax.sharding import PartitionSpec as P

FILTER_DEG = 4
GLL_WEIGHTS = (0.1, 49.0 / 90.0, 32.0 / 45.0, 49.0 / 90.0, 0.1)
CENTER = 11.0
HALF_WIDTH = 9.0
HIGHEST = lax.Precision.HIGHEST
MESH = pl.DeviceIdType.MESH

CELLS_Y = 20
CELLS_Z = 6
CHUNKS = CELLS_Y // 2
TILES = CHUNKS * CELLS_Z
SLOTS = 2 * TILES
HALF = 64
LANES = 128
ROWS = 128
PLANE = 24
CORNERS = 5 * PLANE
MESSAGE = 2 * CELLS_Z + 1
EDGE = CELLS_Z + 1

NODES = 10125
PAIRS = 5120
BLOCK = 256
PIECES = 5
GROUPS = 2 * PAIRS // LANES
PLANE_PEERS = 16
BANDS_DEV = 64
N_BAND = 4


def row_of_node(a, b, c):
    if (b, c) == (4, 4):
        return CORNERS + a
    rows = {(0, 0): 0, (4, 0): 8, (0, 4): 16, (1, 1): 7, (1, 2): 15, (1, 3): 23}
    for k in (1, 2, 3):
        rows[(0, k)] = k
        rows[(4, k)] = 8 + k
        rows[(k, 0)] = 3 + k
        rows[(k, 4)] = 16 + 3 + k
        rows[(2, k)] = 8 + 3 + k
        rows[(3, k)] = 16 + k
    return PLANE * a + rows[(b, c)]


def node_rows(planes, chosen):
    return [
        (25 * a + 5 * b + c, row_of_node(a, b, c))
        for a in planes for b in range(5) for c in range(5) if chosen(b, c)
    ]


LOCAL_ROWS = [row for _, row in node_rows(range(5), lambda b, c: True)]


def owners():
    owned = np.zeros((LANES, SLOTS), np.float32)
    for slot in range(SLOTS):
        tile, half = divmod(slot, 2)
        last_y = half == 1 and tile >= TILES - CELLS_Z
        last_z = tile % CELLS_Z == CELLS_Z - 1
        for node, _ in node_rows(range(5), lambda b, c: (b < 4 or last_y) and (c < 4 or last_z)):
            owned[node, slot] = 1.0
    return owned


def place_codes():
    codes = np.zeros((LANES, LANES), np.float32)
    codes[:125, :] = 2.0 * np.array(LOCAL_ROWS)[:, None] + np.arange(LANES)[None, :] % 2
    return codes


def row_selector():
    chosen = np.zeros((ROWS, 125), np.float32)
    chosen[LOCAL_ROWS, np.arange(125)] = 1.0
    return chosen


def row_mass():
    weights = np.array(GLL_WEIGHTS, np.float32)
    mass = (weights[:, None, None] * weights[None, :, None] * weights[None, None, :]).reshape(-1)
    spread = np.zeros((ROWS, LANES), np.float32)
    spread[LOCAL_ROWS, :] = mass[:, None]
    return spread


def local(a, b, c):
    return 25 * a + 5 * b + c


def exact_dot(x, y):
    return jnp.dot(x, y, precision=HIGHEST, preferred_element_type=jnp.float32)


def chain_counts(before, doublings):
    size = before.shape[0]
    eye = (
        lax.broadcasted_iota(jnp.int32, (size, size), 0) == lax.broadcasted_iota(jnp.int32, (size, size), 1)
    ).astype(jnp.float32)
    total, power = eye + before, before
    for _ in range(doublings):
        power = jnp.dot(power, power, preferred_element_type=jnp.float32)
        total = total + jnp.dot(total, power, preferred_element_type=jnp.float32)
    return jnp.sum(total, axis=0, keepdims=True) - 1.0


def layout_kernel(
    conn_ref, cell_scale_ref, cell_potential_ref, stiff_ref, select_ref, owned_ref,
    index_ref, keys_ref, scale_ref, potential_ref, stiffness_ref,
):
    conn = conn_ref[...].astype(jnp.float32)
    cells = conn.shape[1]
    on_rows = lax.broadcasted_iota(jnp.int32, (cells, cells), 0)
    on_lanes = lax.broadcasted_iota(jnp.int32, (cells, cells), 1)

    def as_column(row):
        return jnp.sum(jnp.where(on_rows == on_lanes, row, 0.0), axis=1, keepdims=True)

    def row_of(node):
        return conn[node : node + 1, :]

    after_z = (as_column(row_of(local(2, 2, 4))) == row_of(local(2, 2, 0))).astype(jnp.float32)
    after_y = (as_column(row_of(local(2, 4, 2))) == row_of(local(2, 0, 2))).astype(jnp.float32)
    at_z = chain_counts(after_z, 2)
    at_y = chain_counts(after_y, 4)
    upper_half = at_y >= CHUNKS
    tile = (at_y - jnp.where(upper_half, 1.0 * CHUNKS, 0.0)) * CELLS_Z + at_z
    slot = 2.0 * tile + jnp.where(upper_half, 1.0, 0.0)
    moved = (as_column(slot) == on_lanes.astype(jnp.float32)).astype(jnp.float32)
    index = (exact_dot(conn, moved) + 0.5).astype(jnp.int32)
    index_ref[...] = index
    index = jnp.concatenate([index, jnp.zeros((LANES - index.shape[0], cells), jnp.int32)], axis=0)
    keys = jnp.where(owned_ref[...] > 0.5, index, -1)
    keys_ref[...] = jnp.concatenate([keys, jnp.full((LANES, LANES - cells), -1, jnp.int32)], axis=1)

    wanted = lax.broadcasted_iota(jnp.int32, (TILES, cells), 0).astype(jnp.float32)
    lane = lax.broadcasted_iota(jnp.int32, (TILES, LANES), 1)

    def spread(row):
        low, high = [
            jnp.sum(jnp.where(slot == 2.0 * wanted + half, row, 0.0), axis=1, keepdims=True) for half in (0.0, 1.0)
        ]
        return jnp.where(lane < HALF, low, high)

    scale_ref[...] = spread(cell_scale_ref[...])
    potential_ref[...] = spread(cell_potential_ref[...])

    select = select_ref[...]
    part = exact_dot(select, stiff_ref[...])
    stiff = lax.dot_general(
        part, select, (((1,), (1,)), ((), ())), precision=HIGHEST, preferred_element_type=jnp.float32
    )
    high = stiff.astype(jnp.bfloat16)
    low = (stiff - high.astype(jnp.float32)).astype(jnp.bfloat16)
    stiffness_ref[...] = jnp.concatenate(
        [jnp.concatenate([high, high], axis=1), jnp.concatenate([low, low], axis=1)], axis=0
    )


def make_layout(connectivity, cell_scale, cell_potential, stiffness):
    cells = connectivity.shape[1]
    whole = pl.BlockSpec(memory_space=pltpu.VMEM)
    return pl.pallas_call(
        layout_kernel,
        out_shape=(
            jax.ShapeDtypeStruct((125, cells), jnp.int32),
            jax.ShapeDtypeStruct((LANES, LANES), jnp.int32),
            jax.ShapeDtypeStruct((TILES, LANES), jnp.float32),
            jax.ShapeDtypeStruct((TILES, LANES), jnp.float32),
            jax.ShapeDtypeStruct((2 * ROWS, 2 * ROWS), jnp.bfloat16),
        ),
        in_specs=[whole] * 6,
        out_specs=(whole,) * 5,
        name="layout",
    )(connectivity, cell_scale[None, :], cell_potential[None, :], stiffness, row_selector(), owners())


def each_node_once(planes, visit):
    def loop(count, tile_of, nodes, halves=(0, 1)):
        def body(i, carry):
            visit(tile_of(i), nodes, halves)
            return carry

        lax.fori_loop(0, count, body, 0)

    loop(TILES, lambda i: i, node_rows(planes, lambda b, c: b < 4 and c < 4))
    loop(CELLS_Z, lambda i: TILES - CELLS_Z + i, node_rows(planes, lambda b, c: b == 4 and c < 4), (1,))
    loop(1, lambda i: TILES - 1, node_rows(planes, lambda b, c: b == 4 and c == 4), (1,))
    loop(CHUNKS, lambda i: i * CELLS_Z + CELLS_Z - 1, node_rows(planes, lambda b, c: b < 4 and c == 4))


def filter_kernel(
    index_vector_ref, keys_ref, codes_ref, waves_ref, stiff_ref, mass_ref, scale_ref, potential_ref, out_ref, table_ref,
    index_ref, other, product, face, doubled, sends, edge_sends, receives, edge_receives,
    send_sems, receive_sems, edge_send_sems, edge_receive_sems, index_sem,
):
    count = lax.axis_size("space")
    me = lax.axis_index("space")
    above, below = lax.rem(me + 1, count), lax.rem(me + count - 1, count)
    has_below, has_above = me > 0, me < count - 1

    barrier = pltpu.get_barrier_semaphore()
    for neighbour in (below, above):
        pl.semaphore_signal(barrier, inc=1, device_id={"space": neighbour}, device_id_type=MESH)
    pl.semaphore_wait(barrier, 2)

    sub = lax.broadcasted_iota(jnp.int32, (8, LANES), 0)
    lane = lax.broadcasted_iota(jnp.int32, (8, LANES), 1)
    corner = sub == 0
    along_y = sub <= 3
    along_z = corner | ((sub >= 4) & (sub <= 6))
    in_y_group = (sub >= 4) & (sub <= 6)
    in_z_group = ((sub >= 1) & (sub <= 3)) | (sub == 7)
    low_half = lane < HALF
    corners = slice(CORNERS, CORNERS + 8)
    last_tile = TILES - 1
    bottom, top = 0, 4
    inner = (1, 2, 3)

    def group(a, g):
        return slice(PLANE * a + 8 * g, PLANE * a + 8 * g + 8)

    def turn(value, by):
        return pltpu.roll(value, by % 8, 0) if by % 8 else value

    def over_chunks(body):
        def step(c, carry):
            body(c)
            return carry

        lax.fori_loop(0, CHUNKS, step, 0)

    def message(step, way, c):
        return pltpu.make_async_remote_copy(
            src_ref=sends.at[way, c],
            dst_ref=receives.at[step, way, c],
            send_sem=send_sems.at[step, way, c],
            recv_sem=receive_sems.at[step, way, c],
            device_id={"space": above if way == 0 else below},
            device_id_type=MESH,
        )

    def edge_message(step, way):
        return pltpu.make_async_remote_copy(
            src_ref=edge_sends.at[way],
            dst_ref=edge_receives.at[step, way],
            send_sem=edge_send_sems.at[step, way],
            recv_sem=edge_receive_sems.at[step, way],
            device_id={"space": above if way == 0 else below},
            device_id_type=MESH,
        )

    def start(copy, way):
        @pl.when(has_above if way == 0 else has_below)
        def _():
            copy.start()

    def finish_copy(copy, way):
        @pl.when(has_above if way == 0 else has_below)
        def _():
            copy.wait_send()

        @pl.when(has_below if way == 0 else has_above)
        def _():
            copy.wait_recv()

    def send_chunk(step, way, c, tiles, ends):
        for z, (own, y, d) in enumerate(tiles):
            sends[way, c, 2 * z] = own
            sends[way, c, 2 * z + 1] = jnp.where(corner, turn(y, 1), jnp.where(in_y_group, y, d))
        sends[way, c, MESSAGE - 1] = tiles[CELLS_Z - 1][2]
        start(message(step, way, c), way)

        @pl.when(c == CHUNKS - 1)
        def _():
            for z in range(CELLS_Z):
                edge_sends[way, z] = tiles[z][1]
            edge_sends[way, EDGE - 1] = ends
            start(edge_message(step, way), way)

    def unpack(step, way, c, z):
        inside = receives[step, way, c, 2 * z + 1]
        y = jnp.where(in_y_group, inside, jnp.where(sub == 7, turn(inside, 7), 0.0))
        d = jnp.where(in_z_group, inside, receives[step, way, c, MESSAGE - 1])
        return [receives[step, way, c, 2 * z], y, d]

    def unpack_corner(step, way):
        return turn(edge_receives[step, way, EDGE - 1], 4)

    def fill(ref, c):
        @pl.when(c == CHUNKS - 1)
        def _():
            end = ref[last_tile, corners, :]
            for a in range(5):
                for z in range(CELLS_Z):
                    ref[TILES + z, group(a, 0), :] = jnp.where(
                        low_half, pltpu.roll(ref[z, group(a, 0), :], HALF, 1), ref[TILES - CELLS_Z + z, group(a, 1), :]
                    )
                ref[TILES + CELLS_Z - 1, group(a, 2), :] = jnp.where(
                    low_half, pltpu.roll(ref[CELLS_Z - 1, group(a, 2), :], HALF, 1), turn(end, -a)
                )

        first = c * CELLS_Z
        ends = [ref[first + z, corners, :] for z in range(CELLS_Z)]
        for a in range(5):
            y_new = [
                jnp.where(along_y, ref[first + CELLS_Z + z, group(a, 0), :], ref[first + z, group(a, 1), :])
                for z in range(CELLS_Z)
            ]
            for z in range(CELLS_Z):
                ref[first + z, group(a, 1), :] = y_new[z]
                if z < CELLS_Z - 1:
                    ref[first + z, group(a, 2), :] = jnp.where(
                        along_z, ref[first + z + 1, group(a, 0), :], ref[first + z, group(a, 2), :]
                    )
                    ahead = y_new[z + 1]
                else:
                    ahead = ref[first + CELLS_Z + z, group(a, 2), :]
                ends[z] = jnp.where(sub == a, turn(ahead, a), ends[z])
        for z in range(CELLS_Z):
            ref[first + z, corners, :] = ends[z]

    def assembled(c, a):
        tiles, corner_terms = [], []
        for z in range(CELLS_Z):
            t = c * CELLS_Z + z
            own, y, d = [product[t + CELLS_Z, group(a, g), :] for g in range(3)]
            own = own + jnp.where(along_y, product[t, group(a, 1), :], 0.0)
            d = d + jnp.where(corner, turn(product[t, corners, :], -a), 0.0)
            tiles.append([own, y, d])
            corner_terms.append(turn(product[t + CELLS_Z, corners, :], -a))
        for z in range(1, CELLS_Z):
            tiles[z][0] = tiles[z][0] + jnp.where(along_z, tiles[z - 1][2], 0.0)
            tiles[z][1] = tiles[z][1] + jnp.where(corner, corner_terms[z - 1], 0.0)
        return tiles

    def multiply(current, c):
        mass = mass_ref[...]
        for pair in range(CELLS_Z // 2):
            t = c * CELLS_Z + 2 * pair
            values = [current[t], current[t + 1]]
            high, low = split(jnp.concatenate(values, axis=1))
            result = jnp.dot(
                stiff_ref[...], jnp.concatenate([high, low], axis=0), preferred_element_type=jnp.float32
            )
            result = result[:ROWS] + result[ROWS:]
            for k in range(2):
                product[t + CELLS_Z + k] = result[:, k * LANES : (k + 1) * LANES] * scale_ref[
                    pl.ds(t + k, 1), :
                ] + mass * potential_ref[pl.ds(t + k, 1), :] * values[k]

        @pl.when(c == CHUNKS - 1)
        def _():
            for z in range(CELLS_Z):
                for rows in [group(a, 1) for a in range(5)] + [corners]:
                    turned = pltpu.roll(product[TILES + z, rows, :], HALF, 1)
                    product[z, rows, :] = jnp.where(low_half, 0.0, turned)

    def buffers(step):
        return (out_ref, other) if step % 2 == 0 else (other, out_ref)

    def factor(step):
        return (1.0 if step == 0 else 2.0) / HALF_WIDTH

    def advance(step, t, rows, total):
        current, previous = buffers(step)
        value = (total - CENTER * current[t, rows, :]) * factor(step)
        previous[t, rows, :] = value if step == 0 else value - previous[t, rows, :]

    def assemble(step, c):
        ends = product[TILES + CELLS_Z - 1, corners, :]
        for way, a in ((0, top), (1, bottom)):
            tiles = assembled(c, a)
            for z in range(CELLS_Z):
                for g in range(3):
                    face[way, c * CELLS_Z + z, 8 * g : 8 * g + 8, :] = tiles[z][g]
            send_chunk(step + 1, way, c, tiles, ends)
        for a in inner:
            tiles = assembled(c, a)
            for z in range(CELLS_Z):
                for g in range(3):
                    advance(step, c * CELLS_Z + z, group(a, g), tiles[z][g])

    def advance_faces(step, c):
        for way, a, valid in ((0, bottom, has_below), (1, top, has_above)):
            finish_copy(message(step + 1, way, c), way)
            for z in range(CELLS_Z):
                t = c * CELLS_Z + z
                arrived = unpack(step + 1, way, c, z)
                for g in range(3):
                    total = face[1 - way, t, 8 * g : 8 * g + 8, :] + jnp.where(valid, arrived[g], 0.0)
                    advance(step, t, group(a, g), total)

        @pl.when(c == CHUNKS - 1)
        def _():
            previous = buffers(step)[1]
            ends = product[TILES + CELLS_Z - 1, corners, :]
            for way, a, valid in ((0, bottom, has_below), (1, top, has_above)):
                finish_copy(edge_message(step + 1, way), way)
                for z in range(CELLS_Z):
                    rows = group(a, 1)
                    edge = jnp.where(along_y & valid, edge_receives[step + 1, way, z], 0.0)
                    previous[TILES - CELLS_Z + z, rows, :] = previous[TILES - CELLS_Z + z, rows, :] + factor(step) * edge
                ends = ends + jnp.where((sub == a) & valid, unpack_corner(step + 1, way), 0.0)
            advance(step, last_tile, corners, ends)

    def tabulate():
        high = lax.broadcasted_iota(jnp.int32, (GROUPS, LANES), 0)
        low = lax.broadcasted_iota(jnp.int32, (LANES, LANES), 0)
        tile = (lax.broadcasted_iota(jnp.int32, (1, LANES), 1) // 2).astype(jnp.float32)

        def body(i, total):
            left, right = [], []
            for k in range(2):
                at = pl.ds(2 * i + k, 1)
                key = keys_ref[at, :]
                left.append(jnp.where(high == key >> 7, 1.0, 0.0).astype(jnp.bfloat16))
                hit = low == key & (LANES - 1)
                values = [jnp.where(hit, tile, 0.0), jnp.where(hit, codes_ref[at, :], 0.0)]
                right.append(jnp.concatenate(values, axis=0).astype(jnp.bfloat16))
            return total + lax.dot_general(
                jnp.concatenate(left, axis=1),
                jnp.concatenate(right, axis=1),
                (((1,), (1,)), ((), ())),
                preferred_element_type=jnp.float32,
            )

        total = lax.fori_loop(0, LANES // 2, body, jnp.zeros((GROUPS, 2 * LANES), jnp.float32)) + 0.5
        tiles = total[:, :LANES].astype(jnp.int32)
        codes = total[:, LANES:].astype(jnp.int32)
        node = high * LANES + lax.broadcasted_iota(jnp.int32, (GROUPS, LANES), 1)
        place = (codes & 1) * (TILES * ROWS) + tiles * ROWS + (codes >> 1)
        table_ref[...] = jnp.where(node < NODES, place, CORNERS + 5)

    index_copy = pltpu.make_async_copy(index_vector_ref, index_ref, index_sem)
    index_copy.start()
    node_count = waves_ref.shape[1]
    whole_blocks = node_count // LANES

    def transpose(i, carry):
        at = pl.ds(pl.multiple_of(i * LANES, LANES), LANES)
        block = waves_ref[:, at]
        doubled[at, :] = jnp.concatenate([block, block], axis=0).T
        return carry

    lax.fori_loop(0, whole_blocks, transpose, 0)
    rest = node_count - whole_blocks * LANES
    block = jnp.concatenate(
        [waves_ref[:, whole_blocks * LANES :], jnp.zeros((HALF, LANES - rest), jnp.float32)], axis=1
    )
    doubled[whole_blocks * LANES : (whole_blocks + 1) * LANES, :] = jnp.concatenate([block, block], axis=0).T

    out_ref[...] = jnp.zeros_like(out_ref)
    low_row = lax.broadcasted_iota(jnp.int32, (1, LANES), 1) < HALF

    def gather(t, nodes, halves):
        for node, row in nodes:
            first = doubled[pl.ds(index_ref[node, 2 * t], 1), :]
            second = doubled[pl.ds(index_ref[node, 2 * t + 1], 1), :]
            out_ref[t, row : row + 1, :] = jnp.where(low_row, first, second)

    index_copy.wait()
    each_node_once((top,), gather)

    def send_owner(c):
        tiles = [[out_ref[c * CELLS_Z + z, group(top, g), :] for g in range(3)] for z in range(CELLS_Z)]
        send_chunk(0, 0, c, tiles, out_ref[last_tile, corners, :])

    over_chunks(send_owner)
    each_node_once((0, 1, 2, 3), gather)
    other[...] = jnp.zeros_like(other)

    def take_owner(c):
        finish_copy(message(0, 0, c), 0)
        for z in range(CELLS_Z):
            t = c * CELLS_Z + z
            arrived = unpack(0, 0, c, z)
            for g in range(3):
                out_ref[t, group(bottom, g), :] = jnp.where(has_below, arrived[g], out_ref[t, group(bottom, g), :])

    over_chunks(take_owner)
    finish_copy(edge_message(0, 0), 0)
    for z in range(CELLS_Z):
        t = TILES - CELLS_Z + z
        out_ref[t, group(bottom, 1), :] = jnp.where(
            along_y & has_below, edge_receives[0, 0, z], out_ref[t, group(bottom, 1), :]
        )
    out_ref[last_tile, corners, :] = jnp.where(
        (sub == bottom) & has_below, unpack_corner(0, 0), out_ref[last_tile, corners, :]
    )
    over_chunks(lambda c: fill(out_ref, c))

    multiply(out_ref, CHUNKS - 1)

    def first_step(c):
        multiply(out_ref, c)
        assemble(0, c)

    lax.fori_loop(0, CHUNKS - 1, lambda c, carry: (first_step(c), carry)[1], 0)
    assemble(0, CHUNKS - 1)
    tabulate()

    for step in range(1, FILTER_DEG):
        base = step - 1
        current = buffers(step)[0]

        def refresh(c):
            fill(current, c)
            multiply(current, c)

        def next_chunk(i, carry):
            advance_faces(step - 1, lax.rem(base + i, CHUNKS))
            c = lax.rem(base + i - 1, CHUNKS)
            refresh(c)
            assemble(step, c)
            return carry

        advance_faces(step - 1, base)
        advance_faces(step - 1, base + 1)
        refresh(base)
        lax.fori_loop(2, CHUNKS, next_chunk, 0)
        refresh((base + CHUNKS - 1) % CHUNKS)
        assemble(step, (base + CHUNKS - 1) % CHUNKS)
        assemble(step, base)

    last = FILTER_DEG - 1
    lax.fori_loop(
        0, CHUNKS, lambda i, carry: (advance_faces(last, lax.rem(last + i, CHUNKS)), carry)[1], 0
    )


def filter_cells(index, keys, wavefunctions, stiff, scale, potential):
    whole = pl.BlockSpec(memory_space=pltpu.VMEM)
    cells = (TILES + CELLS_Z, ROWS, LANES)
    rounds = FILTER_DEG + 1
    blocks = wavefunctions.shape[1] // LANES + 1
    return pl.pallas_call(
        filter_kernel,
        out_shape=(
            jax.ShapeDtypeStruct(cells, jnp.float32), jax.ShapeDtypeStruct((GROUPS, LANES), jnp.int32)
        ),
        in_specs=[whole] * 8,
        out_specs=(whole, whole),
        scratch_shapes=[
            pltpu.SMEM(index.shape, jnp.int32),
            pltpu.VMEM(cells, jnp.float32),
            pltpu.VMEM(cells, jnp.float32),
            pltpu.VMEM((2, TILES, PLANE, LANES), jnp.float32),
            pltpu.VMEM((blocks * LANES, LANES), jnp.float32),
            pltpu.VMEM((2, CHUNKS, MESSAGE, 8, LANES), jnp.float32),
            pltpu.VMEM((2, EDGE, 8, LANES), jnp.float32),
            pltpu.VMEM((rounds, 2, CHUNKS, MESSAGE, 8, LANES), jnp.float32),
            pltpu.VMEM((rounds, 2, EDGE, 8, LANES), jnp.float32),
            pltpu.SemaphoreType.DMA((rounds, 2, CHUNKS)),
            pltpu.SemaphoreType.DMA((rounds, 2, CHUNKS)),
            pltpu.SemaphoreType.DMA((rounds, 2)),
            pltpu.SemaphoreType.DMA((rounds, 2)),
            pltpu.SemaphoreType.DMA(()),
        ],
        compiler_params=pltpu.CompilerParams(
            collective_id=0, has_side_effects=True, vmem_limit_bytes=56 * 2**20
        ),
        name="filter_cells",
    )(index, keys, place_codes(), wavefunctions, stiff, row_mass(), scale, potential)


def split(x):
    high = x.astype(jnp.bfloat16)
    return high, (x - high.astype(jnp.float32)).astype(jnp.bfloat16)


def exact_dot_t(x, y):
    return lax.dot_general(
        x, y, (((1,), (1,)), ((), ())), precision=HIGHEST, preferred_element_type=jnp.float32
    )


def inverse_of_block(block):
    size = BANDS_DEV
    row_at = lax.broadcasted_iota(jnp.int32, (size, LANES), 0)
    lane = lax.broadcasted_iota(jnp.int32, (size, LANES), 1)
    wide = jnp.concatenate([block, jnp.zeros((size, LANES - size), jnp.float32)], axis=1)
    wide = jnp.where(lane == row_at + size, 1.0, wide)
    tiles = [wide[8 * g : 8 * g + 8] for g in range(size // 8)]
    sub = lax.broadcasted_iota(jnp.int32, (8, LANES), 0)
    for home in range(size // 8):
        live = range(home, size // 8)
        columns = {
            (g, n): jnp.broadcast_to(tiles[g][:, 8 * home + n : 8 * home + n + 1], (8, LANES))
            for g in live for n in range(8)
        }
        for at in range(8):
            scale = 1.0 / columns[home, at][at : at + 1, :]
            ratio = tiles[home][at : at + 1, :] * scale
            ahead = {n: columns[home, n][at : at + 1, :] * scale for n in range(at + 1, 8)}
            for g in live:
                factor = columns[g, at]
                if g == home:
                    factor = jnp.where(sub > at, factor, 0.0)
                for n in range(at + 1, 8):
                    columns[g, n] = columns[g, n] - factor * ahead[n]
                tiles[g] = tiles[g] - factor * ratio
    wide = jnp.concatenate(tiles, axis=0)
    pivots = jnp.sum(jnp.where(lane == row_at, wide, 0.0), axis=1, keepdims=True)
    return wide[:, size:] * (1.0 / jnp.sqrt(pivots))


def finish_kernel(
    owned, cells, table_vector, out, table, low_rows, high_rows, own, weight, partner, cross, partner_cross,
    sums, by_plane, piece, by_z, everyone, inverse,
    table_sem, pair_sems, first_sems, second_sems, forward_sems, again_sems, plane_sems, z_sems, band_sems, back_sems,
):
    table_copy = pltpu.make_async_copy(table_vector, table, table_sem)
    table_copy.start()
    space, band = lax.axis_index("space"), lax.axis_index("band")
    at_plane = lax.rem(space, PLANE_PEERS)
    core = lax.rem(band, 2)
    chip = band // 2
    mate = band + 1 - 2 * core
    across = lax.rem(band + 2, N_BAND)
    across_mate = lax.rem(mate + 2, N_BAND)

    def plane_peer(k):
        return {"space": space - at_plane + lax.rem(at_plane + k, PLANE_PEERS)}

    z_peer = {"space": lax.rem(space + PLANE_PEERS, 2 * PLANE_PEERS)}
    band_peers = [{"band": lax.rem(band + k, N_BAND)} for k in (1, 2, 3)]
    barrier = pltpu.get_barrier_semaphore()
    peers = [plane_peer(k) for k in range(1, PLANE_PEERS)] + [z_peer] + band_peers
    for peer in peers:
        pl.semaphore_signal(barrier, inc=1, device_id=peer, device_id_type=MESH)

    def send(source, target, sems, slot, peer):
        return pltpu.make_async_remote_copy(
            src_ref=source,
            dst_ref=target,
            send_sem=sems.at[0, slot],
            recv_sem=sems.at[1, slot],
            device_id=peer,
            device_id_type=MESH,
        )

    row_at = lax.broadcasted_iota(jnp.int32, (ROWS, LANES), 0)
    left_half = lax.broadcasted_iota(jnp.int32, (ROWS, LANES), 1) < HALF
    shared = ((row_at < PLANE) | (row_at == CORNERS)) & (space > 0)
    row_weight = jnp.where(shared | (row_at >= CORNERS + 5), 0.0, 1.0)

    def spread(t, carry):
        values = cells[t]
        turned = pltpu.roll(values, HALF, 1)
        for half, (left, right) in enumerate(((values, turned), (turned, values))):
            rows = pl.ds(pl.multiple_of((half * TILES + t) * ROWS, ROWS), ROWS)
            low_rows[rows, :] = jnp.where(left_half, left, row_weight)
            high_rows[rows, :] = jnp.where(left_half, row_weight, right)
        return carry

    lax.fori_loop(0, TILES, spread, 0)
    table_copy.wait()
    low_lane = lax.broadcasted_iota(jnp.int32, (1, LANES), 1) < HALF

    def gather(i):
        start = pl.multiple_of(i * LANES, LANES)
        for k in range(LANES):
            first = low_rows[pl.ds(table[i, k], 1), :]
            second = high_rows[pl.ds(table[i + GROUPS // 2, k], 1), :]
            own[pl.ds(start + k, 1), :] = jnp.where(low_lane, first, second)
            weight[pl.ds(start + k, 1), :] = jnp.where(low_lane, second, first)

    half = PAIRS // 2
    size = half // PIECES

    def piece_rows(side, p):
        return pl.ds(pl.multiple_of(side * half + p * size, size), size)

    to_mate, to_across = {"band": mate}, {"band": across}
    pieces = range(PIECES)
    first = [
        send(own.at[piece_rows(chip, p)], cross.at[piece_rows(chip, p)], first_sems, p, to_across) for p in pieces
    ]
    second = [
        send(own.at[piece_rows(1 - chip, p)], cross.at[piece_rows(1 - chip, p)], second_sems, p, to_across)
        for p in pieces
    ]
    forward_first = [
        send(cross.at[piece_rows(1 - chip, p)], partner_cross.at[piece_rows(1 - chip, p)], forward_sems, p, to_mate)
        for p in pieces
    ]
    forward_second = [
        send(cross.at[piece_rows(chip, p)], partner_cross.at[piece_rows(chip, p)], again_sems, p, to_mate)
        for p in pieces
    ]
    pair = send(own, partner, pair_sems, 0, to_mate)

    groups = GROUPS // 4
    per_piece = groups // PIECES
    pl.semaphore_wait(barrier, len(peers))
    for p in pieces:
        base = chip * groups + p * per_piece
        lax.fori_loop(0, per_piece, lambda i, carry, base=base: (gather(base + i), carry)[1], 0)
        first[p].start()
    lax.fori_loop(0, groups, lambda i, carry: (gather((1 - chip) * groups + i), carry)[1], 0)
    pair.start()
    pair.wait()

    def products(left, right):
        left_high, left_low = split(left)
        right_high, right_low = split(right)
        return lax.dot_general(
            jnp.concatenate([left_high, left_high, left_low], axis=0),
            jnp.concatenate([right_high, right_low, right_high], axis=0),
            (((0,), (0,)), ((), ())),
            preferred_element_type=jnp.float32,
        )

    def block_rows(i):
        return pl.ds(pl.multiple_of(i * BLOCK, BLOCK), BLOCK)

    def own_terms(i, total):
        rows = block_rows(i)
        mine = own[rows, :]
        scale = pltpu.roll(weight[rows, :], HALF, 1)
        return total + products(mine * scale, jnp.concatenate([mine, partner[rows, :]], axis=1))

    def cross_terms(i, total):
        rows = block_rows(i)
        scale = pltpu.roll(weight[rows, :], HALF, 1)
        return total + products(
            cross[rows, :], jnp.concatenate([own[rows, :] * scale, partner[rows, :] * scale], axis=1)
        )

    low_half = lax.broadcasted_iota(jnp.int32, (BANDS_DEV, LANES), 1) < HALF

    def fold(total):
        size = BANDS_DEV
        left = total[:size, :LANES] + pltpu.roll(total[size:, :LANES], HALF, 1)
        right = pltpu.roll(total[:size, LANES:], HALF, 1) + total[size:, LANES:]
        return jnp.where(low_half, left, right)

    zero = jnp.zeros((LANES, 2 * LANES), jnp.float32)
    sums[0:BANDS_DEV, :] = fold(lax.fori_loop(0, PAIRS // BLOCK, own_terms, zero))
    blocks = size // BLOCK
    total = zero
    for p in pieces:
        first[p].wait()
        forward_first[p].start()
        base = (1 - chip) * (half // BLOCK) + p * blocks
        total = lax.fori_loop(0, blocks, lambda i, total, base=base: cross_terms(base + i, total), total)
    sums[BANDS_DEV : 2 * BANDS_DEV, :] = fold(total)

    second[0].start()

    def rows_of(at):
        return pl.ds(pl.multiple_of(8 * at, 8), 8)

    others = range(1, PLANE_PEERS)
    scatter = [
        send(sums.at[rows_of(lax.rem(at_plane + k, PLANE_PEERS))], by_plane.at[k - 1], plane_sems, k - 1, plane_peer(k))
        for k in others
    ]
    for step in scatter:
        step.start()
    for step in scatter:
        step.wait()
    mine = sums[rows_of(at_plane), :]
    for k in others:
        mine = mine + by_plane[k - 1]
    piece[...] = mine
    to_z = send(piece, by_z, z_sems, 0, z_peer)
    to_z.start()
    to_z.wait()
    everyone[at_plane, band] = piece[...] + by_z[...]
    to_band = [
        send(everyone.at[at_plane, band], everyone.at[at_plane, band], band_sems, k, peer)
        for k, peer in enumerate(band_peers)
    ]
    for step in to_band:
        step.start()
    for step in to_band:
        step.wait()
    for p in pieces[1:]:
        second[p].start()
    back = [send(everyone.at[at_plane], everyone.at[at_plane], back_sems, k - 1, plane_peer(k)) for k in others]
    for step in back:
        step.start()
    for step in back:
        step.wait()

    totals = [
        jnp.concatenate([everyone[q, b] for q in range(PLANE_PEERS)], axis=0) * (1.0 / owned) for b in range(N_BAND)
    ]

    def part(b, r, c):
        size = BANDS_DEV
        return totals[b][r * size : (r + 1) * size, c * size : (c + 1) * size]

    margin = {(b, b): part(b, 0, 0) for b in range(N_BAND)}
    margin[1, 0], margin[3, 2] = part(1, 0, 1), part(3, 0, 1)
    margin[2, 0] = part(0, 1, 0) + part(2, 1, 0).T
    margin[2, 1] = part(0, 1, 1) + part(3, 1, 1).T
    margin[3, 0] = part(1, 1, 1) + part(2, 1, 1).T
    margin[3, 1] = part(1, 1, 0) + part(3, 1, 0).T

    inverses, factor, whole = [], {}, {}
    for k in range(N_BAND):
        diagonal = inverse_of_block(margin[k, k])
        inverses.append(diagonal)
        for i in range(k + 1, N_BAND):
            factor[i, k] = exact_dot_t(margin[i, k], diagonal)
        for i in range(k + 1, N_BAND):
            for j in range(k + 1, i + 1):
                margin[i, j] = margin[i, j] - exact_dot_t(factor[i, k], factor[j, k])
        whole[k, k] = diagonal
        for j in range(k):
            total = exact_dot(factor[k, j], whole[j, j])
            for m in range(j + 1, k):
                total = total + exact_dot(factor[k, m], whole[m, j])
            whole[k, j] = -exact_dot(diagonal, total)
        if k == 2:
            second[0].wait()
            forward_second[0].start()
    padding = jnp.zeros((BANDS_DEV, LANES - BANDS_DEV), jnp.float32)
    for i in range(N_BAND):
        for j in range(N_BAND):
            if j <= i:
                inverse[i, j] = jnp.concatenate([whole[i, j], padding], axis=1)
            else:
                inverse[i, j] = jnp.zeros((BANDS_DEV, LANES), jnp.float32)
    for p in pieces[1:]:
        second[p].wait()
        forward_second[p].start()
    for p in pieces:
        forward_first[p].wait()

    panels = [inverse[band, source] for source in (band, mate, across, across_mate)]
    left = jnp.concatenate(
        [
            jnp.concatenate(panels, axis=1),
            jnp.concatenate([pltpu.roll(panel, HALF, 1) for panel in panels], axis=1),
        ],
        axis=0,
    )
    left_high, left_low = split(left)
    left = jnp.concatenate([left_high, left_high, left_low], axis=1)

    def rotate(i, carry):
        rows = block_rows(i)
        right = jnp.concatenate([ref[rows, :] for ref in (own, partner, cross, partner_cross)], axis=1)
        right_high, right_low = split(right)
        rotated = lax.dot_general(
            left,
            jnp.concatenate([right_high, right_low, right_high], axis=1),
            (((1,), (1,)), ((), ())),
            preferred_element_type=jnp.float32,
        )
        out[:, rows] = rotated[:BANDS_DEV]
        out[:, pl.ds(pl.multiple_of(PAIRS + i * BLOCK, BLOCK), BLOCK)] = rotated[BANDS_DEV:]
        return carry

    done = (1 - chip) * (half // BLOCK)
    lax.fori_loop(0, half // BLOCK, lambda i, carry: rotate(done + i, carry), 0)
    for p in pieces:
        forward_second[p].wait()
        base = chip * (half // BLOCK) + p * blocks
        lax.fori_loop(0, blocks, lambda i, carry, base=base: rotate(base + i, carry), 0)


def finish(cells, table, owned_count):
    whole = pl.BlockSpec(memory_space=pltpu.VMEM)
    nodes = pltpu.VMEM((PAIRS, LANES), jnp.float32)

    def small(*shape):
        return pltpu.VMEM(shape, jnp.float32)

    def sems(slots):
        return pltpu.SemaphoreType.DMA((2, slots))

    return pl.pallas_call(
        functools.partial(finish_kernel, owned_count),
        out_shape=jax.ShapeDtypeStruct((BANDS_DEV, 2 * PAIRS), jnp.float32),
        in_specs=[whole, whole],
        out_specs=whole,
        scratch_shapes=[
            pltpu.SMEM(table.shape, jnp.int32),
            small(2 * TILES * ROWS, LANES), small(2 * TILES * ROWS, LANES),
            nodes, nodes, nodes, nodes, nodes,
            small(LANES, LANES), small(PLANE_PEERS - 1, 8, LANES), small(8, LANES), small(8, LANES),
            small(PLANE_PEERS, N_BAND, 8, LANES),
            small(N_BAND, N_BAND, BANDS_DEV, LANES),
            pltpu.SemaphoreType.DMA(()),
            sems(1), sems(PIECES), sems(PIECES), sems(PIECES), sems(PIECES),
            sems(PLANE_PEERS - 1), sems(1), sems(3), sems(PLANE_PEERS - 1),
        ],
        compiler_params=pltpu.CompilerParams(
            collective_id=1, has_side_effects=True, vmem_limit_bytes=56 * 2**20
        ),
        name="finish",
    )(cells, table)


def shards(
    wavefunctions, stiffness, cell_scale, cell_potential, connectivity, lower_face, upper_face
):
    node_count = wavefunctions.shape[1]
    face_count = lower_face.shape[0]
    space_count = lax.axis_size("space")
    owned_count = node_count * space_count - face_count * (space_count - 1)

    index, keys, scale, potential, stiff = make_layout(connectivity, cell_scale, cell_potential, stiffness)
    cells, table = filter_cells(index, keys, wavefunctions, stiff, scale, potential)
    return finish(cells, table, owned_count)[:, :node_count]


def solution(mesh):
    placed = (
        P("band", "space"),
        P(),
        P("space"),
        P("space"),
        P(None, "space"),
        P("space"),
        P("space"),
    )
    return jax.shard_map(
        shards, mesh=mesh, in_specs=placed, out_specs=P("band", "space"), check_vma=False
    )
```

```python
import functools

import jax
import jax.numpy as jnp
import numpy as np
from jax import lax
from jax.experimental import pallas as pl
from jax.experimental.pallas import tpu as pltpu
from jax.sharding import PartitionSpec as P

FILTER_DEG = 4
GLL_WEIGHTS = (0.1, 49.0 / 90.0, 32.0 / 45.0, 49.0 / 90.0, 0.1)
CENTER = 11.0
HALF_WIDTH = 9.0
HIGHEST = lax.Precision.HIGHEST
MESH = pl.DeviceIdType.MESH

CELLS_Y = 20
CELLS_Z = 6
CHUNKS = CELLS_Y // 2
TILES = CHUNKS * CELLS_Z
SLOTS = 2 * TILES
HALF = 64
LANES = 128
ROWS = 128
PLANE = 24
CORNERS = 5 * PLANE
MESSAGE = 2 * CELLS_Z + 1
EDGE = CELLS_Z + 1

NODES = 10125
PAIRS = 5120
BLOCK = 256
PIECES = 5
CELL_PARTS = 4
GROUPS = 2 * PAIRS // LANES
PLANE_PEERS = 16
BANDS_DEV = 64
N_BAND = 4


def row_of_node(a, b, c):
    if (b, c) == (4, 4):
        return CORNERS + a
    rows = {(0, 0): 0, (4, 0): 8, (0, 4): 16, (1, 1): 7, (1, 2): 15, (1, 3): 23}
    for k in (1, 2, 3):
        rows[(0, k)] = k
        rows[(4, k)] = 8 + k
        rows[(k, 0)] = 3 + k
        rows[(k, 4)] = 16 + 3 + k
        rows[(2, k)] = 8 + 3 + k
        rows[(3, k)] = 16 + k
    return PLANE * a + rows[(b, c)]


def node_rows(planes, chosen):
    return [
        (25 * a + 5 * b + c, row_of_node(a, b, c))
        for a in planes for b in range(5) for c in range(5) if chosen(b, c)
    ]


LOCAL_ROWS = [row for _, row in node_rows(range(5), lambda b, c: True)]


def owners():
    owned = np.zeros((LANES, SLOTS), np.float32)
    for slot in range(SLOTS):
        tile, half = divmod(slot, 2)
        last_y = half == 1 and tile >= TILES - CELLS_Z
        last_z = tile % CELLS_Z == CELLS_Z - 1
        for node, _ in node_rows(range(5), lambda b, c: (b < 4 or last_y) and (c < 4 or last_z)):
            owned[node, slot] = 1.0
    return owned


def place_codes():
    codes = np.zeros((LANES, LANES), np.float32)
    codes[:125, :] = 2.0 * np.array(LOCAL_ROWS)[:, None] + np.arange(LANES)[None, :] % 2
    return codes


def row_selector():
    chosen = np.zeros((ROWS, 125), np.float32)
    chosen[LOCAL_ROWS, np.arange(125)] = 1.0
    return chosen


def row_mass():
    weights = np.array(GLL_WEIGHTS, np.float32)
    mass = (weights[:, None, None] * weights[None, :, None] * weights[None, None, :]).reshape(-1)
    spread = np.zeros((ROWS, LANES), np.float32)
    spread[LOCAL_ROWS, :] = mass[:, None]
    return spread


def local(a, b, c):
    return 25 * a + 5 * b + c


def exact_dot(x, y):
    return jnp.dot(x, y, precision=HIGHEST, preferred_element_type=jnp.float32)


def chain_counts(before, doublings):
    size = before.shape[0]
    eye = (
        lax.broadcasted_iota(jnp.int32, (size, size), 0) == lax.broadcasted_iota(jnp.int32, (size, size), 1)
    ).astype(jnp.float32)
    total, power = eye + before, before
    for _ in range(doublings):
        power = jnp.dot(power, power, preferred_element_type=jnp.float32)
        total = total + jnp.dot(total, power, preferred_element_type=jnp.float32)
    return jnp.sum(total, axis=0, keepdims=True) - 1.0


def layout_kernel(
    conn_ref, cell_scale_ref, cell_potential_ref, stiff_ref, select_ref, owned_ref,
    index_ref, keys_ref, scale_ref, potential_ref, stiffness_ref,
):
    conn = conn_ref[...].astype(jnp.float32)
    cells = conn.shape[1]
    on_rows = lax.broadcasted_iota(jnp.int32, (cells, cells), 0)
    on_lanes = lax.broadcasted_iota(jnp.int32, (cells, cells), 1)

    def as_column(row):
        return jnp.sum(jnp.where(on_rows == on_lanes, row, 0.0), axis=1, keepdims=True)

    def row_of(node):
        return conn[node : node + 1, :]

    after_z = (as_column(row_of(local(2, 2, 4))) == row_of(local(2, 2, 0))).astype(jnp.float32)
    after_y = (as_column(row_of(local(2, 4, 2))) == row_of(local(2, 0, 2))).astype(jnp.float32)
    at_z = chain_counts(after_z, 2)
    at_y = chain_counts(after_y, 4)
    upper_half = at_y >= CHUNKS
    tile = (at_y - jnp.where(upper_half, 1.0 * CHUNKS, 0.0)) * CELLS_Z + at_z
    slot = 2.0 * tile + jnp.where(upper_half, 1.0, 0.0)
    moved = (as_column(slot) == on_lanes.astype(jnp.float32)).astype(jnp.float32)
    index = (exact_dot(conn, moved) + 0.5).astype(jnp.int32)
    index_ref[...] = index
    index = jnp.concatenate([index, jnp.zeros((LANES - index.shape[0], cells), jnp.int32)], axis=0)
    keys = jnp.where(owned_ref[...] > 0.5, index, -1)
    keys_ref[...] = jnp.concatenate([keys, jnp.full((LANES, LANES - cells), -1, jnp.int32)], axis=1)

    wanted = lax.broadcasted_iota(jnp.int32, (TILES, cells), 0).astype(jnp.float32)
    lane = lax.broadcasted_iota(jnp.int32, (TILES, LANES), 1)

    def spread(row):
        low, high = [
            jnp.sum(jnp.where(slot == 2.0 * wanted + half, row, 0.0), axis=1, keepdims=True) for half in (0.0, 1.0)
        ]
        return jnp.where(lane < HALF, low, high)

    scale_ref[...] = spread(cell_scale_ref[...])
    potential_ref[...] = spread(cell_potential_ref[...])

    select = select_ref[...]
    part = exact_dot(select, stiff_ref[...])
    stiff = lax.dot_general(
        part, select, (((1,), (1,)), ((), ())), precision=HIGHEST, preferred_element_type=jnp.float32
    )
    high = stiff.astype(jnp.bfloat16)
    low = (stiff - high.astype(jnp.float32)).astype(jnp.bfloat16)
    stiffness_ref[...] = jnp.concatenate(
        [jnp.concatenate([high, high], axis=1), jnp.concatenate([low, low], axis=1)], axis=0
    )


def make_layout(connectivity, cell_scale, cell_potential, stiffness):
    cells = connectivity.shape[1]
    whole = pl.BlockSpec(memory_space=pltpu.VMEM)
    return pl.pallas_call(
        layout_kernel,
        out_shape=(
            jax.ShapeDtypeStruct((125, cells), jnp.int32),
            jax.ShapeDtypeStruct((LANES, LANES), jnp.int32),
            jax.ShapeDtypeStruct((TILES, LANES), jnp.float32),
            jax.ShapeDtypeStruct((TILES, LANES), jnp.float32),
            jax.ShapeDtypeStruct((2 * ROWS, 2 * ROWS), jnp.bfloat16),
        ),
        in_specs=[whole] * 6,
        out_specs=(whole,) * 5,
        name="layout",
    )(connectivity, cell_scale[None, :], cell_potential[None, :], stiffness, row_selector(), owners())


def each_node_once(planes, visit):
    def loop(count, tile_of, nodes, halves=(0, 1)):
        def body(i, carry):
            visit(tile_of(i), nodes, halves)
            return carry

        lax.fori_loop(0, count, body, 0)

    loop(TILES, lambda i: i, node_rows(planes, lambda b, c: b < 4 and c < 4))
    loop(CELLS_Z, lambda i: TILES - CELLS_Z + i, node_rows(planes, lambda b, c: b == 4 and c < 4), (1,))
    loop(1, lambda i: TILES - 1, node_rows(planes, lambda b, c: b == 4 and c == 4), (1,))
    loop(CHUNKS, lambda i: i * CELLS_Z + CELLS_Z - 1, node_rows(planes, lambda b, c: b < 4 and c == 4))


def filter_kernel(
    index_vector_ref, keys_ref, codes_ref, waves_ref, stiff_ref, mass_ref, scale_ref, potential_ref, out_ref, table_ref,
    index_ref, places, other, product, face, doubled, sends, edge_sends, receives, edge_receives,
    send_sems, receive_sems, edge_send_sems, edge_receive_sems, index_sem,
):
    count = lax.axis_size("space")
    me = lax.axis_index("space")
    above, below = lax.rem(me + 1, count), lax.rem(me + count - 1, count)
    has_below, has_above = me > 0, me < count - 1

    barrier = pltpu.get_barrier_semaphore()
    for neighbour in (below, above):
        pl.semaphore_signal(barrier, inc=1, device_id={"space": neighbour}, device_id_type=MESH)
    pl.semaphore_wait(barrier, 2)

    sub = lax.broadcasted_iota(jnp.int32, (8, LANES), 0)
    lane = lax.broadcasted_iota(jnp.int32, (8, LANES), 1)
    corner = sub == 0
    along_y = sub <= 3
    along_z = corner | ((sub >= 4) & (sub <= 6))
    in_y_group = (sub >= 4) & (sub <= 6)
    in_z_group = ((sub >= 1) & (sub <= 3)) | (sub == 7)
    low_half = lane < HALF
    corners = slice(CORNERS, CORNERS + 8)
    last_tile = TILES - 1
    bottom, top = 0, 4
    inner = (1, 2, 3)

    def group(a, g):
        return slice(PLANE * a + 8 * g, PLANE * a + 8 * g + 8)

    def turn(value, by):
        return pltpu.roll(value, by % 8, 0) if by % 8 else value

    def over_chunks(body):
        def step(c, carry):
            body(c)
            return carry

        lax.fori_loop(0, CHUNKS, step, 0)

    def message(step, way, c):
        return pltpu.make_async_remote_copy(
            src_ref=sends.at[way, c],
            dst_ref=receives.at[step, way, c],
            send_sem=send_sems.at[step, way, c],
            recv_sem=receive_sems.at[step, way, c],
            device_id={"space": above if way == 0 else below},
            device_id_type=MESH,
        )

    def edge_message(step, way):
        return pltpu.make_async_remote_copy(
            src_ref=edge_sends.at[way],
            dst_ref=edge_receives.at[step, way],
            send_sem=edge_send_sems.at[step, way],
            recv_sem=edge_receive_sems.at[step, way],
            device_id={"space": above if way == 0 else below},
            device_id_type=MESH,
        )

    def start(copy, way):
        @pl.when(has_above if way == 0 else has_below)
        def _():
            copy.start()

    def finish_copy(copy, way):
        @pl.when(has_above if way == 0 else has_below)
        def _():
            copy.wait_send()

        @pl.when(has_below if way == 0 else has_above)
        def _():
            copy.wait_recv()

    def send_chunk(step, way, c, tiles, ends):
        for z, (own, y, d) in enumerate(tiles):
            sends[way, c, 2 * z] = own
            sends[way, c, 2 * z + 1] = jnp.where(corner, turn(y, 1), jnp.where(in_y_group, y, d))
        sends[way, c, MESSAGE - 1] = tiles[CELLS_Z - 1][2]
        start(message(step, way, c), way)

        @pl.when(c == CHUNKS - 1)
        def _():
            for z in range(CELLS_Z):
                edge_sends[way, z] = tiles[z][1]
            edge_sends[way, EDGE - 1] = ends
            start(edge_message(step, way), way)

    def unpack(step, way, c, z):
        inside = receives[step, way, c, 2 * z + 1]
        y = jnp.where(in_y_group, inside, jnp.where(sub == 7, turn(inside, 7), 0.0))
        d = jnp.where(in_z_group, inside, receives[step, way, c, MESSAGE - 1])
        return [receives[step, way, c, 2 * z], y, d]

    def unpack_corner(step, way):
        return turn(edge_receives[step, way, EDGE - 1], 4)

    def fill(ref, c):
        @pl.when(c == CHUNKS - 1)
        def _():
            end = ref[last_tile, corners, :]
            for a in range(5):
                for z in range(CELLS_Z):
                    ref[TILES + z, group(a, 0), :] = jnp.where(
                        low_half, pltpu.roll(ref[z, group(a, 0), :], HALF, 1), ref[TILES - CELLS_Z + z, group(a, 1), :]
                    )
                ref[TILES + CELLS_Z - 1, group(a, 2), :] = jnp.where(
                    low_half, pltpu.roll(ref[CELLS_Z - 1, group(a, 2), :], HALF, 1), turn(end, -a)
                )

        first = c * CELLS_Z
        ends = [ref[first + z, corners, :] for z in range(CELLS_Z)]
        for a in range(5):
            y_new = [
                jnp.where(along_y, ref[first + CELLS_Z + z, group(a, 0), :], ref[first + z, group(a, 1), :])
                for z in range(CELLS_Z)
            ]
            for z in range(CELLS_Z):
                ref[first + z, group(a, 1), :] = y_new[z]
                if z < CELLS_Z - 1:
                    ref[first + z, group(a, 2), :] = jnp.where(
                        along_z, ref[first + z + 1, group(a, 0), :], ref[first + z, group(a, 2), :]
                    )
                    ahead = y_new[z + 1]
                else:
                    ahead = ref[first + CELLS_Z + z, group(a, 2), :]
                ends[z] = jnp.where(sub == a, turn(ahead, a), ends[z])
        for z in range(CELLS_Z):
            ref[first + z, corners, :] = ends[z]

    def assembled(c, a):
        tiles, corner_terms = [], []
        for z in range(CELLS_Z):
            t = c * CELLS_Z + z
            own, y, d = [product[t + CELLS_Z, group(a, g), :] for g in range(3)]
            own = own + jnp.where(along_y, product[t, group(a, 1), :], 0.0)
            d = d + jnp.where(corner, turn(product[t, corners, :], -a), 0.0)
            tiles.append([own, y, d])
            corner_terms.append(turn(product[t + CELLS_Z, corners, :], -a))
        for z in range(1, CELLS_Z):
            tiles[z][0] = tiles[z][0] + jnp.where(along_z, tiles[z - 1][2], 0.0)
            tiles[z][1] = tiles[z][1] + jnp.where(corner, corner_terms[z - 1], 0.0)
        return tiles

    def multiply(current, c):
        mass = mass_ref[...]
        for pair in range(CELLS_Z // 2):
            t = c * CELLS_Z + 2 * pair
            values = [current[t], current[t + 1]]
            high, low = split(jnp.concatenate(values, axis=1))
            result = jnp.dot(
                stiff_ref[...], jnp.concatenate([high, low], axis=0), preferred_element_type=jnp.float32
            )
            result = result[:ROWS] + result[ROWS:]
            for k in range(2):
                product[t + CELLS_Z + k] = result[:, k * LANES : (k + 1) * LANES] * scale_ref[
                    pl.ds(t + k, 1), :
                ] + mass * potential_ref[pl.ds(t + k, 1), :] * values[k]

        @pl.when(c == CHUNKS - 1)
        def _():
            for z in range(CELLS_Z):
                for rows in [group(a, 1) for a in range(5)] + [corners]:
                    turned = pltpu.roll(product[TILES + z, rows, :], HALF, 1)
                    product[z, rows, :] = jnp.where(low_half, 0.0, turned)

    def buffers(step):
        return (out_ref, other) if step % 2 == 0 else (other, out_ref)

    def factor(step):
        return (1.0 if step == 0 else 2.0) / HALF_WIDTH

    def advance(step, t, rows, total):
        current, previous = buffers(step)
        value = (total - CENTER * current[t, rows, :]) * factor(step)
        previous[t, rows, :] = value if step == 0 else value - previous[t, rows, :]

    def assemble(step, c):
        ends = product[TILES + CELLS_Z - 1, corners, :]
        for way, a in ((0, top), (1, bottom)):
            tiles = assembled(c, a)
            for z in range(CELLS_Z):
                for g in range(3):
                    face[way, c * CELLS_Z + z, 8 * g : 8 * g + 8, :] = tiles[z][g]
            send_chunk(step + 1, way, c, tiles, ends)
        for a in inner:
            tiles = assembled(c, a)
            for z in range(CELLS_Z):
                for g in range(3):
                    advance(step, c * CELLS_Z + z, group(a, g), tiles[z][g])

    def advance_faces(step, c):
        for way, a, valid in ((0, bottom, has_below), (1, top, has_above)):
            finish_copy(message(step + 1, way, c), way)
            for z in range(CELLS_Z):
                t = c * CELLS_Z + z
                arrived = unpack(step + 1, way, c, z)
                for g in range(3):
                    total = face[1 - way, t, 8 * g : 8 * g + 8, :] + jnp.where(valid, arrived[g], 0.0)
                    advance(step, t, group(a, g), total)

        @pl.when(c == CHUNKS - 1)
        def _():
            previous = buffers(step)[1]
            ends = product[TILES + CELLS_Z - 1, corners, :]
            for way, a, valid in ((0, bottom, has_below), (1, top, has_above)):
                finish_copy(edge_message(step + 1, way), way)
                for z in range(CELLS_Z):
                    rows = group(a, 1)
                    edge = jnp.where(along_y & valid, edge_receives[step + 1, way, z], 0.0)
                    previous[TILES - CELLS_Z + z, rows, :] = previous[TILES - CELLS_Z + z, rows, :] + factor(step) * edge
                ends = ends + jnp.where((sub == a) & valid, unpack_corner(step + 1, way), 0.0)
            advance(step, last_tile, corners, ends)

    def tabulate(step):
        high = lax.broadcasted_iota(jnp.int32, (GROUPS, LANES), 0)
        low = lax.broadcasted_iota(jnp.int32, (LANES, LANES), 0)
        tile = (lax.broadcasted_iota(jnp.int32, (1, LANES), 1) // 2).astype(jnp.float32)

        def body(i, total):
            left, right = [], []
            for k in range(2):
                at = pl.ds(2 * i + k, 1)
                key = keys_ref[at, :]
                left.append(jnp.where(high == key >> 7, 1.0, 0.0).astype(jnp.bfloat16))
                hit = low == key & (LANES - 1)
                values = [jnp.where(hit, tile, 0.0), jnp.where(hit, codes_ref[at, :], 0.0)]
                right.append(jnp.concatenate(values, axis=0).astype(jnp.bfloat16))
            return total + lax.dot_general(
                jnp.concatenate(left, axis=1),
                jnp.concatenate(right, axis=1),
                (((1,), (1,)), ((), ())),
                preferred_element_type=jnp.float32,
            )

        part = LANES // 2 // FILTER_DEG
        total = jnp.zeros((GROUPS, 2 * LANES), jnp.float32) if step == 0 else places[...]
        total = lax.fori_loop(part * step, part * (step + 1), body, total)
        if step < FILTER_DEG - 1:
            places[...] = total
            return
        total = total + 0.5
        tiles = total[:, :LANES].astype(jnp.int32)
        codes = total[:, LANES:].astype(jnp.int32)
        node = high * LANES + lax.broadcasted_iota(jnp.int32, (GROUPS, LANES), 1)
        place = (codes & 1) * (TILES * ROWS) + tiles * ROWS + (codes >> 1)
        table_ref[...] = jnp.where(node < NODES, place, CORNERS + 5)

    index_copy = pltpu.make_async_copy(index_vector_ref, index_ref, index_sem)
    index_copy.start()
    node_count = waves_ref.shape[1]
    whole_blocks = node_count // LANES

    def transpose(i, carry):
        at = pl.ds(pl.multiple_of(i * LANES, LANES), LANES)
        block = waves_ref[:, at]
        doubled[at, :] = jnp.concatenate([block, block], axis=0).T
        return carry

    lax.fori_loop(0, whole_blocks, transpose, 0)
    rest = node_count - whole_blocks * LANES
    block = jnp.concatenate(
        [waves_ref[:, whole_blocks * LANES :], jnp.zeros((HALF, LANES - rest), jnp.float32)], axis=1
    )
    doubled[whole_blocks * LANES : (whole_blocks + 1) * LANES, :] = jnp.concatenate([block, block], axis=0).T

    out_ref[...] = jnp.zeros_like(out_ref)
    low_row = lax.broadcasted_iota(jnp.int32, (1, LANES), 1) < HALF

    def gather(t, nodes, halves):
        for node, row in nodes:
            first = doubled[pl.ds(index_ref[node, 2 * t], 1), :]
            second = doubled[pl.ds(index_ref[node, 2 * t + 1], 1), :]
            out_ref[t, row : row + 1, :] = jnp.where(low_row, first, second)

    index_copy.wait()
    each_node_once((top,), gather)

    def send_owner(c):
        tiles = [[out_ref[c * CELLS_Z + z, group(top, g), :] for g in range(3)] for z in range(CELLS_Z)]
        send_chunk(0, 0, c, tiles, out_ref[last_tile, corners, :])

    over_chunks(send_owner)
    each_node_once((0, 1, 2, 3), gather)
    other[...] = jnp.zeros_like(other)

    def take_owner(c):
        finish_copy(message(0, 0, c), 0)
        for z in range(CELLS_Z):
            t = c * CELLS_Z + z
            arrived = unpack(0, 0, c, z)
            for g in range(3):
                out_ref[t, group(bottom, g), :] = jnp.where(has_below, arrived[g], out_ref[t, group(bottom, g), :])

    over_chunks(take_owner)
    finish_copy(edge_message(0, 0), 0)
    for z in range(CELLS_Z):
        t = TILES - CELLS_Z + z
        out_ref[t, group(bottom, 1), :] = jnp.where(
            along_y & has_below, edge_receives[0, 0, z], out_ref[t, group(bottom, 1), :]
        )
    out_ref[last_tile, corners, :] = jnp.where(
        (sub == bottom) & has_below, unpack_corner(0, 0), out_ref[last_tile, corners, :]
    )
    over_chunks(lambda c: fill(out_ref, c))

    multiply(out_ref, CHUNKS - 1)

    def first_step(c):
        multiply(out_ref, c)
        assemble(0, c)

    lax.fori_loop(0, CHUNKS - 1, lambda c, carry: (first_step(c), carry)[1], 0)
    assemble(0, CHUNKS - 1)
    tabulate(0)

    for step in range(1, FILTER_DEG):
        base = step - 1
        current = buffers(step)[0]

        def refresh(c):
            fill(current, c)
            multiply(current, c)

        def next_chunk(i, carry):
            advance_faces(step - 1, lax.rem(base + i, CHUNKS))
            c = lax.rem(base + i - 1, CHUNKS)
            refresh(c)
            assemble(step, c)
            return carry

        advance_faces(step - 1, base)
        advance_faces(step - 1, base + 1)
        refresh(base)
        lax.fori_loop(2, CHUNKS, next_chunk, 0)
        refresh((base + CHUNKS - 1) % CHUNKS)
        assemble(step, (base + CHUNKS - 1) % CHUNKS)
        assemble(step, base)
        tabulate(step)

    last = FILTER_DEG - 1
    lax.fori_loop(
        0, CHUNKS, lambda i, carry: (advance_faces(last, lax.rem(last + i, CHUNKS)), carry)[1], 0
    )


def filter_cells(index, keys, wavefunctions, stiff, scale, potential):
    whole = pl.BlockSpec(memory_space=pltpu.VMEM)
    cells = (TILES + CELLS_Z, ROWS, LANES)
    rounds = FILTER_DEG + 1
    blocks = wavefunctions.shape[1] // LANES + 1
    return pl.pallas_call(
        filter_kernel,
        out_shape=(
            jax.ShapeDtypeStruct(cells, jnp.float32), jax.ShapeDtypeStruct((GROUPS, LANES), jnp.int32)
        ),
        in_specs=[whole] * 8,
        out_specs=(whole, whole),
        scratch_shapes=[
            pltpu.SMEM(index.shape, jnp.int32),
            pltpu.VMEM((GROUPS, 2 * LANES), jnp.float32),
            pltpu.VMEM(cells, jnp.float32),
            pltpu.VMEM(cells, jnp.float32),
            pltpu.VMEM((2, TILES, PLANE, LANES), jnp.float32),
            pltpu.VMEM((blocks * LANES, LANES), jnp.float32),
            pltpu.VMEM((2, CHUNKS, MESSAGE, 8, LANES), jnp.float32),
            pltpu.VMEM((2, EDGE, 8, LANES), jnp.float32),
            pltpu.VMEM((rounds, 2, CHUNKS, MESSAGE, 8, LANES), jnp.float32),
            pltpu.VMEM((rounds, 2, EDGE, 8, LANES), jnp.float32),
            pltpu.SemaphoreType.DMA((rounds, 2, CHUNKS)),
            pltpu.SemaphoreType.DMA((rounds, 2, CHUNKS)),
            pltpu.SemaphoreType.DMA((rounds, 2)),
            pltpu.SemaphoreType.DMA((rounds, 2)),
            pltpu.SemaphoreType.DMA(()),
        ],
        compiler_params=pltpu.CompilerParams(
            collective_id=0, has_side_effects=True, vmem_limit_bytes=56 * 2**20
        ),
        name="filter_cells",
    )(index, keys, place_codes(), wavefunctions, stiff, row_mass(), scale, potential)


def split(x):
    high = x.astype(jnp.bfloat16)
    return high, (x - high.astype(jnp.float32)).astype(jnp.bfloat16)


def exact_dot_t(x, y):
    return lax.dot_general(
        x, y, (((1,), (1,)), ((), ())), precision=HIGHEST, preferred_element_type=jnp.float32
    )


def inverse_of_block(block):
    size = BANDS_DEV
    row_at = lax.broadcasted_iota(jnp.int32, (size, LANES), 0)
    lane = lax.broadcasted_iota(jnp.int32, (size, LANES), 1)
    wide = jnp.concatenate([block, jnp.zeros((size, LANES - size), jnp.float32)], axis=1)
    wide = jnp.where(lane == row_at + size, 1.0, wide)
    tiles = [wide[8 * g : 8 * g + 8] for g in range(size // 8)]
    sub = lax.broadcasted_iota(jnp.int32, (8, LANES), 0)
    for home in range(size // 8):
        live = range(home, size // 8)
        columns = {
            (g, n): jnp.broadcast_to(tiles[g][:, 8 * home + n : 8 * home + n + 1], (8, LANES))
            for g in live for n in range(8)
        }
        for at in range(8):
            scale = 1.0 / columns[home, at][at : at + 1, :]
            ratio = tiles[home][at : at + 1, :] * scale
            ahead = {n: columns[home, n][at : at + 1, :] * scale for n in range(at + 1, 8)}
            for g in live:
                factor = columns[g, at]
                if g == home:
                    factor = jnp.where(sub > at, factor, 0.0)
                for n in range(at + 1, 8):
                    columns[g, n] = columns[g, n] - factor * ahead[n]
                tiles[g] = tiles[g] - factor * ratio
    wide = jnp.concatenate(tiles, axis=0)
    pivots = jnp.sum(jnp.where(lane == row_at, wide, 0.0), axis=1, keepdims=True)
    return wide[:, size:] * (1.0 / jnp.sqrt(pivots))


def finish_kernel(
    owned, far_cells, table_vector, out, table, cells, wide_rows, own, weight, partner, cross, partner_cross,
    sums, by_plane, piece, by_z, everyone, inverse,
    table_sem, cell_sems, pair_sems, first_sems, second_sems, forward_sems, again_sems, plane_sems, z_sems, band_sems, back_sems,
):
    table_copy = pltpu.make_async_copy(table_vector, table, table_sem)
    table_copy.start()
    part = TILES // CELL_PARTS
    cell_copies = [
        pltpu.make_async_copy(far_cells.at[pl.ds(p * part, part)], cells.at[pl.ds(p * part, part)], cell_sems.at[p])
        for p in range(CELL_PARTS)
    ]
    for step in cell_copies:
        step.start()
    space, band = lax.axis_index("space"), lax.axis_index("band")
    at_plane = lax.rem(space, PLANE_PEERS)
    core = lax.rem(band, 2)
    chip = band // 2
    mate = band + 1 - 2 * core
    across = lax.rem(band + 2, N_BAND)
    across_mate = lax.rem(mate + 2, N_BAND)

    def plane_peer(k):
        return {"space": space - at_plane + lax.rem(at_plane + k, PLANE_PEERS)}

    z_peer = {"space": lax.rem(space + PLANE_PEERS, 2 * PLANE_PEERS)}
    band_peers = [{"band": lax.rem(band + k, N_BAND)} for k in (1, 2, 3)]
    barrier = pltpu.get_barrier_semaphore()
    peers = [plane_peer(k) for k in range(1, PLANE_PEERS)] + [z_peer] + band_peers
    for peer in peers:
        pl.semaphore_signal(barrier, inc=1, device_id=peer, device_id_type=MESH)

    def send(source, target, sems, slot, peer):
        return pltpu.make_async_remote_copy(
            src_ref=source,
            dst_ref=target,
            send_sem=sems.at[0, slot],
            recv_sem=sems.at[1, slot],
            device_id=peer,
            device_id_type=MESH,
        )

    left_half = lax.broadcasted_iota(jnp.int32, (ROWS, LANES), 1) < HALF

    def widen(t, carry):
        values = cells[t]
        turned = pltpu.roll(values, HALF, 1)
        for slot, (left, right) in enumerate(((values, turned), (turned, values))):
            rows = pl.ds(pl.multiple_of((slot * TILES + t) * ROWS, ROWS), ROWS)
            wide_rows[rows, :] = jnp.where(left_half, left, right)
        return carry

    for p in range(CELL_PARTS):
        cell_copies[p].wait()
        lax.fori_loop(p * part, (p + 1) * part, widen, 0)
    table_copy.wait()
    low_lane = lax.broadcasted_iota(jnp.int32, (1, LANES), 1) < HALF

    def gather(i):
        start = pl.multiple_of(i * LANES, LANES)
        for k in range(LANES):
            first = wide_rows[pl.ds(table[i, k], 1), :]
            second = wide_rows[pl.ds(table[i + GROUPS // 2, k], 1), :]
            own[pl.ds(start + k, 1), :] = jnp.where(low_lane, first, second)

    def weigh(i, carry):
        def weights(at):
            row = table_vector[pl.ds(at, 1), :] & (ROWS - 1)
            shared = ((row < PLANE) | (row == CORNERS)) & (space > 0)
            return jnp.broadcast_to(jnp.where(shared | (row >= CORNERS + 5), 0.0, 1.0), (HALF, LANES))

        both = jnp.concatenate([weights(i), weights(i + GROUPS // 2)], axis=0)
        weight[pl.ds(pl.multiple_of(i * LANES, LANES), LANES), :] = both.T
        return carry

    half = PAIRS // 2
    size = half // PIECES

    def piece_rows(side, p):
        return pl.ds(pl.multiple_of(side * half + p * size, size), size)

    to_mate, to_across = {"band": mate}, {"band": across}
    pieces = range(PIECES)
    first = [
        send(own.at[piece_rows(chip, p)], cross.at[piece_rows(chip, p)], first_sems, p, to_across) for p in pieces
    ]
    second = [
        send(own.at[piece_rows(1 - chip, p)], cross.at[piece_rows(1 - chip, p)], second_sems, p, to_across)
        for p in pieces
    ]
    forward_first = [
        send(cross.at[piece_rows(1 - chip, p)], partner_cross.at[piece_rows(1 - chip, p)], forward_sems, p, to_mate)
        for p in pieces
    ]
    forward_second = [
        send(cross.at[piece_rows(chip, p)], partner_cross.at[piece_rows(chip, p)], again_sems, p, to_mate)
        for p in pieces
    ]
    halves = [pl.ds(pl.multiple_of(side * half, half), half) for side in (chip, 1 - chip)]
    pair = [send(own.at[rows], partner.at[rows], pair_sems, k, to_mate) for k, rows in enumerate(halves)]

    groups = GROUPS // 4
    per_piece = groups // PIECES
    pl.semaphore_wait(barrier, len(peers))
    for p in pieces:
        base = chip * groups + p * per_piece
        lax.fori_loop(0, per_piece, lambda i, carry, base=base: (gather(base + i), carry)[1], 0)
        first[p].start()
    for p in pieces:
        base = (1 - chip) * groups + p * per_piece
        lax.fori_loop(0, per_piece, lambda i, carry, base=base: (gather(base + i), carry)[1], 0)
        if p == 0:
            second[0].start()
            pair[0].start()
    pair[1].start()
    lax.fori_loop(0, GROUPS // 2, weigh, 0)

    def products(left, right):
        both = lax.dot_general(
            jnp.concatenate(split(left), axis=1),
            jnp.concatenate(split(right), axis=1),
            (((0,), (0,)), ((), ())),
            preferred_element_type=jnp.float32,
        )
        upper = both[:LANES, : 2 * LANES] + both[:LANES, 2 * LANES :]
        return upper + (both[LANES:, : 2 * LANES] + both[LANES:, 2 * LANES :])

    def block_rows(i):
        return pl.ds(pl.multiple_of(i * BLOCK, BLOCK), BLOCK)

    def own_terms(i, total):
        rows = block_rows(i)
        mine = own[rows, :]
        scale = weight[rows, :]
        return total + products(mine * scale, jnp.concatenate([mine, partner[rows, :]], axis=1))

    def cross_terms(i, total):
        rows = block_rows(i)
        scale = weight[rows, :]
        return total + products(
            cross[rows, :], jnp.concatenate([own[rows, :] * scale, partner[rows, :] * scale], axis=1)
        )

    low_half = lax.broadcasted_iota(jnp.int32, (BANDS_DEV, LANES), 1) < HALF

    def fold(total):
        size = BANDS_DEV
        left = total[:size, :LANES] + pltpu.roll(total[size:, :LANES], HALF, 1)
        right = pltpu.roll(total[:size, LANES:], HALF, 1) + total[size:, LANES:]
        return jnp.where(low_half, left, right)

    zero = jnp.zeros((LANES, 2 * LANES), jnp.float32)
    per_half = half // BLOCK
    total = zero
    for k, side in enumerate((chip, 1 - chip)):
        pair[k].wait()
        total = lax.fori_loop(
            0, per_half, lambda i, total, side=side: own_terms(side * per_half + i, total), total
        )
    sums[0:BANDS_DEV, :] = fold(total)
    blocks = size // BLOCK
    total = zero
    for p in pieces:
        first[p].wait()
        forward_first[p].start()
        base = (1 - chip) * (half // BLOCK) + p * blocks
        total = lax.fori_loop(0, blocks, lambda i, total, base=base: cross_terms(base + i, total), total)
    sums[BANDS_DEV : 2 * BANDS_DEV, :] = fold(total)


    def rows_of(at):
        return pl.ds(pl.multiple_of(8 * at, 8), 8)

    others = range(1, PLANE_PEERS)
    scatter = [
        send(sums.at[rows_of(lax.rem(at_plane + k, PLANE_PEERS))], by_plane.at[k - 1], plane_sems, k - 1, plane_peer(k))
        for k in others
    ]
    for step in scatter:
        step.start()
    for step in scatter:
        step.wait()
    mine = sums[rows_of(at_plane), :]
    for k in others:
        mine = mine + by_plane[k - 1]
    piece[...] = mine
    to_z = send(piece, by_z, z_sems, 0, z_peer)
    to_z.start()
    to_z.wait()
    everyone[at_plane, band] = piece[...] + by_z[...]
    to_band = [
        send(everyone.at[at_plane, band], everyone.at[at_plane, band], band_sems, k, peer)
        for k, peer in enumerate(band_peers)
    ]
    for step in to_band:
        step.start()
    for step in to_band:
        step.wait()
    for p in pieces[1:]:
        second[p].start()
    back = [send(everyone.at[at_plane], everyone.at[at_plane], back_sems, k - 1, plane_peer(k)) for k in others]
    for step in back:
        step.start()
    for step in back:
        step.wait()

    totals = [
        jnp.concatenate([everyone[q, b] for q in range(PLANE_PEERS)], axis=0) * (1.0 / owned) for b in range(N_BAND)
    ]

    def part(b, r, c):
        size = BANDS_DEV
        return totals[b][r * size : (r + 1) * size, c * size : (c + 1) * size]

    margin = {(b, b): part(b, 0, 0) for b in range(N_BAND)}
    margin[1, 0], margin[3, 2] = part(1, 0, 1), part(3, 0, 1)
    margin[2, 0] = part(0, 1, 0) + part(2, 1, 0).T
    margin[2, 1] = part(0, 1, 1) + part(3, 1, 1).T
    margin[3, 0] = part(1, 1, 1) + part(2, 1, 1).T
    margin[3, 1] = part(1, 1, 0) + part(3, 1, 0).T

    inverses, factor, whole = [], {}, {}
    for k in range(N_BAND):
        diagonal = inverse_of_block(margin[k, k])
        inverses.append(diagonal)
        for i in range(k + 1, N_BAND):
            factor[i, k] = exact_dot_t(margin[i, k], diagonal)
        for i in range(k + 1, N_BAND):
            for j in range(k + 1, i + 1):
                margin[i, j] = margin[i, j] - exact_dot_t(factor[i, k], factor[j, k])
        whole[k, k] = diagonal
        for j in range(k):
            total = exact_dot(factor[k, j], whole[j, j])
            for m in range(j + 1, k):
                total = total + exact_dot(factor[k, m], whole[m, j])
            whole[k, j] = -exact_dot(diagonal, total)
        if k == 2:
            second[0].wait()
            forward_second[0].start()
    padding = jnp.zeros((BANDS_DEV, LANES - BANDS_DEV), jnp.float32)
    for i in range(N_BAND):
        for j in range(N_BAND):
            if j <= i:
                inverse[i, j] = jnp.concatenate([whole[i, j], padding], axis=1)
            else:
                inverse[i, j] = jnp.zeros((BANDS_DEV, LANES), jnp.float32)
    panels = [inverse[band, source] for source in (band, mate, across, across_mate)]
    left = jnp.concatenate(
        [
            jnp.concatenate(panels, axis=1),
            jnp.concatenate([pltpu.roll(panel, HALF, 1) for panel in panels], axis=1),
        ],
        axis=0,
    )
    left_high, left_low = split(left)
    left = jnp.concatenate(
        [jnp.concatenate([left_high, left_high], axis=1), jnp.concatenate([left_low, left_low], axis=1)], axis=0
    )

    def rotate(i, carry):
        rows = block_rows(i)
        right = jnp.concatenate([ref[rows, :] for ref in (own, partner, cross, partner_cross)], axis=1)
        both = lax.dot_general(
            left,
            jnp.concatenate(split(right), axis=1),
            (((1,), (1,)), ((), ())),
            preferred_element_type=jnp.float32,
        )
        rotated = both[: 2 * BANDS_DEV] + both[2 * BANDS_DEV :]
        out[:, rows] = rotated[:BANDS_DEV]
        out[:, pl.ds(pl.multiple_of(PAIRS + i * BLOCK, BLOCK), BLOCK)] = rotated[BANDS_DEV:]
        return carry

    def rotate_piece(side, p):
        base = side * per_half + p * blocks
        lax.fori_loop(0, blocks, lambda i, carry: rotate(base + i, carry), 0)

    for p in pieces:
        forward_first[p].wait()
        rotate_piece(1 - chip, p)
        if p > 0:
            second[p].wait()
            forward_second[p].start()
    for p in pieces:
        forward_second[p].wait()
        rotate_piece(chip, p)


def finish(cells, table, owned_count):
    whole = pl.BlockSpec(memory_space=pltpu.VMEM)
    nodes = pltpu.VMEM((PAIRS, LANES), jnp.float32)

    def small(*shape):
        return pltpu.VMEM(shape, jnp.float32)

    def sems(slots):
        return pltpu.SemaphoreType.DMA((2, slots))

    return pl.pallas_call(
        functools.partial(finish_kernel, owned_count),
        out_shape=jax.ShapeDtypeStruct((BANDS_DEV, 2 * PAIRS), jnp.float32),
        in_specs=[pl.BlockSpec(memory_space=pltpu.MemorySpace.HBM), whole],
        out_specs=whole,
        scratch_shapes=[
            pltpu.SMEM(table.shape, jnp.int32),
            small(TILES, ROWS, LANES),
            small(2 * TILES * ROWS, LANES),
            nodes, nodes, nodes, nodes, nodes,
            small(LANES, LANES), small(PLANE_PEERS - 1, 8, LANES), small(8, LANES), small(8, LANES),
            small(PLANE_PEERS, N_BAND, 8, LANES),
            small(N_BAND, N_BAND, BANDS_DEV, LANES),
            pltpu.SemaphoreType.DMA(()),
            pltpu.SemaphoreType.DMA((CELL_PARTS,)),
            sems(2), sems(PIECES), sems(PIECES), sems(PIECES), sems(PIECES),
            sems(PLANE_PEERS - 1), sems(1), sems(3), sems(PLANE_PEERS - 1),
        ],
        compiler_params=pltpu.CompilerParams(
            collective_id=1, has_side_effects=True, vmem_limit_bytes=48 * 2**20
        ),
        name="finish",
    )(cells, table)


def shards(
    wavefunctions, stiffness, cell_scale, cell_potential, connectivity, lower_face, upper_face
):
    node_count = wavefunctions.shape[1]
    face_count = lower_face.shape[0]
    space_count = lax.axis_size("space")
    owned_count = node_count * space_count - face_count * (space_count - 1)

    index, keys, scale, potential, stiff = make_layout(connectivity, cell_scale, cell_potential, stiffness)
    cells, table = filter_cells(index, keys, wavefunctions, stiff, scale, potential)
    return finish(cells, table, owned_count)[:, :node_count]


def solution(mesh):
    placed = (
        P("band", "space"),
        P(),
        P("space"),
        P("space"),
        P(None, "space"),
        P("space"),
        P("space"),
    )
    return jax.shard_map(
        shards, mesh=mesh, in_specs=placed, out_specs=P("band", "space"), check_vma=False
    )
```

```python
import functools

import jax
import jax.numpy as jnp
import numpy as np
from jax import lax
from jax.experimental import pallas as pl
from jax.experimental.pallas import tpu as pltpu
from jax.sharding import PartitionSpec as P

FILTER_DEG = 4
GLL_WEIGHTS = (0.1, 49.0 / 90.0, 32.0 / 45.0, 49.0 / 90.0, 0.1)
CENTER = 11.0
HALF_WIDTH = 9.0
HIGHEST = lax.Precision.HIGHEST
MESH = pl.DeviceIdType.MESH

CELLS_Y = 20
CELLS_Z = 6
CHUNKS = CELLS_Y // 2
TILES = CHUNKS * CELLS_Z
SLOTS = 2 * TILES
HALF = 64
LANES = 128
ROWS = 128
PLANE = 24
CORNERS = 5 * PLANE
MESSAGE = 2 * CELLS_Z + 1
EDGE = CELLS_Z + 1

NODES = 10125
PAIRS = 5120
BLOCK = 256
PIECES = 5
CELL_PARTS = 4
GROUPS = 2 * PAIRS // LANES
PLANE_PEERS = 16
BANDS_DEV = 64
N_BAND = 4


def row_of_node(a, b, c):
    if (b, c) == (4, 4):
        return CORNERS + a
    rows = {(0, 0): 0, (4, 0): 8, (0, 4): 16, (1, 1): 7, (1, 2): 15, (1, 3): 23}
    for k in (1, 2, 3):
        rows[(0, k)] = k
        rows[(4, k)] = 8 + k
        rows[(k, 0)] = 3 + k
        rows[(k, 4)] = 16 + 3 + k
        rows[(2, k)] = 8 + 3 + k
        rows[(3, k)] = 16 + k
    return PLANE * a + rows[(b, c)]


def node_rows(planes, chosen):
    return [
        (25 * a + 5 * b + c, row_of_node(a, b, c))
        for a in planes for b in range(5) for c in range(5) if chosen(b, c)
    ]


LOCAL_ROWS = [row for _, row in node_rows(range(5), lambda b, c: True)]


def owners():
    owned = np.zeros((LANES, SLOTS), np.float32)
    for slot in range(SLOTS):
        tile, half = divmod(slot, 2)
        last_y = half == 1 and tile >= TILES - CELLS_Z
        last_z = tile % CELLS_Z == CELLS_Z - 1
        for node, _ in node_rows(range(5), lambda b, c: (b < 4 or last_y) and (c < 4 or last_z)):
            owned[node, slot] = 1.0
    return owned


def place_codes():
    codes = np.zeros((LANES, LANES), np.float32)
    codes[:125, :] = 2.0 * np.array(LOCAL_ROWS)[:, None] + np.arange(LANES)[None, :] % 2
    return codes


def row_selector():
    chosen = np.zeros((ROWS, 125), np.float32)
    chosen[LOCAL_ROWS, np.arange(125)] = 1.0
    return chosen


def row_mass():
    weights = np.array(GLL_WEIGHTS, np.float32)
    mass = (weights[:, None, None] * weights[None, :, None] * weights[None, None, :]).reshape(-1)
    spread = np.zeros((ROWS, LANES), np.float32)
    spread[LOCAL_ROWS, :] = mass[:, None]
    return spread


def local(a, b, c):
    return 25 * a + 5 * b + c


def exact_dot(x, y):
    return jnp.dot(x, y, precision=HIGHEST, preferred_element_type=jnp.float32)


def chain_counts(before, doublings):
    size = before.shape[0]
    eye = (
        lax.broadcasted_iota(jnp.int32, (size, size), 0) == lax.broadcasted_iota(jnp.int32, (size, size), 1)
    ).astype(jnp.float32)
    total, power = eye + before, before
    for _ in range(doublings):
        power = jnp.dot(power, power, preferred_element_type=jnp.float32)
        total = total + jnp.dot(total, power, preferred_element_type=jnp.float32)
    return jnp.sum(total, axis=0, keepdims=True) - 1.0


def layout_kernel(
    conn_ref, cell_scale_ref, cell_potential_ref, stiff_ref, select_ref, owned_ref,
    index_ref, keys_ref, scale_ref, potential_ref, stiffness_ref,
):
    conn = conn_ref[...].astype(jnp.float32)
    cells = conn.shape[1]
    on_rows = lax.broadcasted_iota(jnp.int32, (cells, cells), 0)
    on_lanes = lax.broadcasted_iota(jnp.int32, (cells, cells), 1)

    def as_column(row):
        return jnp.sum(jnp.where(on_rows == on_lanes, row, 0.0), axis=1, keepdims=True)

    def row_of(node):
        return conn[node : node + 1, :]

    after_z = (as_column(row_of(local(2, 2, 4))) == row_of(local(2, 2, 0))).astype(jnp.float32)
    after_y = (as_column(row_of(local(2, 4, 2))) == row_of(local(2, 0, 2))).astype(jnp.float32)
    at_z = chain_counts(after_z, 2)
    at_y = chain_counts(after_y, 4)
    upper_half = at_y >= CHUNKS
    tile = (at_y - jnp.where(upper_half, 1.0 * CHUNKS, 0.0)) * CELLS_Z + at_z
    slot = 2.0 * tile + jnp.where(upper_half, 1.0, 0.0)
    moved = (as_column(slot) == on_lanes.astype(jnp.float32)).astype(jnp.float32)
    index = (exact_dot(conn, moved) + 0.5).astype(jnp.int32)
    index_ref[...] = index
    index = jnp.concatenate([index, jnp.zeros((LANES - index.shape[0], cells), jnp.int32)], axis=0)
    keys = jnp.where(owned_ref[...] > 0.5, index, -1)
    keys_ref[...] = jnp.concatenate([keys, jnp.full((LANES, LANES - cells), -1, jnp.int32)], axis=1)

    wanted = lax.broadcasted_iota(jnp.int32, (TILES, cells), 0).astype(jnp.float32)
    lane = lax.broadcasted_iota(jnp.int32, (TILES, LANES), 1)

    def spread(row):
        low, high = [
            jnp.sum(jnp.where(slot == 2.0 * wanted + half, row, 0.0), axis=1, keepdims=True) for half in (0.0, 1.0)
        ]
        return jnp.where(lane < HALF, low, high)

    scale_ref[...] = spread(cell_scale_ref[...])
    potential_ref[...] = spread(cell_potential_ref[...])

    select = select_ref[...]
    part = exact_dot(select, stiff_ref[...])
    stiff = lax.dot_general(
        part, select, (((1,), (1,)), ((), ())), precision=HIGHEST, preferred_element_type=jnp.float32
    )
    high = stiff.astype(jnp.bfloat16)
    low = (stiff - high.astype(jnp.float32)).astype(jnp.bfloat16)
    stiffness_ref[...] = jnp.concatenate(
        [jnp.concatenate([high, high], axis=1), jnp.concatenate([low, low], axis=1)], axis=0
    )


def make_layout(connectivity, cell_scale, cell_potential, stiffness):
    cells = connectivity.shape[1]
    whole = pl.BlockSpec(memory_space=pltpu.VMEM)
    return pl.pallas_call(
        layout_kernel,
        out_shape=(
            jax.ShapeDtypeStruct((125, cells), jnp.int32),
            jax.ShapeDtypeStruct((LANES, LANES), jnp.int32),
            jax.ShapeDtypeStruct((TILES, LANES), jnp.float32),
            jax.ShapeDtypeStruct((TILES, LANES), jnp.float32),
            jax.ShapeDtypeStruct((2 * ROWS, 2 * ROWS), jnp.bfloat16),
        ),
        in_specs=[whole] * 6,
        out_specs=(whole,) * 5,
        name="layout",
    )(connectivity, cell_scale[None, :], cell_potential[None, :], stiffness, row_selector(), owners())


def each_node_once(planes, visit):
    def loop(count, tile_of, nodes, halves=(0, 1)):
        def body(i, carry):
            visit(tile_of(i), nodes, halves)
            return carry

        lax.fori_loop(0, count, body, 0)

    loop(TILES, lambda i: i, node_rows(planes, lambda b, c: b < 4 and c < 4))
    loop(CELLS_Z, lambda i: TILES - CELLS_Z + i, node_rows(planes, lambda b, c: b == 4 and c < 4), (1,))
    loop(1, lambda i: TILES - 1, node_rows(planes, lambda b, c: b == 4 and c == 4), (1,))
    loop(CHUNKS, lambda i: i * CELLS_Z + CELLS_Z - 1, node_rows(planes, lambda b, c: b < 4 and c == 4))


def filter_kernel(
    index_vector_ref, keys_ref, codes_ref, waves_ref, stiff_ref, mass_ref, scale_ref, potential_ref, out_ref, table_ref,
    index_ref, places, other, product, face, doubled, sends, edge_sends, receives, edge_receives,
    send_sems, receive_sems, edge_send_sems, edge_receive_sems, index_sem,
):
    count = lax.axis_size("space")
    me = lax.axis_index("space")
    above, below = lax.rem(me + 1, count), lax.rem(me + count - 1, count)
    has_below, has_above = me > 0, me < count - 1

    barrier = pltpu.get_barrier_semaphore()
    for neighbour in (below, above):
        pl.semaphore_signal(barrier, inc=1, device_id={"space": neighbour}, device_id_type=MESH)
    pl.semaphore_wait(barrier, 2)

    sub = lax.broadcasted_iota(jnp.int32, (8, LANES), 0)
    lane = lax.broadcasted_iota(jnp.int32, (8, LANES), 1)
    corner = sub == 0
    along_y = sub <= 3
    along_z = corner | ((sub >= 4) & (sub <= 6))
    in_y_group = (sub >= 4) & (sub <= 6)
    in_z_group = ((sub >= 1) & (sub <= 3)) | (sub == 7)
    low_half = lane < HALF
    corners = slice(CORNERS, CORNERS + 8)
    last_tile = TILES - 1
    bottom, top = 0, 4
    inner = (1, 2, 3)

    def group(a, g):
        return slice(PLANE * a + 8 * g, PLANE * a + 8 * g + 8)

    def turn(value, by):
        return pltpu.roll(value, by % 8, 0) if by % 8 else value

    def over_chunks(body):
        def step(c, carry):
            body(c)
            return carry

        lax.fori_loop(0, CHUNKS, step, 0)

    def message(step, way, c):
        return pltpu.make_async_remote_copy(
            src_ref=sends.at[way, c],
            dst_ref=receives.at[step, way, c],
            send_sem=send_sems.at[step, way, c],
            recv_sem=receive_sems.at[step, way, c],
            device_id={"space": above if way == 0 else below},
            device_id_type=MESH,
        )

    def edge_message(step, way):
        return pltpu.make_async_remote_copy(
            src_ref=edge_sends.at[way],
            dst_ref=edge_receives.at[step, way],
            send_sem=edge_send_sems.at[step, way],
            recv_sem=edge_receive_sems.at[step, way],
            device_id={"space": above if way == 0 else below},
            device_id_type=MESH,
        )

    def start(copy, way):
        @pl.when(has_above if way == 0 else has_below)
        def _():
            copy.start()

    def finish_copy(copy, way):
        @pl.when(has_above if way == 0 else has_below)
        def _():
            copy.wait_send()

        @pl.when(has_below if way == 0 else has_above)
        def _():
            copy.wait_recv()

    def send_chunk(step, way, c, tiles, ends):
        for z, (own, y, d) in enumerate(tiles):
            sends[way, c, 2 * z] = own
            sends[way, c, 2 * z + 1] = jnp.where(corner, turn(y, 1), jnp.where(in_y_group, y, d))
        sends[way, c, MESSAGE - 1] = tiles[CELLS_Z - 1][2]
        start(message(step, way, c), way)

        @pl.when(c == CHUNKS - 1)
        def _():
            for z in range(CELLS_Z):
                edge_sends[way, z] = tiles[z][1]
            edge_sends[way, EDGE - 1] = ends
            start(edge_message(step, way), way)

    def unpack(step, way, c, z):
        inside = receives[step, way, c, 2 * z + 1]
        y = jnp.where(in_y_group, inside, jnp.where(sub == 7, turn(inside, 7), 0.0))
        d = jnp.where(in_z_group, inside, receives[step, way, c, MESSAGE - 1])
        return [receives[step, way, c, 2 * z], y, d]

    def unpack_corner(step, way):
        return turn(edge_receives[step, way, EDGE - 1], 4)

    def fill(ref, c):
        @pl.when(c == CHUNKS - 1)
        def _():
            end = ref[last_tile, corners, :]
            for a in range(5):
                for z in range(CELLS_Z):
                    ref[TILES + z, group(a, 0), :] = jnp.where(
                        low_half, pltpu.roll(ref[z, group(a, 0), :], HALF, 1), ref[TILES - CELLS_Z + z, group(a, 1), :]
                    )
                ref[TILES + CELLS_Z - 1, group(a, 2), :] = jnp.where(
                    low_half, pltpu.roll(ref[CELLS_Z - 1, group(a, 2), :], HALF, 1), turn(end, -a)
                )

        first = c * CELLS_Z
        ends = [ref[first + z, corners, :] for z in range(CELLS_Z)]
        for a in range(5):
            y_new = [
                jnp.where(along_y, ref[first + CELLS_Z + z, group(a, 0), :], ref[first + z, group(a, 1), :])
                for z in range(CELLS_Z)
            ]
            for z in range(CELLS_Z):
                ref[first + z, group(a, 1), :] = y_new[z]
                if z < CELLS_Z - 1:
                    ref[first + z, group(a, 2), :] = jnp.where(
                        along_z, ref[first + z + 1, group(a, 0), :], ref[first + z, group(a, 2), :]
                    )
                    ahead = y_new[z + 1]
                else:
                    ahead = ref[first + CELLS_Z + z, group(a, 2), :]
                ends[z] = jnp.where(sub == a, turn(ahead, a), ends[z])
        for z in range(CELLS_Z):
            ref[first + z, corners, :] = ends[z]

    def assembled(c, a):
        tiles, corner_terms = [], []
        for z in range(CELLS_Z):
            t = c * CELLS_Z + z
            own, y, d = [product[t + CELLS_Z, group(a, g), :] for g in range(3)]
            own = own + jnp.where(along_y, product[t, group(a, 1), :], 0.0)
            d = d + jnp.where(corner, turn(product[t, corners, :], -a), 0.0)
            tiles.append([own, y, d])
            corner_terms.append(turn(product[t + CELLS_Z, corners, :], -a))
        for z in range(1, CELLS_Z):
            tiles[z][0] = tiles[z][0] + jnp.where(along_z, tiles[z - 1][2], 0.0)
            tiles[z][1] = tiles[z][1] + jnp.where(corner, corner_terms[z - 1], 0.0)
        return tiles

    def multiply(current, c):
        mass = mass_ref[...]
        for pair in range(CELLS_Z // 2):
            t = c * CELLS_Z + 2 * pair
            values = [current[t], current[t + 1]]
            high, low = split(jnp.concatenate(values, axis=1))
            result = jnp.dot(
                stiff_ref[...], jnp.concatenate([high, low], axis=0), preferred_element_type=jnp.float32
            )
            result = result[:ROWS] + result[ROWS:]
            for k in range(2):
                product[t + CELLS_Z + k] = result[:, k * LANES : (k + 1) * LANES] * scale_ref[
                    pl.ds(t + k, 1), :
                ] + mass * potential_ref[pl.ds(t + k, 1), :] * values[k]

        @pl.when(c == CHUNKS - 1)
        def _():
            for z in range(CELLS_Z):
                for rows in [group(a, 1) for a in range(5)] + [corners]:
                    turned = pltpu.roll(product[TILES + z, rows, :], HALF, 1)
                    product[z, rows, :] = jnp.where(low_half, 0.0, turned)

    def buffers(step):
        return (out_ref, other) if step % 2 == 0 else (other, out_ref)

    def factor(step):
        return (1.0 if step == 0 else 2.0) / HALF_WIDTH

    def advance(step, t, rows, total):
        current, previous = buffers(step)
        value = (total - CENTER * current[t, rows, :]) * factor(step)
        previous[t, rows, :] = value if step == 0 else value - previous[t, rows, :]

    def assemble(step, c):
        ends = product[TILES + CELLS_Z - 1, corners, :]
        for way, a in ((0, top), (1, bottom)):
            tiles = assembled(c, a)
            for z in range(CELLS_Z):
                for g in range(3):
                    face[way, c * CELLS_Z + z, 8 * g : 8 * g + 8, :] = tiles[z][g]
            send_chunk(step + 1, way, c, tiles, ends)
        for a in inner:
            tiles = assembled(c, a)
            for z in range(CELLS_Z):
                for g in range(3):
                    advance(step, c * CELLS_Z + z, group(a, g), tiles[z][g])

    def advance_faces(step, c):
        for way, a, valid in ((0, bottom, has_below), (1, top, has_above)):
            finish_copy(message(step + 1, way, c), way)
            for z in range(CELLS_Z):
                t = c * CELLS_Z + z
                arrived = unpack(step + 1, way, c, z)
                for g in range(3):
                    total = face[1 - way, t, 8 * g : 8 * g + 8, :] + jnp.where(valid, arrived[g], 0.0)
                    advance(step, t, group(a, g), total)

        @pl.when(c == CHUNKS - 1)
        def _():
            previous = buffers(step)[1]
            ends = product[TILES + CELLS_Z - 1, corners, :]
            for way, a, valid in ((0, bottom, has_below), (1, top, has_above)):
                finish_copy(edge_message(step + 1, way), way)
                for z in range(CELLS_Z):
                    rows = group(a, 1)
                    edge = jnp.where(along_y & valid, edge_receives[step + 1, way, z], 0.0)
                    previous[TILES - CELLS_Z + z, rows, :] = previous[TILES - CELLS_Z + z, rows, :] + factor(step) * edge
                ends = ends + jnp.where((sub == a) & valid, unpack_corner(step + 1, way), 0.0)
            advance(step, last_tile, corners, ends)

    def tabulate(step):
        high = lax.broadcasted_iota(jnp.int32, (GROUPS, LANES), 0)
        low = lax.broadcasted_iota(jnp.int32, (LANES, LANES), 0)
        tile = (lax.broadcasted_iota(jnp.int32, (1, LANES), 1) // 2).astype(jnp.float32)

        def body(i, total):
            left, right = [], []
            for k in range(2):
                at = pl.ds(2 * i + k, 1)
                key = keys_ref[at, :]
                left.append(jnp.where(high == key >> 7, 1.0, 0.0).astype(jnp.bfloat16))
                hit = low == key & (LANES - 1)
                values = [jnp.where(hit, tile, 0.0), jnp.where(hit, codes_ref[at, :], 0.0)]
                right.append(jnp.concatenate(values, axis=0).astype(jnp.bfloat16))
            return total + lax.dot_general(
                jnp.concatenate(left, axis=1),
                jnp.concatenate(right, axis=1),
                (((1,), (1,)), ((), ())),
                preferred_element_type=jnp.float32,
            )

        part = LANES // 2 // FILTER_DEG
        total = jnp.zeros((GROUPS, 2 * LANES), jnp.float32) if step == 0 else places[...]
        total = lax.fori_loop(part * step, part * (step + 1), body, total)
        if step < FILTER_DEG - 1:
            places[...] = total
            return
        total = total + 0.5
        tiles = total[:, :LANES].astype(jnp.int32)
        codes = total[:, LANES:].astype(jnp.int32)
        node = high * LANES + lax.broadcasted_iota(jnp.int32, (GROUPS, LANES), 1)
        place = (codes & 1) * (TILES * ROWS) + tiles * ROWS + (codes >> 1)
        table_ref[...] = jnp.where(node < NODES, place, CORNERS + 5)

    index_copy = pltpu.make_async_copy(index_vector_ref, index_ref, index_sem)
    index_copy.start()
    node_count = waves_ref.shape[1]
    whole_blocks = node_count // LANES

    def transpose(i, carry):
        at = pl.ds(pl.multiple_of(i * LANES, LANES), LANES)
        block = waves_ref[:, at]
        doubled[at, :] = jnp.concatenate([block, block], axis=0).T
        return carry

    lax.fori_loop(0, whole_blocks, transpose, 0)
    rest = node_count - whole_blocks * LANES
    block = jnp.concatenate(
        [waves_ref[:, whole_blocks * LANES :], jnp.zeros((HALF, LANES - rest), jnp.float32)], axis=1
    )
    doubled[whole_blocks * LANES : (whole_blocks + 1) * LANES, :] = jnp.concatenate([block, block], axis=0).T

    unused = jnp.zeros((TILES + CELLS_Z, ROWS - CORNERS, LANES), jnp.float32)
    out_ref[:, CORNERS:, :] = unused
    other[:, CORNERS:, :] = unused
    low_row = lax.broadcasted_iota(jnp.int32, (1, LANES), 1) < HALF

    def gather(t, nodes, halves):
        for node, row in nodes:
            first = doubled[pl.ds(index_ref[node, 2 * t], 1), :]
            second = doubled[pl.ds(index_ref[node, 2 * t + 1], 1), :]
            out_ref[t, row : row + 1, :] = jnp.where(low_row, first, second)

    index_copy.wait()
    each_node_once((top,), gather)

    def send_owner(c):
        tiles = [[out_ref[c * CELLS_Z + z, group(top, g), :] for g in range(3)] for z in range(CELLS_Z)]
        send_chunk(0, 0, c, tiles, out_ref[last_tile, corners, :])

    over_chunks(send_owner)
    each_node_once((0, 1, 2, 3), gather)

    def take_owner(c):
        finish_copy(message(0, 0, c), 0)
        for z in range(CELLS_Z):
            t = c * CELLS_Z + z
            arrived = unpack(0, 0, c, z)
            for g in range(3):
                out_ref[t, group(bottom, g), :] = jnp.where(has_below, arrived[g], out_ref[t, group(bottom, g), :])

        @pl.when(c == CHUNKS - 1)
        def _():
            finish_copy(edge_message(0, 0), 0)
            for z in range(CELLS_Z):
                t = TILES - CELLS_Z + z
                out_ref[t, group(bottom, 1), :] = jnp.where(
                    along_y & has_below, edge_receives[0, 0, z], out_ref[t, group(bottom, 1), :]
                )
            out_ref[last_tile, corners, :] = jnp.where(
                (sub == bottom) & has_below, unpack_corner(0, 0), out_ref[last_tile, corners, :]
            )

    for step in range(FILTER_DEG):
        current = buffers(step)[0]

        def arrive(c):
            if step == 0:
                take_owner(c)
            else:
                advance_faces(step - 1, c)

        def refresh(c):
            fill(current, c)
            multiply(current, c)

        def next_chunk(i, carry):
            arrive(lax.rem(step + i, CHUNKS))
            c = lax.rem(step + i - 1, CHUNKS)
            refresh(c)
            assemble(step, c)
            return carry

        arrive(step)
        arrive(step + 1)
        refresh(step)
        lax.fori_loop(2, CHUNKS, next_chunk, 0)
        refresh((step + CHUNKS - 1) % CHUNKS)
        assemble(step, (step + CHUNKS - 1) % CHUNKS)
        assemble(step, step)
        tabulate(step)

    last = FILTER_DEG
    lax.fori_loop(
        0, CHUNKS, lambda i, carry: (advance_faces(last - 1, lax.rem(last + i, CHUNKS)), carry)[1], 0
    )


def filter_cells(index, keys, wavefunctions, stiff, scale, potential):
    whole = pl.BlockSpec(memory_space=pltpu.VMEM)
    cells = (TILES + CELLS_Z, ROWS, LANES)
    rounds = FILTER_DEG + 1
    blocks = wavefunctions.shape[1] // LANES + 1
    return pl.pallas_call(
        filter_kernel,
        out_shape=(
            jax.ShapeDtypeStruct(cells, jnp.float32), jax.ShapeDtypeStruct((GROUPS, LANES), jnp.int32)
        ),
        in_specs=[whole] * 8,
        out_specs=(whole, whole),
        scratch_shapes=[
            pltpu.SMEM(index.shape, jnp.int32),
            pltpu.VMEM((GROUPS, 2 * LANES), jnp.float32),
            pltpu.VMEM(cells, jnp.float32),
            pltpu.VMEM(cells, jnp.float32),
            pltpu.VMEM((2, TILES, PLANE, LANES), jnp.float32),
            pltpu.VMEM((blocks * LANES, LANES), jnp.float32),
            pltpu.VMEM((2, CHUNKS, MESSAGE, 8, LANES), jnp.float32),
            pltpu.VMEM((2, EDGE, 8, LANES), jnp.float32),
            pltpu.VMEM((rounds, 2, CHUNKS, MESSAGE, 8, LANES), jnp.float32),
            pltpu.VMEM((rounds, 2, EDGE, 8, LANES), jnp.float32),
            pltpu.SemaphoreType.DMA((rounds, 2, CHUNKS)),
            pltpu.SemaphoreType.DMA((rounds, 2, CHUNKS)),
            pltpu.SemaphoreType.DMA((rounds, 2)),
            pltpu.SemaphoreType.DMA((rounds, 2)),
            pltpu.SemaphoreType.DMA(()),
        ],
        compiler_params=pltpu.CompilerParams(
            collective_id=0, has_side_effects=True, vmem_limit_bytes=56 * 2**20
        ),
        name="filter_cells",
    )(index, keys, place_codes(), wavefunctions, stiff, row_mass(), scale, potential)


def split(x):
    high = x.astype(jnp.bfloat16)
    return high, (x - high.astype(jnp.float32)).astype(jnp.bfloat16)


def exact_dot_t(x, y):
    return lax.dot_general(
        x, y, (((1,), (1,)), ((), ())), precision=HIGHEST, preferred_element_type=jnp.float32
    )


def inverse_of_block(block):
    size = BANDS_DEV
    row_at = lax.broadcasted_iota(jnp.int32, (size, LANES), 0)
    lane = lax.broadcasted_iota(jnp.int32, (size, LANES), 1)
    wide = jnp.concatenate([block, jnp.zeros((size, LANES - size), jnp.float32)], axis=1)
    wide = jnp.where(lane == row_at + size, 1.0, wide)
    tiles = [wide[8 * g : 8 * g + 8] for g in range(size // 8)]
    sub = lax.broadcasted_iota(jnp.int32, (8, LANES), 0)
    for home in range(size // 8):
        live = range(home, size // 8)
        columns = {
            (g, n): jnp.broadcast_to(tiles[g][:, 8 * home + n : 8 * home + n + 1], (8, LANES))
            for g in live for n in range(8)
        }
        for at in range(8):
            scale = 1.0 / columns[home, at][at : at + 1, :]
            ratio = tiles[home][at : at + 1, :] * scale
            ahead = {n: columns[home, n][at : at + 1, :] * scale for n in range(at + 1, 8)}
            for g in live:
                factor = columns[g, at]
                if g == home:
                    factor = jnp.where(sub > at, factor, 0.0)
                for n in range(at + 1, 8):
                    columns[g, n] = columns[g, n] - factor * ahead[n]
                tiles[g] = tiles[g] - factor * ratio
    wide = jnp.concatenate(tiles, axis=0)
    pivots = jnp.sum(jnp.where(lane == row_at, wide, 0.0), axis=1, keepdims=True)
    return wide[:, size:] * (1.0 / jnp.sqrt(pivots))


def finish_kernel(
    owned, far_cells, table_vector, out, table, cells, wide_rows, own, weight, partner, cross, partner_cross,
    sums, by_plane, piece, by_z, everyone, inverse,
    table_sem, cell_sems, pair_sems, first_sems, second_sems, forward_sems, again_sems, plane_sems, z_sems, band_sems, back_sems,
):
    table_copy = pltpu.make_async_copy(table_vector, table, table_sem)
    table_copy.start()
    part = TILES // CELL_PARTS
    cell_copies = [
        pltpu.make_async_copy(far_cells.at[pl.ds(p * part, part)], cells.at[pl.ds(p * part, part)], cell_sems.at[p])
        for p in range(CELL_PARTS)
    ]
    for step in cell_copies:
        step.start()
    space, band = lax.axis_index("space"), lax.axis_index("band")
    at_plane = lax.rem(space, PLANE_PEERS)
    core = lax.rem(band, 2)
    chip = band // 2
    mate = band + 1 - 2 * core
    across = lax.rem(band + 2, N_BAND)
    across_mate = lax.rem(mate + 2, N_BAND)

    def plane_peer(k):
        return {"space": space - at_plane + lax.rem(at_plane + k, PLANE_PEERS)}

    z_peer = {"space": lax.rem(space + PLANE_PEERS, 2 * PLANE_PEERS)}
    band_peers = [{"band": lax.rem(band + k, N_BAND)} for k in (1, 2, 3)]
    barrier = pltpu.get_barrier_semaphore()
    peers = [plane_peer(k) for k in range(1, PLANE_PEERS)] + [z_peer] + band_peers
    for peer in peers:
        pl.semaphore_signal(barrier, inc=1, device_id=peer, device_id_type=MESH)

    def send(source, target, sems, slot, peer):
        return pltpu.make_async_remote_copy(
            src_ref=source,
            dst_ref=target,
            send_sem=sems.at[0, slot],
            recv_sem=sems.at[1, slot],
            device_id=peer,
            device_id_type=MESH,
        )

    left_half = lax.broadcasted_iota(jnp.int32, (ROWS, LANES), 1) < HALF

    def widen(t, carry):
        values = cells[t]
        turned = pltpu.roll(values, HALF, 1)
        for slot, (left, right) in enumerate(((values, turned), (turned, values))):
            rows = pl.ds(pl.multiple_of((slot * TILES + t) * ROWS, ROWS), ROWS)
            wide_rows[rows, :] = jnp.where(left_half, left, right)
        return carry

    for p in range(CELL_PARTS):
        cell_copies[p].wait()
        lax.fori_loop(p * part, (p + 1) * part, widen, 0)
    table_copy.wait()
    low_lane = lax.broadcasted_iota(jnp.int32, (1, LANES), 1) < HALF

    def gather(i):
        start = pl.multiple_of(i * LANES, LANES)
        for k in range(LANES):
            first = wide_rows[pl.ds(table[i, k], 1), :]
            second = wide_rows[pl.ds(table[i + GROUPS // 2, k], 1), :]
            own[pl.ds(start + k, 1), :] = jnp.where(low_lane, first, second)

    def weigh(i, carry):
        def weights(at):
            row = table_vector[pl.ds(at, 1), :] & (ROWS - 1)
            shared = ((row < PLANE) | (row == CORNERS)) & (space > 0)
            return jnp.broadcast_to(jnp.where(shared | (row >= CORNERS + 5), 0.0, 1.0), (HALF, LANES))

        both = jnp.concatenate([weights(i), weights(i + GROUPS // 2)], axis=0)
        weight[pl.ds(pl.multiple_of(i * LANES, LANES), LANES), :] = both.T
        return carry

    half = PAIRS // 2
    size = half // PIECES

    def piece_rows(side, p):
        return pl.ds(pl.multiple_of(side * half + p * size, size), size)

    to_mate, to_across = {"band": mate}, {"band": across}
    pieces = range(PIECES)
    first = [
        send(own.at[piece_rows(chip, p)], cross.at[piece_rows(chip, p)], first_sems, p, to_across) for p in pieces
    ]
    second = [
        send(own.at[piece_rows(1 - chip, p)], cross.at[piece_rows(1 - chip, p)], second_sems, p, to_across)
        for p in pieces
    ]
    forward_first = [
        send(cross.at[piece_rows(1 - chip, p)], partner_cross.at[piece_rows(1 - chip, p)], forward_sems, p, to_mate)
        for p in pieces
    ]
    forward_second = [
        send(cross.at[piece_rows(chip, p)], partner_cross.at[piece_rows(chip, p)], again_sems, p, to_mate)
        for p in pieces
    ]
    halves = [pl.ds(pl.multiple_of(side * half, half), half) for side in (chip, 1 - chip)]
    pair = [send(own.at[rows], partner.at[rows], pair_sems, k, to_mate) for k, rows in enumerate(halves)]

    groups = GROUPS // 4
    per_piece = groups // PIECES
    pl.semaphore_wait(barrier, len(peers))
    for p in pieces:
        base = chip * groups + p * per_piece
        lax.fori_loop(0, per_piece, lambda i, carry, base=base: (gather(base + i), carry)[1], 0)
        first[p].start()
    for p in pieces:
        base = (1 - chip) * groups + p * per_piece
        lax.fori_loop(0, per_piece, lambda i, carry, base=base: (gather(base + i), carry)[1], 0)
        if p == 0:
            second[0].start()
            pair[0].start()
    pair[1].start()
    lax.fori_loop(0, GROUPS // 2, weigh, 0)

    def products(left, right):
        both = lax.dot_general(
            jnp.concatenate(split(left), axis=1),
            jnp.concatenate(split(right), axis=1),
            (((0,), (0,)), ((), ())),
            preferred_element_type=jnp.float32,
        )
        upper = both[:LANES, : 2 * LANES] + both[:LANES, 2 * LANES :]
        return upper + (both[LANES:, : 2 * LANES] + both[LANES:, 2 * LANES :])

    def block_rows(i):
        return pl.ds(pl.multiple_of(i * BLOCK, BLOCK), BLOCK)

    def own_terms(i, total):
        rows = block_rows(i)
        mine = own[rows, :]
        scale = weight[rows, :]
        return total + products(mine * scale, jnp.concatenate([mine, partner[rows, :]], axis=1))

    def cross_terms(i, total):
        rows = block_rows(i)
        scale = weight[rows, :]
        return total + products(
            cross[rows, :], jnp.concatenate([own[rows, :] * scale, partner[rows, :] * scale], axis=1)
        )

    low_half = lax.broadcasted_iota(jnp.int32, (BANDS_DEV, LANES), 1) < HALF

    def fold(total):
        size = BANDS_DEV
        left = total[:size, :LANES] + pltpu.roll(total[size:, :LANES], HALF, 1)
        right = pltpu.roll(total[:size, LANES:], HALF, 1) + total[size:, LANES:]
        return jnp.where(low_half, left, right)

    zero = jnp.zeros((LANES, 2 * LANES), jnp.float32)
    per_half = half // BLOCK
    total = zero
    for k, side in enumerate((chip, 1 - chip)):
        pair[k].wait()
        total = lax.fori_loop(
            0, per_half, lambda i, total, side=side: own_terms(side * per_half + i, total), total
        )
    sums[0:BANDS_DEV, :] = fold(total)
    blocks = size // BLOCK
    total = zero
    for p in pieces:
        first[p].wait()
        forward_first[p].start()
        base = (1 - chip) * (half // BLOCK) + p * blocks
        total = lax.fori_loop(0, blocks, lambda i, total, base=base: cross_terms(base + i, total), total)
    sums[BANDS_DEV : 2 * BANDS_DEV, :] = fold(total)


    def rows_of(at):
        return pl.ds(pl.multiple_of(8 * at, 8), 8)

    others = range(1, PLANE_PEERS)
    scatter = [
        send(sums.at[rows_of(lax.rem(at_plane + k, PLANE_PEERS))], by_plane.at[k - 1], plane_sems, k - 1, plane_peer(k))
        for k in others
    ]
    for step in scatter:
        step.start()
    for step in scatter:
        step.wait()
    mine = sums[rows_of(at_plane), :]
    for k in others:
        mine = mine + by_plane[k - 1]
    piece[...] = mine
    to_z = send(piece, by_z, z_sems, 0, z_peer)
    to_z.start()
    to_z.wait()
    everyone[at_plane, band] = piece[...] + by_z[...]
    to_band = [
        send(everyone.at[at_plane, band], everyone.at[at_plane, band], band_sems, k, peer)
        for k, peer in enumerate(band_peers)
    ]
    for step in to_band:
        step.start()
    for step in to_band:
        step.wait()
    for p in pieces[1:]:
        second[p].start()
    back = [send(everyone.at[at_plane], everyone.at[at_plane], back_sems, k - 1, plane_peer(k)) for k in others]
    for step in back:
        step.start()
    for step in back:
        step.wait()

    totals = [
        jnp.concatenate([everyone[q, b] for q in range(PLANE_PEERS)], axis=0) * (1.0 / owned) for b in range(N_BAND)
    ]

    def part(b, r, c):
        size = BANDS_DEV
        return totals[b][r * size : (r + 1) * size, c * size : (c + 1) * size]

    margin = {(b, b): part(b, 0, 0) for b in range(N_BAND)}
    margin[1, 0], margin[3, 2] = part(1, 0, 1), part(3, 0, 1)
    margin[2, 0] = part(0, 1, 0) + part(2, 1, 0).T
    margin[2, 1] = part(0, 1, 1) + part(3, 1, 1).T
    margin[3, 0] = part(1, 1, 1) + part(2, 1, 1).T
    margin[3, 1] = part(1, 1, 0) + part(3, 1, 0).T

    inverses, factor, whole = [], {}, {}
    for k in range(N_BAND):
        diagonal = inverse_of_block(margin[k, k])
        inverses.append(diagonal)
        for i in range(k + 1, N_BAND):
            factor[i, k] = exact_dot_t(margin[i, k], diagonal)
        for i in range(k + 1, N_BAND):
            for j in range(k + 1, i + 1):
                margin[i, j] = margin[i, j] - exact_dot_t(factor[i, k], factor[j, k])
        whole[k, k] = diagonal
        for j in range(k):
            total = exact_dot(factor[k, j], whole[j, j])
            for m in range(j + 1, k):
                total = total + exact_dot(factor[k, m], whole[m, j])
            whole[k, j] = -exact_dot(diagonal, total)
        if k == 2:
            second[0].wait()
            forward_second[0].start()
    padding = jnp.zeros((BANDS_DEV, LANES - BANDS_DEV), jnp.float32)
    for i in range(N_BAND):
        for j in range(N_BAND):
            if j <= i:
                inverse[i, j] = jnp.concatenate([whole[i, j], padding], axis=1)
            else:
                inverse[i, j] = jnp.zeros((BANDS_DEV, LANES), jnp.float32)
    panels = [inverse[band, source] for source in (band, mate, across, across_mate)]
    left = jnp.concatenate(
        [
            jnp.concatenate(panels, axis=1),
            jnp.concatenate([pltpu.roll(panel, HALF, 1) for panel in panels], axis=1),
        ],
        axis=0,
    )
    left_high, left_low = split(left)
    left = jnp.concatenate(
        [jnp.concatenate([left_high, left_high], axis=1), jnp.concatenate([left_low, left_low], axis=1)], axis=0
    )

    def rotate(i, carry):
        rows = block_rows(i)
        right = jnp.concatenate([ref[rows, :] for ref in (own, partner, cross, partner_cross)], axis=1)
        both = lax.dot_general(
            left,
            jnp.concatenate(split(right), axis=1),
            (((1,), (1,)), ((), ())),
            preferred_element_type=jnp.float32,
        )
        rotated = both[: 2 * BANDS_DEV] + both[2 * BANDS_DEV :]
        out[:, rows] = rotated[:BANDS_DEV]
        out[:, pl.ds(pl.multiple_of(PAIRS + i * BLOCK, BLOCK), BLOCK)] = rotated[BANDS_DEV:]
        return carry

    def rotate_piece(side, p):
        base = side * per_half + p * blocks
        lax.fori_loop(0, blocks, lambda i, carry: rotate(base + i, carry), 0)

    for p in pieces:
        forward_first[p].wait()
        rotate_piece(1 - chip, p)
        if p > 0:
            second[p].wait()
            forward_second[p].start()
    for p in pieces:
        forward_second[p].wait()
        rotate_piece(chip, p)


def finish(cells, table, owned_count):
    whole = pl.BlockSpec(memory_space=pltpu.VMEM)
    nodes = pltpu.VMEM((PAIRS, LANES), jnp.float32)

    def small(*shape):
        return pltpu.VMEM(shape, jnp.float32)

    def sems(slots):
        return pltpu.SemaphoreType.DMA((2, slots))

    return pl.pallas_call(
        functools.partial(finish_kernel, owned_count),
        out_shape=jax.ShapeDtypeStruct((BANDS_DEV, 2 * PAIRS), jnp.float32),
        in_specs=[pl.BlockSpec(memory_space=pltpu.MemorySpace.HBM), whole],
        out_specs=whole,
        scratch_shapes=[
            pltpu.SMEM(table.shape, jnp.int32),
            small(TILES, ROWS, LANES),
            small(2 * TILES * ROWS, LANES),
            nodes, nodes, nodes, nodes, nodes,
            small(LANES, LANES), small(PLANE_PEERS - 1, 8, LANES), small(8, LANES), small(8, LANES),
            small(PLANE_PEERS, N_BAND, 8, LANES),
            small(N_BAND, N_BAND, BANDS_DEV, LANES),
            pltpu.SemaphoreType.DMA(()),
            pltpu.SemaphoreType.DMA((CELL_PARTS,)),
            sems(2), sems(PIECES), sems(PIECES), sems(PIECES), sems(PIECES),
            sems(PLANE_PEERS - 1), sems(1), sems(3), sems(PLANE_PEERS - 1),
        ],
        compiler_params=pltpu.CompilerParams(
            collective_id=1, has_side_effects=True, vmem_limit_bytes=48 * 2**20
        ),
        name="finish",
    )(cells, table)


def shards(
    wavefunctions, stiffness, cell_scale, cell_potential, connectivity, lower_face, upper_face
):
    node_count = wavefunctions.shape[1]
    face_count = lower_face.shape[0]
    space_count = lax.axis_size("space")
    owned_count = node_count * space_count - face_count * (space_count - 1)

    index, keys, scale, potential, stiff = make_layout(connectivity, cell_scale, cell_potential, stiffness)
    cells, table = filter_cells(index, keys, wavefunctions, stiff, scale, potential)
    return finish(cells, table, owned_count)[:, :node_count]


def solution(mesh):
    placed = (
        P("band", "space"),
        P(),
        P("space"),
        P("space"),
        P(None, "space"),
        P("space"),
        P("space"),
    )
    return jax.shard_map(
        shards, mesh=mesh, in_specs=placed, out_specs=P("band", "space"), check_vma=False
    )
```

```python
import functools

import jax
import jax.numpy as jnp
import numpy as np
from jax import lax
from jax.experimental import pallas as pl
from jax.experimental.pallas import tpu as pltpu
from jax.sharding import PartitionSpec as P

FILTER_DEG = 4
GLL_WEIGHTS = (0.1, 49.0 / 90.0, 32.0 / 45.0, 49.0 / 90.0, 0.1)
CENTER = 11.0
HALF_WIDTH = 9.0
HIGHEST = lax.Precision.HIGHEST
MESH = pl.DeviceIdType.MESH

CELLS_Y = 20
CELLS_Z = 6
CHUNKS = CELLS_Y // 2
TILES = CHUNKS * CELLS_Z
SLOTS = 2 * TILES
HALF = 64
LANES = 128
ROWS = 128
PLANE = 24
CORNERS = 5 * PLANE
MESSAGE = 2 * CELLS_Z + 1
EDGE = CELLS_Z + 1

NODES = 10125
PAIRS = 5120
BLOCK = 256
PIECES = 5
CELL_PARTS = 4
GROUPS = 2 * PAIRS // LANES
PLANE_PEERS = 16
BANDS_DEV = 64
N_BAND = 4


def row_of_node(a, b, c):
    if (b, c) == (4, 4):
        return CORNERS + a
    rows = {(0, 0): 0, (4, 0): 8, (0, 4): 16, (1, 1): 7, (1, 2): 15, (1, 3): 23}
    for k in (1, 2, 3):
        rows[(0, k)] = k
        rows[(4, k)] = 8 + k
        rows[(k, 0)] = 3 + k
        rows[(k, 4)] = 16 + 3 + k
        rows[(2, k)] = 8 + 3 + k
        rows[(3, k)] = 16 + k
    return PLANE * a + rows[(b, c)]


def node_rows(planes, chosen):
    return [
        (25 * a + 5 * b + c, row_of_node(a, b, c))
        for a in planes for b in range(5) for c in range(5) if chosen(b, c)
    ]


LOCAL_ROWS = [row for _, row in node_rows(range(5), lambda b, c: True)]


def owners():
    owned = np.zeros((LANES, SLOTS), np.float32)
    for slot in range(SLOTS):
        tile, half = divmod(slot, 2)
        last_y = half == 1 and tile >= TILES - CELLS_Z
        last_z = tile % CELLS_Z == CELLS_Z - 1
        for node, _ in node_rows(range(5), lambda b, c: (b < 4 or last_y) and (c < 4 or last_z)):
            owned[node, slot] = 1.0
    return owned


def place_codes():
    codes = np.zeros((LANES, LANES), np.float32)
    codes[:125, :] = 2.0 * np.array(LOCAL_ROWS)[:, None] + np.arange(LANES)[None, :] % 2
    return codes


def row_selector():
    chosen = np.zeros((ROWS, 125), np.float32)
    chosen[LOCAL_ROWS, np.arange(125)] = 1.0
    return chosen


def row_mass():
    weights = np.array(GLL_WEIGHTS, np.float32)
    mass = (weights[:, None, None] * weights[None, :, None] * weights[None, None, :]).reshape(-1)
    spread = np.zeros((ROWS, LANES), np.float32)
    spread[LOCAL_ROWS, :] = mass[:, None]
    return spread


def local(a, b, c):
    return 25 * a + 5 * b + c


def exact_dot(x, y):
    return jnp.dot(x, y, precision=HIGHEST, preferred_element_type=jnp.float32)


def chain_counts(before, doublings):
    size = before.shape[0]
    eye = (
        lax.broadcasted_iota(jnp.int32, (size, size), 0) == lax.broadcasted_iota(jnp.int32, (size, size), 1)
    ).astype(jnp.float32)
    total, power = eye + before, before
    for _ in range(doublings):
        power = jnp.dot(power, power, preferred_element_type=jnp.float32)
        total = total + jnp.dot(total, power, preferred_element_type=jnp.float32)
    return jnp.sum(total, axis=0, keepdims=True) - 1.0


def layout_kernel(
    conn_ref, cell_scale_ref, cell_potential_ref, stiff_ref, select_ref, owned_ref,
    index_ref, keys_ref, scale_ref, potential_ref, stiffness_ref,
):
    conn = conn_ref[...].astype(jnp.float32)
    cells = conn.shape[1]
    on_rows = lax.broadcasted_iota(jnp.int32, (cells, cells), 0)
    on_lanes = lax.broadcasted_iota(jnp.int32, (cells, cells), 1)

    def as_column(row):
        return jnp.sum(jnp.where(on_rows == on_lanes, row, 0.0), axis=1, keepdims=True)

    def row_of(node):
        return conn[node : node + 1, :]

    after_z = (as_column(row_of(local(2, 2, 4))) == row_of(local(2, 2, 0))).astype(jnp.float32)
    after_y = (as_column(row_of(local(2, 4, 2))) == row_of(local(2, 0, 2))).astype(jnp.float32)
    at_z = chain_counts(after_z, 2)
    at_y = chain_counts(after_y, 4)
    upper_half = at_y >= CHUNKS
    tile = (at_y - jnp.where(upper_half, 1.0 * CHUNKS, 0.0)) * CELLS_Z + at_z
    slot = 2.0 * tile + jnp.where(upper_half, 1.0, 0.0)
    moved = (as_column(slot) == on_lanes.astype(jnp.float32)).astype(jnp.float32)
    index = (exact_dot(conn, moved) + 0.5).astype(jnp.int32)
    index_ref[...] = index
    index = jnp.concatenate([index, jnp.zeros((LANES - index.shape[0], cells), jnp.int32)], axis=0)
    keys = jnp.where(owned_ref[...] > 0.5, index, -1)
    keys_ref[...] = jnp.concatenate([keys, jnp.full((LANES, LANES - cells), -1, jnp.int32)], axis=1)

    wanted = lax.broadcasted_iota(jnp.int32, (TILES, cells), 0).astype(jnp.float32)
    lane = lax.broadcasted_iota(jnp.int32, (TILES, LANES), 1)

    def spread(row):
        low, high = [
            jnp.sum(jnp.where(slot == 2.0 * wanted + half, row, 0.0), axis=1, keepdims=True) for half in (0.0, 1.0)
        ]
        return jnp.where(lane < HALF, low, high)

    scale_ref[...] = spread(cell_scale_ref[...])
    potential_ref[...] = spread(cell_potential_ref[...])

    select = select_ref[...]
    part = exact_dot(select, stiff_ref[...])
    stiff = lax.dot_general(
        part, select, (((1,), (1,)), ((), ())), precision=HIGHEST, preferred_element_type=jnp.float32
    )
    high = stiff.astype(jnp.bfloat16)
    low = (stiff - high.astype(jnp.float32)).astype(jnp.bfloat16)
    stiffness_ref[...] = jnp.concatenate(
        [jnp.concatenate([high, high], axis=1), jnp.concatenate([low, low], axis=1)], axis=0
    )


def make_layout(connectivity, cell_scale, cell_potential, stiffness):
    cells = connectivity.shape[1]
    whole = pl.BlockSpec(memory_space=pltpu.VMEM)
    return pl.pallas_call(
        layout_kernel,
        out_shape=(
            jax.ShapeDtypeStruct((125, cells), jnp.int32),
            jax.ShapeDtypeStruct((LANES, LANES), jnp.int32),
            jax.ShapeDtypeStruct((TILES, LANES), jnp.float32),
            jax.ShapeDtypeStruct((TILES, LANES), jnp.float32),
            jax.ShapeDtypeStruct((2 * ROWS, 2 * ROWS), jnp.bfloat16),
        ),
        in_specs=[whole] * 6,
        out_specs=(whole,) * 5,
        name="layout",
    )(connectivity, cell_scale[None, :], cell_potential[None, :], stiffness, row_selector(), owners())


def each_node_once(planes, visit):
    def loop(count, tile_of, nodes, halves=(0, 1)):
        def body(i, carry):
            visit(tile_of(i), nodes, halves)
            return carry

        lax.fori_loop(0, count, body, 0)

    loop(TILES, lambda i: i, node_rows(planes, lambda b, c: b < 4 and c < 4))
    loop(CELLS_Z, lambda i: TILES - CELLS_Z + i, node_rows(planes, lambda b, c: b == 4 and c < 4), (1,))
    loop(1, lambda i: TILES - 1, node_rows(planes, lambda b, c: b == 4 and c == 4), (1,))
    loop(CHUNKS, lambda i: i * CELLS_Z + CELLS_Z - 1, node_rows(planes, lambda b, c: b < 4 and c == 4))


def filter_kernel(
    index_vector_ref, keys_ref, codes_ref, waves_ref, stiff_ref, mass_ref, scale_ref, potential_ref, out_ref, table_ref,
    index_ref, places, other, product, face, doubled, sends, edge_sends, receives, edge_receives,
    send_sems, receive_sems, edge_send_sems, edge_receive_sems, index_sem,
):
    count = lax.axis_size("space")
    me = lax.axis_index("space")
    above, below = lax.rem(me + 1, count), lax.rem(me + count - 1, count)
    has_below, has_above = me > 0, me < count - 1

    barrier = pltpu.get_barrier_semaphore()
    for neighbour in (below, above):
        pl.semaphore_signal(barrier, inc=1, device_id={"space": neighbour}, device_id_type=MESH)
    pl.semaphore_wait(barrier, 2)

    sub = lax.broadcasted_iota(jnp.int32, (8, LANES), 0)
    lane = lax.broadcasted_iota(jnp.int32, (8, LANES), 1)
    corner = sub == 0
    along_y = sub <= 3
    along_z = corner | ((sub >= 4) & (sub <= 6))
    in_y_group = (sub >= 4) & (sub <= 6)
    in_z_group = ((sub >= 1) & (sub <= 3)) | (sub == 7)
    low_half = lane < HALF
    corners = slice(CORNERS, CORNERS + 8)
    last_tile = TILES - 1
    bottom, top = 0, 4
    inner = (1, 2, 3)

    def group(a, g):
        return slice(PLANE * a + 8 * g, PLANE * a + 8 * g + 8)

    def turn(value, by):
        return pltpu.roll(value, by % 8, 0) if by % 8 else value

    def over_chunks(body):
        def step(c, carry):
            body(c)
            return carry

        lax.fori_loop(0, CHUNKS, step, 0)

    def message(step, way, c):
        return pltpu.make_async_remote_copy(
            src_ref=sends.at[way, c],
            dst_ref=receives.at[step, way, c],
            send_sem=send_sems.at[step, way, c],
            recv_sem=receive_sems.at[step, way, c],
            device_id={"space": above if way == 0 else below},
            device_id_type=MESH,
        )

    def edge_message(step, way):
        return pltpu.make_async_remote_copy(
            src_ref=edge_sends.at[way],
            dst_ref=edge_receives.at[step, way],
            send_sem=edge_send_sems.at[step, way],
            recv_sem=edge_receive_sems.at[step, way],
            device_id={"space": above if way == 0 else below},
            device_id_type=MESH,
        )

    def start(copy, way):
        @pl.when(has_above if way == 0 else has_below)
        def _():
            copy.start()

    def finish_copy(copy, way):
        @pl.when(has_above if way == 0 else has_below)
        def _():
            copy.wait_send()

        @pl.when(has_below if way == 0 else has_above)
        def _():
            copy.wait_recv()

    def send_chunk(step, way, c, tiles, ends):
        for z, (own, y, d) in enumerate(tiles):
            sends[way, c, 2 * z] = own
            sends[way, c, 2 * z + 1] = jnp.where(corner, turn(y, 1), jnp.where(in_y_group, y, d))
        sends[way, c, MESSAGE - 1] = tiles[CELLS_Z - 1][2]
        start(message(step, way, c), way)

        @pl.when(c == CHUNKS - 1)
        def _():
            for z in range(CELLS_Z):
                edge_sends[way, z] = tiles[z][1]
            edge_sends[way, EDGE - 1] = ends
            start(edge_message(step, way), way)

    def unpack(step, way, c, z):
        inside = receives[step, way, c, 2 * z + 1]
        y = jnp.where(in_y_group, inside, jnp.where(sub == 7, turn(inside, 7), 0.0))
        d = jnp.where(in_z_group, inside, receives[step, way, c, MESSAGE - 1])
        return [receives[step, way, c, 2 * z], y, d]

    def unpack_corner(step, way):
        return turn(edge_receives[step, way, EDGE - 1], 4)

    def fill(ref, c):
        @pl.when(c == CHUNKS - 1)
        def _():
            end = ref[last_tile, corners, :]
            for a in range(5):
                for z in range(CELLS_Z):
                    ref[TILES + z, group(a, 0), :] = jnp.where(
                        low_half, pltpu.roll(ref[z, group(a, 0), :], HALF, 1), ref[TILES - CELLS_Z + z, group(a, 1), :]
                    )
                ref[TILES + CELLS_Z - 1, group(a, 2), :] = jnp.where(
                    low_half, pltpu.roll(ref[CELLS_Z - 1, group(a, 2), :], HALF, 1), turn(end, -a)
                )

        first = c * CELLS_Z
        ends = [ref[first + z, corners, :] for z in range(CELLS_Z)]
        for a in range(5):
            y_new = [
                jnp.where(along_y, ref[first + CELLS_Z + z, group(a, 0), :], ref[first + z, group(a, 1), :])
                for z in range(CELLS_Z)
            ]
            for z in range(CELLS_Z):
                ref[first + z, group(a, 1), :] = y_new[z]
                if z < CELLS_Z - 1:
                    ref[first + z, group(a, 2), :] = jnp.where(
                        along_z, ref[first + z + 1, group(a, 0), :], ref[first + z, group(a, 2), :]
                    )
                    ahead = y_new[z + 1]
                else:
                    ahead = ref[first + CELLS_Z + z, group(a, 2), :]
                ends[z] = jnp.where(sub == a, turn(ahead, a), ends[z])
        for z in range(CELLS_Z):
            ref[first + z, corners, :] = ends[z]

    def assembled(c, a):
        tiles, corner_terms = [], []
        for z in range(CELLS_Z):
            t = c * CELLS_Z + z
            own, y, d = [product[t + CELLS_Z, group(a, g), :] for g in range(3)]
            own = own + jnp.where(along_y, product[t, group(a, 1), :], 0.0)
            d = d + jnp.where(corner, turn(product[t, corners, :], -a), 0.0)
            tiles.append([own, y, d])
            corner_terms.append(turn(product[t + CELLS_Z, corners, :], -a))
        for z in range(1, CELLS_Z):
            tiles[z][0] = tiles[z][0] + jnp.where(along_z, tiles[z - 1][2], 0.0)
            tiles[z][1] = tiles[z][1] + jnp.where(corner, corner_terms[z - 1], 0.0)
        return tiles

    def multiply(current, c):
        mass = mass_ref[...]
        for pair in range(CELLS_Z // 2):
            t = c * CELLS_Z + 2 * pair
            values = [current[t], current[t + 1]]
            high, low = split(jnp.concatenate(values, axis=1))
            result = jnp.dot(
                stiff_ref[...], jnp.concatenate([high, low], axis=0), preferred_element_type=jnp.float32
            )
            result = result[:ROWS] + result[ROWS:]
            for k in range(2):
                product[t + CELLS_Z + k] = result[:, k * LANES : (k + 1) * LANES] * scale_ref[
                    pl.ds(t + k, 1), :
                ] + mass * potential_ref[pl.ds(t + k, 1), :] * values[k]

        @pl.when(c == CHUNKS - 1)
        def _():
            for z in range(CELLS_Z):
                for rows in [group(a, 1) for a in range(5)] + [corners]:
                    turned = pltpu.roll(product[TILES + z, rows, :], HALF, 1)
                    product[z, rows, :] = jnp.where(low_half, 0.0, turned)

    def buffers(step):
        return (out_ref, other) if step % 2 == 0 else (other, out_ref)

    def factor(step):
        return (1.0 if step == 0 else 2.0) / HALF_WIDTH

    def advance(step, t, rows, total):
        current, previous = buffers(step)
        value = (total - CENTER * current[t, rows, :]) * factor(step)
        previous[t, rows, :] = value if step == 0 else value - previous[t, rows, :]

    def assemble(step, c):
        ends = product[TILES + CELLS_Z - 1, corners, :]
        for way, a in ((0, top), (1, bottom)):
            tiles = assembled(c, a)
            for z in range(CELLS_Z):
                for g in range(3):
                    face[way, c * CELLS_Z + z, 8 * g : 8 * g + 8, :] = tiles[z][g]
            send_chunk(step + 1, way, c, tiles, ends)
        for a in inner:
            tiles = assembled(c, a)
            for z in range(CELLS_Z):
                for g in range(3):
                    advance(step, c * CELLS_Z + z, group(a, g), tiles[z][g])

    def advance_faces(step, c):
        for way, a, valid in ((0, bottom, has_below), (1, top, has_above)):
            finish_copy(message(step + 1, way, c), way)
            for z in range(CELLS_Z):
                t = c * CELLS_Z + z
                arrived = unpack(step + 1, way, c, z)
                for g in range(3):
                    total = face[1 - way, t, 8 * g : 8 * g + 8, :] + jnp.where(valid, arrived[g], 0.0)
                    advance(step, t, group(a, g), total)

        @pl.when(c == CHUNKS - 1)
        def _():
            previous = buffers(step)[1]
            ends = product[TILES + CELLS_Z - 1, corners, :]
            for way, a, valid in ((0, bottom, has_below), (1, top, has_above)):
                finish_copy(edge_message(step + 1, way), way)
                for z in range(CELLS_Z):
                    rows = group(a, 1)
                    edge = jnp.where(along_y & valid, edge_receives[step + 1, way, z], 0.0)
                    previous[TILES - CELLS_Z + z, rows, :] = previous[TILES - CELLS_Z + z, rows, :] + factor(step) * edge
                ends = ends + jnp.where((sub == a) & valid, unpack_corner(step + 1, way), 0.0)
            advance(step, last_tile, corners, ends)

    def tabulate(step):
        high = lax.broadcasted_iota(jnp.int32, (GROUPS, LANES), 0)
        low = lax.broadcasted_iota(jnp.int32, (LANES, LANES), 0)
        tile = (lax.broadcasted_iota(jnp.int32, (1, LANES), 1) // 2).astype(jnp.float32)

        def body(i, total):
            left, right = [], []
            for k in range(2):
                at = pl.ds(2 * i + k, 1)
                key = keys_ref[at, :]
                left.append(jnp.where(high == key >> 7, 1.0, 0.0).astype(jnp.bfloat16))
                hit = low == key & (LANES - 1)
                values = [jnp.where(hit, tile, 0.0), jnp.where(hit, codes_ref[at, :], 0.0)]
                right.append(jnp.concatenate(values, axis=0).astype(jnp.bfloat16))
            return total + lax.dot_general(
                jnp.concatenate(left, axis=1),
                jnp.concatenate(right, axis=1),
                (((1,), (1,)), ((), ())),
                preferred_element_type=jnp.float32,
            )

        part = LANES // 2 // FILTER_DEG
        total = jnp.zeros((GROUPS, 2 * LANES), jnp.float32) if step == 0 else places[...]
        total = lax.fori_loop(part * step, part * (step + 1), body, total)
        if step < FILTER_DEG - 1:
            places[...] = total
            return
        total = total + 0.5
        tiles = total[:, :LANES].astype(jnp.int32)
        codes = total[:, LANES:].astype(jnp.int32)
        node = high * LANES + lax.broadcasted_iota(jnp.int32, (GROUPS, LANES), 1)
        place = (codes & 1) * (TILES * ROWS) + tiles * ROWS + (codes >> 1)
        table_ref[...] = jnp.where(node < NODES, place, CORNERS + 5)

    index_copy = pltpu.make_async_copy(index_vector_ref, index_ref, index_sem)
    index_copy.start()
    node_count = waves_ref.shape[1]
    whole_blocks = node_count // LANES

    def transpose(i, carry):
        at = pl.ds(pl.multiple_of(i * LANES, LANES), LANES)
        block = waves_ref[:, at]
        doubled[at, :] = jnp.concatenate([block, block], axis=0).T
        return carry

    lax.fori_loop(0, whole_blocks, transpose, 0)
    rest = node_count - whole_blocks * LANES
    block = jnp.concatenate(
        [waves_ref[:, whole_blocks * LANES :], jnp.zeros((HALF, LANES - rest), jnp.float32)], axis=1
    )
    doubled[whole_blocks * LANES : (whole_blocks + 1) * LANES, :] = jnp.concatenate([block, block], axis=0).T

    unused = jnp.zeros((TILES + CELLS_Z, ROWS - CORNERS, LANES), jnp.float32)
    out_ref[:, CORNERS:, :] = unused
    other[:, CORNERS:, :] = unused
    low_row = lax.broadcasted_iota(jnp.int32, (1, LANES), 1) < HALF

    def gather(t, nodes, halves):
        for node, row in nodes:
            first = doubled[pl.ds(index_ref[node, 2 * t], 1), :]
            second = doubled[pl.ds(index_ref[node, 2 * t + 1], 1), :]
            out_ref[t, row : row + 1, :] = jnp.where(low_row, first, second)

    index_copy.wait()
    each_node_once((top,), gather)

    def send_owner(c):
        tiles = [[out_ref[c * CELLS_Z + z, group(top, g), :] for g in range(3)] for z in range(CELLS_Z)]
        send_chunk(0, 0, c, tiles, out_ref[last_tile, corners, :])

    over_chunks(send_owner)
    each_node_once((0, 1, 2, 3), gather)

    def take_owner(c):
        finish_copy(message(0, 0, c), 0)
        for z in range(CELLS_Z):
            t = c * CELLS_Z + z
            arrived = unpack(0, 0, c, z)
            for g in range(3):
                out_ref[t, group(bottom, g), :] = jnp.where(has_below, arrived[g], out_ref[t, group(bottom, g), :])

        @pl.when(c == CHUNKS - 1)
        def _():
            finish_copy(edge_message(0, 0), 0)
            for z in range(CELLS_Z):
                t = TILES - CELLS_Z + z
                out_ref[t, group(bottom, 1), :] = jnp.where(
                    along_y & has_below, edge_receives[0, 0, z], out_ref[t, group(bottom, 1), :]
                )
            out_ref[last_tile, corners, :] = jnp.where(
                (sub == bottom) & has_below, unpack_corner(0, 0), out_ref[last_tile, corners, :]
            )

    for step in range(FILTER_DEG):
        current = buffers(step)[0]

        def arrive(c):
            if step == 0:
                take_owner(c)
            else:
                advance_faces(step - 1, c)

        def refresh(c):
            fill(current, c)
            multiply(current, c)

        def next_chunk(i, carry):
            arrive(lax.rem(step + i, CHUNKS))
            c = lax.rem(step + i - 1, CHUNKS)
            refresh(c)
            assemble(step, c)
            return carry

        arrive(step)
        arrive(step + 1)
        refresh(step)
        lax.fori_loop(2, CHUNKS, next_chunk, 0)
        refresh((step + CHUNKS - 1) % CHUNKS)
        assemble(step, (step + CHUNKS - 1) % CHUNKS)
        assemble(step, step)
        tabulate(step)

    last = FILTER_DEG
    lax.fori_loop(
        0, CHUNKS, lambda i, carry: (advance_faces(last - 1, lax.rem(last + i, CHUNKS)), carry)[1], 0
    )


def filter_cells(index, keys, wavefunctions, stiff, scale, potential):
    whole = pl.BlockSpec(memory_space=pltpu.VMEM)
    cells = (TILES + CELLS_Z, ROWS, LANES)
    rounds = FILTER_DEG + 1
    blocks = wavefunctions.shape[1] // LANES + 1
    return pl.pallas_call(
        filter_kernel,
        out_shape=(
            jax.ShapeDtypeStruct(cells, jnp.float32), jax.ShapeDtypeStruct((GROUPS, LANES), jnp.int32)
        ),
        in_specs=[whole] * 8,
        out_specs=(whole, whole),
        scratch_shapes=[
            pltpu.SMEM(index.shape, jnp.int32),
            pltpu.VMEM((GROUPS, 2 * LANES), jnp.float32),
            pltpu.VMEM(cells, jnp.float32),
            pltpu.VMEM(cells, jnp.float32),
            pltpu.VMEM((2, TILES, PLANE, LANES), jnp.float32),
            pltpu.VMEM((blocks * LANES, LANES), jnp.float32),
            pltpu.VMEM((2, CHUNKS, MESSAGE, 8, LANES), jnp.float32),
            pltpu.VMEM((2, EDGE, 8, LANES), jnp.float32),
            pltpu.VMEM((rounds, 2, CHUNKS, MESSAGE, 8, LANES), jnp.float32),
            pltpu.VMEM((rounds, 2, EDGE, 8, LANES), jnp.float32),
            pltpu.SemaphoreType.DMA((rounds, 2, CHUNKS)),
            pltpu.SemaphoreType.DMA((rounds, 2, CHUNKS)),
            pltpu.SemaphoreType.DMA((rounds, 2)),
            pltpu.SemaphoreType.DMA((rounds, 2)),
            pltpu.SemaphoreType.DMA(()),
        ],
        compiler_params=pltpu.CompilerParams(
            collective_id=0, has_side_effects=True, vmem_limit_bytes=56 * 2**20
        ),
        name="filter_cells",
    )(index, keys, place_codes(), wavefunctions, stiff, row_mass(), scale, potential)


def split(x):
    high = x.astype(jnp.bfloat16)
    return high, (x - high.astype(jnp.float32)).astype(jnp.bfloat16)


def exact_dot_t(x, y):
    return lax.dot_general(
        x, y, (((1,), (1,)), ((), ())), precision=HIGHEST, preferred_element_type=jnp.float32
    )


def inverse_of_block(block):
    size = BANDS_DEV
    row_at = lax.broadcasted_iota(jnp.int32, (size, LANES), 0)
    lane = lax.broadcasted_iota(jnp.int32, (size, LANES), 1)
    wide = jnp.concatenate([block, jnp.zeros((size, LANES - size), jnp.float32)], axis=1)
    wide = jnp.where(lane == row_at + size, 1.0, wide)
    tiles = [wide[8 * g : 8 * g + 8] for g in range(size // 8)]
    sub = lax.broadcasted_iota(jnp.int32, (8, LANES), 0)
    for home in range(size // 8):
        live = range(home, size // 8)
        columns = {
            (g, n): jnp.broadcast_to(tiles[g][:, 8 * home + n : 8 * home + n + 1], (8, LANES))
            for g in live for n in range(8)
        }
        for at in range(8):
            scale = 1.0 / columns[home, at][at : at + 1, :]
            ratio = tiles[home][at : at + 1, :] * scale
            ahead = {n: columns[home, n][at : at + 1, :] * scale for n in range(at + 1, 8)}
            for g in live:
                factor = columns[g, at]
                if g == home:
                    factor = jnp.where(sub > at, factor, 0.0)
                for n in range(at + 1, 8):
                    columns[g, n] = columns[g, n] - factor * ahead[n]
                tiles[g] = tiles[g] - factor * ratio
    wide = jnp.concatenate(tiles, axis=0)
    pivots = jnp.sum(jnp.where(lane == row_at, wide, 0.0), axis=1, keepdims=True)
    return wide[:, size:] * (1.0 / jnp.sqrt(pivots))


def finish_kernel(
    owned, far_cells, table_vector, out, table, cells, wide_rows, own, weight, partner, cross, partner_cross,
    sums, by_plane, piece, by_z, everyone, inverse,
    table_sem, cell_sems, pair_sems, first_sems, second_sems, forward_sems, again_sems, plane_sems, z_sems, band_sems, back_sems,
):
    table_copy = pltpu.make_async_copy(table_vector, table, table_sem)
    table_copy.start()
    part = TILES // CELL_PARTS
    cell_copies = [
        pltpu.make_async_copy(far_cells.at[pl.ds(p * part, part)], cells.at[pl.ds(p * part, part)], cell_sems.at[p])
        for p in range(CELL_PARTS)
    ]
    for step in cell_copies:
        step.start()
    space, band = lax.axis_index("space"), lax.axis_index("band")
    at_plane = lax.rem(space, PLANE_PEERS)
    core = lax.rem(band, 2)
    chip = band // 2
    mate = band + 1 - 2 * core
    across = lax.rem(band + 2, N_BAND)
    across_mate = lax.rem(mate + 2, N_BAND)

    def plane_peer(k):
        return {"space": space - at_plane + lax.rem(at_plane + k, PLANE_PEERS)}

    z_peer = {"space": lax.rem(space + PLANE_PEERS, 2 * PLANE_PEERS)}
    band_peers = [{"band": lax.rem(band + k, N_BAND)} for k in (1, 2, 3)]
    barrier = pltpu.get_barrier_semaphore()
    peers = [plane_peer(k) for k in range(1, PLANE_PEERS)] + [z_peer] + band_peers
    for peer in peers:
        pl.semaphore_signal(barrier, inc=1, device_id=peer, device_id_type=MESH)

    def send(source, target, sems, slot, peer):
        return pltpu.make_async_remote_copy(
            src_ref=source,
            dst_ref=target,
            send_sem=sems.at[0, slot],
            recv_sem=sems.at[1, slot],
            device_id=peer,
            device_id_type=MESH,
        )

    left_half = lax.broadcasted_iota(jnp.int32, (ROWS, LANES), 1) < HALF

    def widen(t, carry):
        values = cells[t]
        turned = pltpu.roll(values, HALF, 1)
        for slot, (left, right) in enumerate(((values, turned), (turned, values))):
            rows = pl.ds(pl.multiple_of((slot * TILES + t) * ROWS, ROWS), ROWS)
            wide_rows[rows, :] = jnp.where(left_half, left, right)
        return carry

    for p in range(CELL_PARTS):
        cell_copies[p].wait()
        lax.fori_loop(p * part, (p + 1) * part, widen, 0)
    table_copy.wait()
    low_lane = lax.broadcasted_iota(jnp.int32, (1, LANES), 1) < HALF

    def gather(i):
        start = pl.multiple_of(i * LANES, LANES)
        for k in range(LANES):
            first = wide_rows[pl.ds(table[i, k], 1), :]
            second = wide_rows[pl.ds(table[i + GROUPS // 2, k], 1), :]
            own[pl.ds(start + k, 1), :] = jnp.where(low_lane, first, second)

    def weigh(i, carry):
        def weights(at):
            row = table_vector[pl.ds(at, 1), :] & (ROWS - 1)
            shared = ((row < PLANE) | (row == CORNERS)) & (space > 0)
            return jnp.broadcast_to(jnp.where(shared | (row >= CORNERS + 5), 0.0, 1.0), (HALF, LANES))

        both = jnp.concatenate([weights(i), weights(i + GROUPS // 2)], axis=0)
        weight[pl.ds(pl.multiple_of(i * LANES, LANES), LANES), :] = both.T
        return carry

    half = PAIRS // 2
    size = half // PIECES

    def piece_rows(side, p):
        return pl.ds(pl.multiple_of(side * half + p * size, size), size)

    to_mate, to_across = {"band": mate}, {"band": across}
    pieces = range(PIECES)
    first = [
        send(own.at[piece_rows(chip, p)], cross.at[piece_rows(chip, p)], first_sems, p, to_across) for p in pieces
    ]
    second = [
        send(own.at[piece_rows(1 - chip, p)], cross.at[piece_rows(1 - chip, p)], second_sems, p, to_across)
        for p in pieces
    ]
    forward_first = [
        send(cross.at[piece_rows(1 - chip, p)], partner_cross.at[piece_rows(1 - chip, p)], forward_sems, p, to_mate)
        for p in pieces
    ]
    forward_second = [
        send(cross.at[piece_rows(chip, p)], partner_cross.at[piece_rows(chip, p)], again_sems, p, to_mate)
        for p in pieces
    ]
    halves = [pl.ds(pl.multiple_of(side * half, half), half) for side in (chip, 1 - chip)]
    pair = [send(own.at[rows], partner.at[rows], pair_sems, k, to_mate) for k, rows in enumerate(halves)]

    groups = GROUPS // 4
    per_piece = groups // PIECES
    pl.semaphore_wait(barrier, len(peers))
    for p in pieces:
        base = chip * groups + p * per_piece
        lax.fori_loop(0, per_piece, lambda i, carry, base=base: (gather(base + i), carry)[1], 0)
        first[p].start()
    for p in pieces:
        base = (1 - chip) * groups + p * per_piece
        lax.fori_loop(0, per_piece, lambda i, carry, base=base: (gather(base + i), carry)[1], 0)
        if p == 0:
            second[0].start()
            pair[0].start()
    pair[1].start()
    lax.fori_loop(0, GROUPS // 2, weigh, 0)

    def products(left, right):
        both = lax.dot_general(
            jnp.concatenate(split(left), axis=1),
            jnp.concatenate(split(right), axis=1),
            (((0,), (0,)), ((), ())),
            preferred_element_type=jnp.float32,
        )
        upper = both[:LANES, : 2 * LANES] + both[:LANES, 2 * LANES :]
        return upper + (both[LANES:, : 2 * LANES] + both[LANES:, 2 * LANES :])

    def block_rows(i):
        return pl.ds(pl.multiple_of(i * BLOCK, BLOCK), BLOCK)

    def own_terms(i, total):
        rows = block_rows(i)
        mine = own[rows, :]
        scale = weight[rows, :]
        return total + products(mine * scale, jnp.concatenate([mine, partner[rows, :]], axis=1))

    def cross_terms(i, total):
        rows = block_rows(i)
        scale = weight[rows, :]
        return total + products(
            cross[rows, :], jnp.concatenate([own[rows, :] * scale, partner[rows, :] * scale], axis=1)
        )

    low_half = lax.broadcasted_iota(jnp.int32, (BANDS_DEV, LANES), 1) < HALF

    def fold(total):
        size = BANDS_DEV
        left = total[:size, :LANES] + pltpu.roll(total[size:, :LANES], HALF, 1)
        right = pltpu.roll(total[:size, LANES:], HALF, 1) + total[size:, LANES:]
        return jnp.where(low_half, left, right)

    zero = jnp.zeros((LANES, 2 * LANES), jnp.float32)
    per_half = half // BLOCK
    total = zero
    for k, side in enumerate((chip, 1 - chip)):
        pair[k].wait()
        total = lax.fori_loop(
            0, per_half, lambda i, total, side=side: own_terms(side * per_half + i, total), total
        )
    sums[0:BANDS_DEV, :] = fold(total)
    blocks = size // BLOCK
    total = zero
    for p in pieces:
        first[p].wait()
        forward_first[p].start()
        base = (1 - chip) * (half // BLOCK) + p * blocks
        total = lax.fori_loop(0, blocks, lambda i, total, base=base: cross_terms(base + i, total), total)
    sums[BANDS_DEV : 2 * BANDS_DEV, :] = fold(total)


    def rows_of(at):
        return pl.ds(pl.multiple_of(8 * at, 8), 8)

    others = range(1, PLANE_PEERS)
    scatter = [
        send(sums.at[rows_of(lax.rem(at_plane + k, PLANE_PEERS))], by_plane.at[k - 1], plane_sems, k - 1, plane_peer(k))
        for k in others
    ]
    for step in scatter:
        step.start()
    for step in scatter:
        step.wait()
    mine = sums[rows_of(at_plane), :]
    for k in others:
        mine = mine + by_plane[k - 1]
    piece[...] = mine
    to_z = send(piece, by_z, z_sems, 0, z_peer)
    to_z.start()
    to_z.wait()
    everyone[at_plane, band] = piece[...] + by_z[...]
    to_band = [
        send(everyone.at[at_plane, band], everyone.at[at_plane, band], band_sems, k, peer)
        for k, peer in enumerate(band_peers)
    ]
    for step in to_band:
        step.start()
    for p in pieces[1:]:
        second[p].start()
    for step in to_band:
        step.wait()
    back = [send(everyone.at[at_plane], everyone.at[at_plane], back_sems, k - 1, plane_peer(k)) for k in others]
    for step in back:
        step.start()
    for step in back:
        step.wait()

    totals = [
        jnp.concatenate([everyone[q, b] for q in range(PLANE_PEERS)], axis=0) * (1.0 / owned) for b in range(N_BAND)
    ]

    def part(b, r, c):
        size = BANDS_DEV
        return totals[b][r * size : (r + 1) * size, c * size : (c + 1) * size]

    margin = {(b, b): part(b, 0, 0) for b in range(N_BAND)}
    margin[1, 0], margin[3, 2] = part(1, 0, 1), part(3, 0, 1)
    margin[2, 0] = part(0, 1, 0) + part(2, 1, 0).T
    margin[2, 1] = part(0, 1, 1) + part(3, 1, 1).T
    margin[3, 0] = part(1, 1, 1) + part(2, 1, 1).T
    margin[3, 1] = part(1, 1, 0) + part(3, 1, 0).T

    inverses, factor, whole = [], {}, {}
    for k in range(N_BAND):
        diagonal = inverse_of_block(margin[k, k])
        inverses.append(diagonal)
        for i in range(k + 1, N_BAND):
            factor[i, k] = exact_dot_t(margin[i, k], diagonal)
        for i in range(k + 1, N_BAND):
            for j in range(k + 1, i + 1):
                margin[i, j] = margin[i, j] - exact_dot_t(factor[i, k], factor[j, k])
        whole[k, k] = diagonal
        for j in range(k):
            total = exact_dot(factor[k, j], whole[j, j])
            for m in range(j + 1, k):
                total = total + exact_dot(factor[k, m], whole[m, j])
            whole[k, j] = -exact_dot(diagonal, total)
        if k == 2:
            second[0].wait()
            forward_second[0].start()
    padding = jnp.zeros((BANDS_DEV, LANES - BANDS_DEV), jnp.float32)
    for i in range(N_BAND):
        for j in range(N_BAND):
            if j <= i:
                inverse[i, j] = jnp.concatenate([whole[i, j], padding], axis=1)
            else:
                inverse[i, j] = jnp.zeros((BANDS_DEV, LANES), jnp.float32)
    panels = [inverse[band, source] for source in (band, mate, across, across_mate)]
    left = jnp.concatenate(
        [
            jnp.concatenate(panels, axis=1),
            jnp.concatenate([pltpu.roll(panel, HALF, 1) for panel in panels], axis=1),
        ],
        axis=0,
    )
    left_high, left_low = split(left)
    left = jnp.concatenate(
        [jnp.concatenate([left_high, left_high], axis=1), jnp.concatenate([left_low, left_low], axis=1)], axis=0
    )

    def rotate(i, carry):
        rows = block_rows(i)
        right = jnp.concatenate([ref[rows, :] for ref in (own, partner, cross, partner_cross)], axis=1)
        both = lax.dot_general(
            left,
            jnp.concatenate(split(right), axis=1),
            (((1,), (1,)), ((), ())),
            preferred_element_type=jnp.float32,
        )
        rotated = both[: 2 * BANDS_DEV] + both[2 * BANDS_DEV :]
        out[:, rows] = rotated[:BANDS_DEV]
        out[:, pl.ds(pl.multiple_of(PAIRS + i * BLOCK, BLOCK), BLOCK)] = rotated[BANDS_DEV:]
        return carry

    def rotate_piece(side, p):
        base = side * per_half + p * blocks
        lax.fori_loop(0, blocks, lambda i, carry: rotate(base + i, carry), 0)

    for p in pieces:
        forward_first[p].wait()
        rotate_piece(1 - chip, p)
        if p > 0:
            second[p].wait()
            forward_second[p].start()
    for p in pieces:
        forward_second[p].wait()
        rotate_piece(chip, p)


def finish(cells, table, owned_count):
    whole = pl.BlockSpec(memory_space=pltpu.VMEM)
    nodes = pltpu.VMEM((PAIRS, LANES), jnp.float32)

    def small(*shape):
        return pltpu.VMEM(shape, jnp.float32)

    def sems(slots):
        return pltpu.SemaphoreType.DMA((2, slots))

    return pl.pallas_call(
        functools.partial(finish_kernel, owned_count),
        out_shape=jax.ShapeDtypeStruct((BANDS_DEV, 2 * PAIRS), jnp.float32),
        in_specs=[pl.BlockSpec(memory_space=pltpu.MemorySpace.HBM), whole],
        out_specs=whole,
        scratch_shapes=[
            pltpu.SMEM(table.shape, jnp.int32),
            small(TILES, ROWS, LANES),
            small(2 * TILES * ROWS, LANES),
            nodes, nodes, nodes, nodes, nodes,
            small(LANES, LANES), small(PLANE_PEERS - 1, 8, LANES), small(8, LANES), small(8, LANES),
            small(PLANE_PEERS, N_BAND, 8, LANES),
            small(N_BAND, N_BAND, BANDS_DEV, LANES),
            pltpu.SemaphoreType.DMA(()),
            pltpu.SemaphoreType.DMA((CELL_PARTS,)),
            sems(2), sems(PIECES), sems(PIECES), sems(PIECES), sems(PIECES),
            sems(PLANE_PEERS - 1), sems(1), sems(3), sems(PLANE_PEERS - 1),
        ],
        compiler_params=pltpu.CompilerParams(
            collective_id=1, has_side_effects=True, vmem_limit_bytes=48 * 2**20
        ),
        name="finish",
    )(cells, table)


def shards(
    wavefunctions, stiffness, cell_scale, cell_potential, connectivity, lower_face, upper_face
):
    node_count = wavefunctions.shape[1]
    face_count = lower_face.shape[0]
    space_count = lax.axis_size("space")
    owned_count = node_count * space_count - face_count * (space_count - 1)

    index, keys, scale, potential, stiff = make_layout(connectivity, cell_scale, cell_potential, stiffness)
    cells, table = filter_cells(index, keys, wavefunctions, stiff, scale, potential)
    return finish(cells, table, owned_count)[:, :node_count]


def solution(mesh):
    placed = (
        P("band", "space"),
        P(),
        P("space"),
        P("space"),
        P(None, "space"),
        P("space"),
        P("space"),
    )
    return jax.shard_map(
        shards, mesh=mesh, in_specs=placed, out_specs=P("band", "space"), check_vma=False
    )
```

```python
import functools

import jax
import jax.numpy as jnp
import numpy as np
from jax import lax
from jax.experimental import pallas as pl
from jax.experimental.pallas import tpu as pltpu
from jax.sharding import PartitionSpec as P

FILTER_DEG = 4
GLL_WEIGHTS = (0.1, 49.0 / 90.0, 32.0 / 45.0, 49.0 / 90.0, 0.1)
CENTER = 11.0
HALF_WIDTH = 9.0
HIGHEST = lax.Precision.HIGHEST
MESH = pl.DeviceIdType.MESH

CELLS_Y = 20
CELLS_Z = 6
CHUNKS = CELLS_Y // 2
TILES = CHUNKS * CELLS_Z
SLOTS = 2 * TILES
HALF = 64
LANES = 128
ROWS = 128
PLANE = 24
CORNERS = 5 * PLANE
MESSAGE = 2 * CELLS_Z + 1
EDGE = CELLS_Z + 1

NODES = 10125
PAIRS = 5120
BLOCK = 256
PIECES = 5
CELL_PARTS = 4
GROUPS = 2 * PAIRS // LANES
PLANE_PEERS = 16
BANDS_DEV = 64
N_BAND = 4


def row_of_node(a, b, c):
    if (b, c) == (4, 4):
        return CORNERS + a
    rows = {(0, 0): 0, (4, 0): 8, (0, 4): 16, (1, 1): 7, (1, 2): 15, (1, 3): 23}
    for k in (1, 2, 3):
        rows[(0, k)] = k
        rows[(4, k)] = 8 + k
        rows[(k, 0)] = 3 + k
        rows[(k, 4)] = 16 + 3 + k
        rows[(2, k)] = 8 + 3 + k
        rows[(3, k)] = 16 + k
    return PLANE * a + rows[(b, c)]


def node_rows(planes, chosen):
    return [
        (25 * a + 5 * b + c, row_of_node(a, b, c))
        for a in planes for b in range(5) for c in range(5) if chosen(b, c)
    ]


LOCAL_ROWS = [row for _, row in node_rows(range(5), lambda b, c: True)]


def owners():
    owned = np.zeros((LANES, SLOTS), np.float32)
    for slot in range(SLOTS):
        tile, half = divmod(slot, 2)
        last_y = half == 1 and tile >= TILES - CELLS_Z
        last_z = tile % CELLS_Z == CELLS_Z - 1
        for node, _ in node_rows(range(5), lambda b, c: (b < 4 or last_y) and (c < 4 or last_z)):
            owned[node, slot] = 1.0
    return owned


def place_codes():
    codes = np.zeros((LANES, LANES), np.float32)
    codes[:125, :] = 2.0 * np.array(LOCAL_ROWS)[:, None] + np.arange(LANES)[None, :] % 2
    return codes


def row_selector():
    chosen = np.zeros((ROWS, 125), np.float32)
    chosen[LOCAL_ROWS, np.arange(125)] = 1.0
    return chosen


def row_mass():
    weights = np.array(GLL_WEIGHTS, np.float32)
    mass = (weights[:, None, None] * weights[None, :, None] * weights[None, None, :]).reshape(-1)
    spread = np.zeros((ROWS, LANES), np.float32)
    spread[LOCAL_ROWS, :] = mass[:, None]
    return spread


def local(a, b, c):
    return 25 * a + 5 * b + c


def exact_dot(x, y):
    return jnp.dot(x, y, precision=HIGHEST, preferred_element_type=jnp.float32)


def chain_counts(before, doublings):
    size = before.shape[0]
    eye = (
        lax.broadcasted_iota(jnp.int32, (size, size), 0) == lax.broadcasted_iota(jnp.int32, (size, size), 1)
    ).astype(jnp.float32)
    total, power = eye + before, before
    for _ in range(doublings):
        power = jnp.dot(power, power, preferred_element_type=jnp.float32)
        total = total + jnp.dot(total, power, preferred_element_type=jnp.float32)
    return jnp.sum(total, axis=0, keepdims=True) - 1.0


def layout_kernel(
    conn_ref, cell_scale_ref, cell_potential_ref, stiff_ref, select_ref, owned_ref,
    index_ref, keys_ref, scale_ref, potential_ref, stiffness_ref,
):
    conn = conn_ref[...].astype(jnp.float32)
    cells = conn.shape[1]
    on_rows = lax.broadcasted_iota(jnp.int32, (cells, cells), 0)
    on_lanes = lax.broadcasted_iota(jnp.int32, (cells, cells), 1)

    def as_column(row):
        return jnp.sum(jnp.where(on_rows == on_lanes, row, 0.0), axis=1, keepdims=True)

    def row_of(node):
        return conn[node : node + 1, :]

    after_z = (as_column(row_of(local(2, 2, 4))) == row_of(local(2, 2, 0))).astype(jnp.float32)
    after_y = (as_column(row_of(local(2, 4, 2))) == row_of(local(2, 0, 2))).astype(jnp.float32)
    at_z = chain_counts(after_z, 2)
    at_y = chain_counts(after_y, 4)
    upper_half = at_y >= CHUNKS
    tile = (at_y - jnp.where(upper_half, 1.0 * CHUNKS, 0.0)) * CELLS_Z + at_z
    slot = 2.0 * tile + jnp.where(upper_half, 1.0, 0.0)
    moved = (as_column(slot) == on_lanes.astype(jnp.float32)).astype(jnp.float32)
    index = (exact_dot(conn, moved) + 0.5).astype(jnp.int32)
    index_ref[...] = index
    index = jnp.concatenate([index, jnp.zeros((LANES - index.shape[0], cells), jnp.int32)], axis=0)
    keys = jnp.where(owned_ref[...] > 0.5, index, -1)
    keys_ref[...] = jnp.concatenate([keys, jnp.full((LANES, LANES - cells), -1, jnp.int32)], axis=1)

    wanted = lax.broadcasted_iota(jnp.int32, (TILES, cells), 0).astype(jnp.float32)
    lane = lax.broadcasted_iota(jnp.int32, (TILES, LANES), 1)

    def spread(row):
        low, high = [
            jnp.sum(jnp.where(slot == 2.0 * wanted + half, row, 0.0), axis=1, keepdims=True) for half in (0.0, 1.0)
        ]
        return jnp.where(lane < HALF, low, high)

    scale_ref[...] = spread(cell_scale_ref[...])
    potential_ref[...] = spread(cell_potential_ref[...])

    select = select_ref[...]
    part = exact_dot(select, stiff_ref[...])
    stiff = lax.dot_general(
        part, select, (((1,), (1,)), ((), ())), precision=HIGHEST, preferred_element_type=jnp.float32
    )
    high = stiff.astype(jnp.bfloat16)
    low = (stiff - high.astype(jnp.float32)).astype(jnp.bfloat16)
    stiffness_ref[...] = jnp.concatenate(
        [jnp.concatenate([high, high], axis=1), jnp.concatenate([low, low], axis=1)], axis=0
    )


def make_layout(connectivity, cell_scale, cell_potential, stiffness):
    cells = connectivity.shape[1]
    whole = pl.BlockSpec(memory_space=pltpu.VMEM)
    return pl.pallas_call(
        layout_kernel,
        out_shape=(
            jax.ShapeDtypeStruct((125, cells), jnp.int32),
            jax.ShapeDtypeStruct((LANES, LANES), jnp.int32),
            jax.ShapeDtypeStruct((TILES, LANES), jnp.float32),
            jax.ShapeDtypeStruct((TILES, LANES), jnp.float32),
            jax.ShapeDtypeStruct((2 * ROWS, 2 * ROWS), jnp.bfloat16),
        ),
        in_specs=[whole] * 6,
        out_specs=(whole,) * 5,
        name="layout",
    )(connectivity, cell_scale[None, :], cell_potential[None, :], stiffness, row_selector(), owners())


def each_node_once(planes, visit):
    def loop(count, tile_of, nodes, halves=(0, 1)):
        def body(i, carry):
            visit(tile_of(i), nodes, halves)
            return carry

        lax.fori_loop(0, count, body, 0)

    loop(TILES, lambda i: i, node_rows(planes, lambda b, c: b < 4 and c < 4))
    loop(CELLS_Z, lambda i: TILES - CELLS_Z + i, node_rows(planes, lambda b, c: b == 4 and c < 4), (1,))
    loop(1, lambda i: TILES - 1, node_rows(planes, lambda b, c: b == 4 and c == 4), (1,))
    loop(CHUNKS, lambda i: i * CELLS_Z + CELLS_Z - 1, node_rows(planes, lambda b, c: b < 4 and c == 4))


def filter_kernel(
    index_vector_ref, keys_ref, codes_ref, waves_ref, stiff_ref, mass_ref, scale_ref, potential_ref, out_ref, table_ref,
    index_ref, places, other, product, face, doubled, sends, edge_sends, receives, edge_receives,
    send_sems, receive_sems, edge_send_sems, edge_receive_sems, index_sem,
):
    count = lax.axis_size("space")
    me = lax.axis_index("space")
    above, below = lax.rem(me + 1, count), lax.rem(me + count - 1, count)
    has_below, has_above = me > 0, me < count - 1

    barrier = pltpu.get_barrier_semaphore()
    for neighbour in (below, above):
        pl.semaphore_signal(barrier, inc=1, device_id={"space": neighbour}, device_id_type=MESH)
    pl.semaphore_wait(barrier, 2)

    sub = lax.broadcasted_iota(jnp.int32, (8, LANES), 0)
    lane = lax.broadcasted_iota(jnp.int32, (8, LANES), 1)
    corner = sub == 0
    along_y = sub <= 3
    along_z = corner | ((sub >= 4) & (sub <= 6))
    in_y_group = (sub >= 4) & (sub <= 6)
    in_z_group = ((sub >= 1) & (sub <= 3)) | (sub == 7)
    low_half = lane < HALF
    corners = slice(CORNERS, CORNERS + 8)
    last_tile = TILES - 1
    bottom, top = 0, 4
    inner = (1, 2, 3)

    def group(a, g):
        return slice(PLANE * a + 8 * g, PLANE * a + 8 * g + 8)

    def turn(value, by):
        return pltpu.roll(value, by % 8, 0) if by % 8 else value

    def over_chunks(body):
        def step(c, carry):
            body(c)
            return carry

        lax.fori_loop(0, CHUNKS, step, 0)

    def message(step, way, c):
        return pltpu.make_async_remote_copy(
            src_ref=sends.at[way, c],
            dst_ref=receives.at[step, way, c],
            send_sem=send_sems.at[step, way, c],
            recv_sem=receive_sems.at[step, way, c],
            device_id={"space": above if way == 0 else below},
            device_id_type=MESH,
        )

    def edge_message(step, way):
        return pltpu.make_async_remote_copy(
            src_ref=edge_sends.at[way],
            dst_ref=edge_receives.at[step, way],
            send_sem=edge_send_sems.at[step, way],
            recv_sem=edge_receive_sems.at[step, way],
            device_id={"space": above if way == 0 else below},
            device_id_type=MESH,
        )

    def start(copy, way):
        @pl.when(has_above if way == 0 else has_below)
        def _():
            copy.start()

    def finish_copy(copy, way):
        @pl.when(has_above if way == 0 else has_below)
        def _():
            copy.wait_send()

        @pl.when(has_below if way == 0 else has_above)
        def _():
            copy.wait_recv()

    def send_chunk(step, way, c, tiles, ends):
        for z, (own, y, d) in enumerate(tiles):
            sends[way, c, 2 * z] = own
            sends[way, c, 2 * z + 1] = jnp.where(corner, turn(y, 1), jnp.where(in_y_group, y, d))
        sends[way, c, MESSAGE - 1] = tiles[CELLS_Z - 1][2]
        start(message(step, way, c), way)

        @pl.when(c == CHUNKS - 1)
        def _():
            for z in range(CELLS_Z):
                edge_sends[way, z] = tiles[z][1]
            edge_sends[way, EDGE - 1] = ends
            start(edge_message(step, way), way)

    def unpack(step, way, c, z):
        inside = receives[step, way, c, 2 * z + 1]
        y = jnp.where(in_y_group, inside, jnp.where(sub == 7, turn(inside, 7), 0.0))
        d = jnp.where(in_z_group, inside, receives[step, way, c, MESSAGE - 1])
        return [receives[step, way, c, 2 * z], y, d]

    def unpack_corner(step, way):
        return turn(edge_receives[step, way, EDGE - 1], 4)

    def fill(ref, c):
        @pl.when(c == CHUNKS - 1)
        def _():
            end = ref[last_tile, corners, :]
            for a in range(5):
                for z in range(CELLS_Z):
                    ref[TILES + z, group(a, 0), :] = jnp.where(
                        low_half, pltpu.roll(ref[z, group(a, 0), :], HALF, 1), ref[TILES - CELLS_Z + z, group(a, 1), :]
                    )
                ref[TILES + CELLS_Z - 1, group(a, 2), :] = jnp.where(
                    low_half, pltpu.roll(ref[CELLS_Z - 1, group(a, 2), :], HALF, 1), turn(end, -a)
                )

        first = c * CELLS_Z
        ends = [ref[first + z, corners, :] for z in range(CELLS_Z)]
        for a in range(5):
            y_new = [
                jnp.where(along_y, ref[first + CELLS_Z + z, group(a, 0), :], ref[first + z, group(a, 1), :])
                for z in range(CELLS_Z)
            ]
            for z in range(CELLS_Z):
                ref[first + z, group(a, 1), :] = y_new[z]
                if z < CELLS_Z - 1:
                    ref[first + z, group(a, 2), :] = jnp.where(
                        along_z, ref[first + z + 1, group(a, 0), :], ref[first + z, group(a, 2), :]
                    )
                    ahead = y_new[z + 1]
                else:
                    ahead = ref[first + CELLS_Z + z, group(a, 2), :]
                ends[z] = jnp.where(sub == a, turn(ahead, a), ends[z])
        for z in range(CELLS_Z):
            ref[first + z, corners, :] = ends[z]

    def assembled(c, a):
        tiles, corner_terms = [], []
        for z in range(CELLS_Z):
            t = c * CELLS_Z + z
            own, y, d = [product[t + CELLS_Z, group(a, g), :] for g in range(3)]
            own = own + jnp.where(along_y, product[t, group(a, 1), :], 0.0)
            d = d + jnp.where(corner, turn(product[t, corners, :], -a), 0.0)
            tiles.append([own, y, d])
            corner_terms.append(turn(product[t + CELLS_Z, corners, :], -a))
        for z in range(1, CELLS_Z):
            tiles[z][0] = tiles[z][0] + jnp.where(along_z, tiles[z - 1][2], 0.0)
            tiles[z][1] = tiles[z][1] + jnp.where(corner, corner_terms[z - 1], 0.0)
        return tiles

    def multiply(current, c):
        mass = mass_ref[...]
        for pair in range(CELLS_Z // 2):
            t = c * CELLS_Z + 2 * pair
            values = [current[t], current[t + 1]]
            high, low = split(jnp.concatenate(values, axis=1))
            result = jnp.dot(
                stiff_ref[...], jnp.concatenate([high, low], axis=0), preferred_element_type=jnp.float32
            )
            result = result[:ROWS] + result[ROWS:]
            for k in range(2):
                product[t + CELLS_Z + k] = result[:, k * LANES : (k + 1) * LANES] * scale_ref[
                    pl.ds(t + k, 1), :
                ] + mass * potential_ref[pl.ds(t + k, 1), :] * values[k]

        @pl.when(c == CHUNKS - 1)
        def _():
            for z in range(CELLS_Z):
                for rows in [group(a, 1) for a in range(5)] + [corners]:
                    turned = pltpu.roll(product[TILES + z, rows, :], HALF, 1)
                    product[z, rows, :] = jnp.where(low_half, 0.0, turned)

    def buffers(step):
        return (out_ref, other) if step % 2 == 0 else (other, out_ref)

    def factor(step):
        return (1.0 if step == 0 else 2.0) / HALF_WIDTH

    def advance(step, t, rows, total):
        current, previous = buffers(step)
        value = (total - CENTER * current[t, rows, :]) * factor(step)
        previous[t, rows, :] = value if step == 0 else value - previous[t, rows, :]

    def assemble(step, c):
        ends = product[TILES + CELLS_Z - 1, corners, :]
        for way, a in ((0, top), (1, bottom)):
            tiles = assembled(c, a)
            for z in range(CELLS_Z):
                for g in range(3):
                    face[way, c * CELLS_Z + z, 8 * g : 8 * g + 8, :] = tiles[z][g]
            send_chunk(step + 1, way, c, tiles, ends)
        for a in inner:
            tiles = assembled(c, a)
            for z in range(CELLS_Z):
                for g in range(3):
                    advance(step, c * CELLS_Z + z, group(a, g), tiles[z][g])

    def advance_faces(step, c):
        for way, a, valid in ((0, bottom, has_below), (1, top, has_above)):
            finish_copy(message(step + 1, way, c), way)
            for z in range(CELLS_Z):
                t = c * CELLS_Z + z
                arrived = unpack(step + 1, way, c, z)
                for g in range(3):
                    total = face[1 - way, t, 8 * g : 8 * g + 8, :] + jnp.where(valid, arrived[g], 0.0)
                    advance(step, t, group(a, g), total)

        @pl.when(c == CHUNKS - 1)
        def _():
            previous = buffers(step)[1]
            ends = product[TILES + CELLS_Z - 1, corners, :]
            for way, a, valid in ((0, bottom, has_below), (1, top, has_above)):
                finish_copy(edge_message(step + 1, way), way)
                for z in range(CELLS_Z):
                    rows = group(a, 1)
                    edge = jnp.where(along_y & valid, edge_receives[step + 1, way, z], 0.0)
                    previous[TILES - CELLS_Z + z, rows, :] = previous[TILES - CELLS_Z + z, rows, :] + factor(step) * edge
                ends = ends + jnp.where((sub == a) & valid, unpack_corner(step + 1, way), 0.0)
            advance(step, last_tile, corners, ends)

    def tabulate(step):
        high = lax.broadcasted_iota(jnp.int32, (GROUPS, LANES), 0)
        low = lax.broadcasted_iota(jnp.int32, (LANES, LANES), 0)
        tile = (lax.broadcasted_iota(jnp.int32, (1, LANES), 1) // 2).astype(jnp.float32)

        def body(i, total):
            left, right = [], []
            for k in range(2):
                at = pl.ds(2 * i + k, 1)
                key = keys_ref[at, :]
                left.append(jnp.where(high == key >> 7, 1.0, 0.0).astype(jnp.bfloat16))
                hit = low == key & (LANES - 1)
                values = [jnp.where(hit, tile, 0.0), jnp.where(hit, codes_ref[at, :], 0.0)]
                right.append(jnp.concatenate(values, axis=0).astype(jnp.bfloat16))
            return total + lax.dot_general(
                jnp.concatenate(left, axis=1),
                jnp.concatenate(right, axis=1),
                (((1,), (1,)), ((), ())),
                preferred_element_type=jnp.float32,
            )

        part = LANES // 2 // FILTER_DEG
        total = jnp.zeros((GROUPS, 2 * LANES), jnp.float32) if step == 0 else places[...]
        total = lax.fori_loop(part * step, part * (step + 1), body, total)
        if step < FILTER_DEG - 1:
            places[...] = total
            return
        total = total + 0.5
        tiles = total[:, :LANES].astype(jnp.int32)
        codes = total[:, LANES:].astype(jnp.int32)
        node = high * LANES + lax.broadcasted_iota(jnp.int32, (GROUPS, LANES), 1)
        place = (codes & 1) * (TILES * ROWS) + tiles * ROWS + (codes >> 1)
        table_ref[...] = jnp.where(node < NODES, place, CORNERS + 5)

    index_copy = pltpu.make_async_copy(index_vector_ref, index_ref, index_sem)
    index_copy.start()
    node_count = waves_ref.shape[1]
    whole_blocks = node_count // LANES

    def transpose(i, carry):
        at = pl.ds(pl.multiple_of(i * LANES, LANES), LANES)
        block = waves_ref[:, at]
        doubled[at, :] = jnp.concatenate([block, block], axis=0).T
        return carry

    lax.fori_loop(0, whole_blocks, transpose, 0)
    rest = node_count - whole_blocks * LANES
    block = jnp.concatenate(
        [waves_ref[:, whole_blocks * LANES :], jnp.zeros((HALF, LANES - rest), jnp.float32)], axis=1
    )
    doubled[whole_blocks * LANES : (whole_blocks + 1) * LANES, :] = jnp.concatenate([block, block], axis=0).T

    unused = jnp.zeros((TILES + CELLS_Z, ROWS - CORNERS, LANES), jnp.float32)
    out_ref[:, CORNERS:, :] = unused
    other[:, CORNERS:, :] = unused
    low_row = lax.broadcasted_iota(jnp.int32, (1, LANES), 1) < HALF

    def gather(t, nodes, halves):
        for node, row in nodes:
            first = doubled[pl.ds(index_ref[node, 2 * t], 1), :]
            second = doubled[pl.ds(index_ref[node, 2 * t + 1], 1), :]
            out_ref[t, row : row + 1, :] = jnp.where(low_row, first, second)

    index_copy.wait()
    each_node_once((top,), gather)

    def send_owner(c):
        tiles = [[out_ref[c * CELLS_Z + z, group(top, g), :] for g in range(3)] for z in range(CELLS_Z)]
        send_chunk(0, 0, c, tiles, out_ref[last_tile, corners, :])

    over_chunks(send_owner)
    each_node_once((0, 1, 2, 3), gather)

    def take_owner(c):
        finish_copy(message(0, 0, c), 0)
        for z in range(CELLS_Z):
            t = c * CELLS_Z + z
            arrived = unpack(0, 0, c, z)
            for g in range(3):
                out_ref[t, group(bottom, g), :] = jnp.where(has_below, arrived[g], out_ref[t, group(bottom, g), :])

        @pl.when(c == CHUNKS - 1)
        def _():
            finish_copy(edge_message(0, 0), 0)
            for z in range(CELLS_Z):
                t = TILES - CELLS_Z + z
                out_ref[t, group(bottom, 1), :] = jnp.where(
                    along_y & has_below, edge_receives[0, 0, z], out_ref[t, group(bottom, 1), :]
                )
            out_ref[last_tile, corners, :] = jnp.where(
                (sub == bottom) & has_below, unpack_corner(0, 0), out_ref[last_tile, corners, :]
            )

    for step in range(FILTER_DEG):
        current = buffers(step)[0]

        def arrive(c):
            if step == 0:
                take_owner(c)
            else:
                advance_faces(step - 1, c)

        def refresh(c):
            fill(current, c)
            multiply(current, c)

        def next_chunk(i, carry):
            arrive(lax.rem(step + i, CHUNKS))
            c = lax.rem(step + i - 1, CHUNKS)
            refresh(c)
            assemble(step, c)
            return carry

        arrive(step)
        arrive(step + 1)
        refresh(step)
        lax.fori_loop(2, CHUNKS, next_chunk, 0)
        refresh((step + CHUNKS - 1) % CHUNKS)
        assemble(step, (step + CHUNKS - 1) % CHUNKS)
        assemble(step, step)
        tabulate(step)

    last = FILTER_DEG
    lax.fori_loop(
        0, CHUNKS, lambda i, carry: (advance_faces(last - 1, lax.rem(last + i, CHUNKS)), carry)[1], 0
    )


def filter_cells(index, keys, wavefunctions, stiff, scale, potential):
    whole = pl.BlockSpec(memory_space=pltpu.VMEM)
    cells = (TILES + CELLS_Z, ROWS, LANES)
    rounds = FILTER_DEG + 1
    blocks = wavefunctions.shape[1] // LANES + 1
    return pl.pallas_call(
        filter_kernel,
        out_shape=(
            jax.ShapeDtypeStruct(cells, jnp.float32), jax.ShapeDtypeStruct((GROUPS, LANES), jnp.int32)
        ),
        in_specs=[whole] * 8,
        out_specs=(whole, whole),
        scratch_shapes=[
            pltpu.SMEM(index.shape, jnp.int32),
            pltpu.VMEM((GROUPS, 2 * LANES), jnp.float32),
            pltpu.VMEM(cells, jnp.float32),
            pltpu.VMEM(cells, jnp.float32),
            pltpu.VMEM((2, TILES, PLANE, LANES), jnp.float32),
            pltpu.VMEM((blocks * LANES, LANES), jnp.float32),
            pltpu.VMEM((2, CHUNKS, MESSAGE, 8, LANES), jnp.float32),
            pltpu.VMEM((2, EDGE, 8, LANES), jnp.float32),
            pltpu.VMEM((rounds, 2, CHUNKS, MESSAGE, 8, LANES), jnp.float32),
            pltpu.VMEM((rounds, 2, EDGE, 8, LANES), jnp.float32),
            pltpu.SemaphoreType.DMA((rounds, 2, CHUNKS)),
            pltpu.SemaphoreType.DMA((rounds, 2, CHUNKS)),
            pltpu.SemaphoreType.DMA((rounds, 2)),
            pltpu.SemaphoreType.DMA((rounds, 2)),
            pltpu.SemaphoreType.DMA(()),
        ],
        compiler_params=pltpu.CompilerParams(
            collective_id=0, has_side_effects=True, vmem_limit_bytes=56 * 2**20
        ),
        name="filter_cells",
    )(index, keys, place_codes(), wavefunctions, stiff, row_mass(), scale, potential)


def split(x):
    high = x.astype(jnp.bfloat16)
    return high, (x - high.astype(jnp.float32)).astype(jnp.bfloat16)


def exact_dot_t(x, y):
    return lax.dot_general(
        x, y, (((1,), (1,)), ((), ())), precision=HIGHEST, preferred_element_type=jnp.float32
    )


def inverse_of_block(block):
    size = BANDS_DEV
    row_at = lax.broadcasted_iota(jnp.int32, (size, LANES), 0)
    lane = lax.broadcasted_iota(jnp.int32, (size, LANES), 1)
    wide = jnp.concatenate([block, jnp.zeros((size, LANES - size), jnp.float32)], axis=1)
    wide = jnp.where(lane == row_at + size, 1.0, wide)
    tiles = [wide[8 * g : 8 * g + 8] for g in range(size // 8)]
    sub = lax.broadcasted_iota(jnp.int32, (8, LANES), 0)
    for home in range(size // 8):
        live = range(home, size // 8)
        columns = {
            (g, n): jnp.broadcast_to(tiles[g][:, 8 * home + n : 8 * home + n + 1], (8, LANES))
            for g in live for n in range(8)
        }
        for at in range(8):
            scale = 1.0 / columns[home, at][at : at + 1, :]
            ratio = tiles[home][at : at + 1, :] * scale
            ahead = {n: columns[home, n][at : at + 1, :] * scale for n in range(at + 1, 8)}
            for g in live:
                factor = columns[g, at]
                if g == home:
                    factor = jnp.where(sub > at, factor, 0.0)
                for n in range(at + 1, 8):
                    columns[g, n] = columns[g, n] - factor * ahead[n]
                tiles[g] = tiles[g] - factor * ratio
    wide = jnp.concatenate(tiles, axis=0)
    pivots = jnp.sum(jnp.where(lane == row_at, wide, 0.0), axis=1, keepdims=True)
    return wide[:, size:] * (1.0 / jnp.sqrt(pivots))


def finish_kernel(
    owned, far_cells, table_vector, out, table, cells, wide_rows, own, weight, partner, cross, partner_cross,
    sums, by_plane, piece, by_z, everyone, inverse,
    table_sem, cell_sems, pair_sems, first_sems, second_sems, forward_sems, again_sems, plane_sems, z_sems, band_sems, back_sems,
):
    table_copy = pltpu.make_async_copy(table_vector, table, table_sem)
    table_copy.start()
    part = TILES // CELL_PARTS
    cell_copies = [
        pltpu.make_async_copy(far_cells.at[pl.ds(p * part, part)], cells.at[pl.ds(p * part, part)], cell_sems.at[p])
        for p in range(CELL_PARTS)
    ]
    for step in cell_copies:
        step.start()
    space, band = lax.axis_index("space"), lax.axis_index("band")
    at_plane = lax.rem(space, PLANE_PEERS)
    core = lax.rem(band, 2)
    chip = band // 2
    mate = band + 1 - 2 * core
    across = lax.rem(band + 2, N_BAND)
    across_mate = lax.rem(mate + 2, N_BAND)

    def plane_peer(k):
        return {"space": space - at_plane + lax.rem(at_plane + k, PLANE_PEERS)}

    z_peer = {"space": lax.rem(space + PLANE_PEERS, 2 * PLANE_PEERS)}
    band_peers = [{"band": lax.rem(band + k, N_BAND)} for k in (1, 2, 3)]
    barrier = pltpu.get_barrier_semaphore()
    peers = [plane_peer(k) for k in range(1, PLANE_PEERS)] + [z_peer] + band_peers
    for peer in peers:
        pl.semaphore_signal(barrier, inc=1, device_id=peer, device_id_type=MESH)

    def send(source, target, sems, slot, peer):
        return pltpu.make_async_remote_copy(
            src_ref=source,
            dst_ref=target,
            send_sem=sems.at[0, slot],
            recv_sem=sems.at[1, slot],
            device_id=peer,
            device_id_type=MESH,
        )

    left_half = lax.broadcasted_iota(jnp.int32, (ROWS, LANES), 1) < HALF

    def widen(t, carry):
        values = cells[t]
        turned = pltpu.roll(values, HALF, 1)
        for slot, (left, right) in enumerate(((values, turned), (turned, values))):
            rows = pl.ds(pl.multiple_of((slot * TILES + t) * ROWS, ROWS), ROWS)
            wide_rows[rows, :] = jnp.where(left_half, left, right)
        return carry

    for p in range(CELL_PARTS):
        cell_copies[p].wait()
        lax.fori_loop(p * part, (p + 1) * part, widen, 0)
    table_copy.wait()
    low_lane = lax.broadcasted_iota(jnp.int32, (1, LANES), 1) < HALF

    def gather(i):
        start = pl.multiple_of(i * LANES, LANES)
        for k in range(LANES):
            first = wide_rows[pl.ds(table[i, k], 1), :]
            second = wide_rows[pl.ds(table[i + GROUPS // 2, k], 1), :]
            own[pl.ds(start + k, 1), :] = jnp.where(low_lane, first, second)

    def weigh(i, carry):
        def weights(at):
            row = table_vector[pl.ds(at, 1), :] & (ROWS - 1)
            shared = ((row < PLANE) | (row == CORNERS)) & (space > 0)
            return jnp.broadcast_to(jnp.where(shared | (row >= CORNERS + 5), 0.0, 1.0), (HALF, LANES))

        both = jnp.concatenate([weights(i), weights(i + GROUPS // 2)], axis=0)
        weight[pl.ds(pl.multiple_of(i * LANES, LANES), LANES), :] = both.T
        return carry

    half = PAIRS // 2
    size = half // PIECES

    def piece_rows(side, p):
        return pl.ds(pl.multiple_of(side * half + p * size, size), size)

    to_mate, to_across = {"band": mate}, {"band": across}
    pieces = range(PIECES)
    first = [
        send(own.at[piece_rows(chip, p)], cross.at[piece_rows(chip, p)], first_sems, p, to_across) for p in pieces
    ]
    second = [
        send(own.at[piece_rows(1 - chip, p)], cross.at[piece_rows(1 - chip, p)], second_sems, p, to_across)
        for p in pieces
    ]
    forward_first = [
        send(cross.at[piece_rows(1 - chip, p)], partner_cross.at[piece_rows(1 - chip, p)], forward_sems, p, to_mate)
        for p in pieces
    ]
    forward_second = [
        send(cross.at[piece_rows(chip, p)], partner_cross.at[piece_rows(chip, p)], again_sems, p, to_mate)
        for p in pieces
    ]
    halves = [pl.ds(pl.multiple_of(side * half, half), half) for side in (chip, 1 - chip)]
    pair = [send(own.at[rows], partner.at[rows], pair_sems, k, to_mate) for k, rows in enumerate(halves)]

    groups = GROUPS // 4
    per_piece = groups // PIECES
    pl.semaphore_wait(barrier, len(peers))
    for p in pieces:
        base = chip * groups + p * per_piece
        lax.fori_loop(0, per_piece, lambda i, carry, base=base: (gather(base + i), carry)[1], 0)
        first[p].start()
    for p in pieces:
        base = (1 - chip) * groups + p * per_piece
        lax.fori_loop(0, per_piece, lambda i, carry, base=base: (gather(base + i), carry)[1], 0)
        if p == 0:
            second[0].start()
            pair[0].start()
    pair[1].start()
    second[1].start()
    lax.fori_loop(0, GROUPS // 2, weigh, 0)

    def products(left, right):
        both = lax.dot_general(
            jnp.concatenate(split(left), axis=1),
            jnp.concatenate(split(right), axis=1),
            (((0,), (0,)), ((), ())),
            preferred_element_type=jnp.float32,
        )
        upper = both[:LANES, : 2 * LANES] + both[:LANES, 2 * LANES :]
        return upper + (both[LANES:, : 2 * LANES] + both[LANES:, 2 * LANES :])

    def block_rows(i):
        return pl.ds(pl.multiple_of(i * BLOCK, BLOCK), BLOCK)

    def own_terms(i, total):
        rows = block_rows(i)
        mine = own[rows, :]
        scale = weight[rows, :]
        return total + products(mine * scale, jnp.concatenate([mine, partner[rows, :]], axis=1))

    def cross_terms(i, total):
        rows = block_rows(i)
        scale = weight[rows, :]
        return total + products(
            cross[rows, :], jnp.concatenate([own[rows, :] * scale, partner[rows, :] * scale], axis=1)
        )

    low_half = lax.broadcasted_iota(jnp.int32, (BANDS_DEV, LANES), 1) < HALF

    def fold(total):
        size = BANDS_DEV
        left = total[:size, :LANES] + pltpu.roll(total[size:, :LANES], HALF, 1)
        right = pltpu.roll(total[:size, LANES:], HALF, 1) + total[size:, LANES:]
        return jnp.where(low_half, left, right)

    zero = jnp.zeros((LANES, 2 * LANES), jnp.float32)
    per_half = half // BLOCK
    total = zero
    for k, side in enumerate((chip, 1 - chip)):
        pair[k].wait()
        total = lax.fori_loop(
            0, per_half, lambda i, total, side=side: own_terms(side * per_half + i, total), total
        )
    sums[0:BANDS_DEV, :] = fold(total)
    blocks = size // BLOCK
    total = zero
    for p in pieces:
        first[p].wait()
        forward_first[p].start()
        base = (1 - chip) * (half // BLOCK) + p * blocks
        total = lax.fori_loop(0, blocks, lambda i, total, base=base: cross_terms(base + i, total), total)
    sums[BANDS_DEV : 2 * BANDS_DEV, :] = fold(total)


    def rows_of(at):
        return pl.ds(pl.multiple_of(8 * at, 8), 8)

    others = range(1, PLANE_PEERS)
    scatter = [
        send(sums.at[rows_of(lax.rem(at_plane + k, PLANE_PEERS))], by_plane.at[k - 1], plane_sems, k - 1, plane_peer(k))
        for k in others
    ]
    for step in scatter:
        step.start()
    for step in scatter:
        step.wait()
    mine = sums[rows_of(at_plane), :]
    for k in others:
        mine = mine + by_plane[k - 1]
    piece[...] = mine
    to_z = send(piece, by_z, z_sems, 0, z_peer)
    to_z.start()
    to_z.wait()
    everyone[at_plane, band] = piece[...] + by_z[...]
    to_band = [
        send(everyone.at[at_plane, band], everyone.at[at_plane, band], band_sems, k, peer)
        for k, peer in enumerate(band_peers)
    ]
    for step in to_band:
        step.start()
    for p in pieces[2:]:
        second[p].start()
    for step in to_band:
        step.wait()
    back = [send(everyone.at[at_plane], everyone.at[at_plane], back_sems, k - 1, plane_peer(k)) for k in others]
    for step in back:
        step.start()
    for step in back:
        step.wait()

    totals = [
        jnp.concatenate([everyone[q, b] for q in range(PLANE_PEERS)], axis=0) * (1.0 / owned) for b in range(N_BAND)
    ]

    def part(b, r, c):
        size = BANDS_DEV
        return totals[b][r * size : (r + 1) * size, c * size : (c + 1) * size]

    margin = {(b, b): part(b, 0, 0) for b in range(N_BAND)}
    margin[1, 0], margin[3, 2] = part(1, 0, 1), part(3, 0, 1)
    margin[2, 0] = part(0, 1, 0) + part(2, 1, 0).T
    margin[2, 1] = part(0, 1, 1) + part(3, 1, 1).T
    margin[3, 0] = part(1, 1, 1) + part(2, 1, 1).T
    margin[3, 1] = part(1, 1, 0) + part(3, 1, 0).T

    inverses, factor, whole = [], {}, {}
    for k in range(N_BAND):
        diagonal = inverse_of_block(margin[k, k])
        inverses.append(diagonal)
        for i in range(k + 1, N_BAND):
            factor[i, k] = exact_dot_t(margin[i, k], diagonal)
        for i in range(k + 1, N_BAND):
            for j in range(k + 1, i + 1):
                margin[i, j] = margin[i, j] - exact_dot_t(factor[i, k], factor[j, k])
        whole[k, k] = diagonal
        for j in range(k):
            total = exact_dot(factor[k, j], whole[j, j])
            for m in range(j + 1, k):
                total = total + exact_dot(factor[k, m], whole[m, j])
            whole[k, j] = -exact_dot(diagonal, total)
        if k == 2:
            second[0].wait()
            forward_second[0].start()
    padding = jnp.zeros((BANDS_DEV, LANES - BANDS_DEV), jnp.float32)
    for i in range(N_BAND):
        for j in range(N_BAND):
            if j <= i:
                inverse[i, j] = jnp.concatenate([whole[i, j], padding], axis=1)
            else:
                inverse[i, j] = jnp.zeros((BANDS_DEV, LANES), jnp.float32)
    panels = [inverse[band, source] for source in (band, mate, across, across_mate)]
    left = jnp.concatenate(
        [
            jnp.concatenate(panels, axis=1),
            jnp.concatenate([pltpu.roll(panel, HALF, 1) for panel in panels], axis=1),
        ],
        axis=0,
    )
    left_high, left_low = split(left)
    left = jnp.concatenate(
        [jnp.concatenate([left_high, left_high], axis=1), jnp.concatenate([left_low, left_low], axis=1)], axis=0
    )

    def rotate(i, carry):
        rows = block_rows(i)
        right = jnp.concatenate([ref[rows, :] for ref in (own, partner, cross, partner_cross)], axis=1)
        both = lax.dot_general(
            left,
            jnp.concatenate(split(right), axis=1),
            (((1,), (1,)), ((), ())),
            preferred_element_type=jnp.float32,
        )
        rotated = both[: 2 * BANDS_DEV] + both[2 * BANDS_DEV :]
        out[:, rows] = rotated[:BANDS_DEV]
        out[:, pl.ds(pl.multiple_of(PAIRS + i * BLOCK, BLOCK), BLOCK)] = rotated[BANDS_DEV:]
        return carry

    def rotate_piece(side, p):
        base = side * per_half + p * blocks
        lax.fori_loop(0, blocks, lambda i, carry: rotate(base + i, carry), 0)

    for p in pieces:
        forward_first[p].wait()
        rotate_piece(1 - chip, p)
        if p > 0:
            second[p].wait()
            forward_second[p].start()
    for p in pieces:
        forward_second[p].wait()
        rotate_piece(chip, p)


def finish(cells, table, owned_count):
    whole = pl.BlockSpec(memory_space=pltpu.VMEM)
    nodes = pltpu.VMEM((PAIRS, LANES), jnp.float32)

    def small(*shape):
        return pltpu.VMEM(shape, jnp.float32)

    def sems(slots):
        return pltpu.SemaphoreType.DMA((2, slots))

    return pl.pallas_call(
        functools.partial(finish_kernel, owned_count),
        out_shape=jax.ShapeDtypeStruct((BANDS_DEV, 2 * PAIRS), jnp.float32),
        in_specs=[pl.BlockSpec(memory_space=pltpu.MemorySpace.HBM), whole],
        out_specs=whole,
        scratch_shapes=[
            pltpu.SMEM(table.shape, jnp.int32),
            small(TILES, ROWS, LANES),
            small(2 * TILES * ROWS, LANES),
            nodes, nodes, nodes, nodes, nodes,
            small(LANES, LANES), small(PLANE_PEERS - 1, 8, LANES), small(8, LANES), small(8, LANES),
            small(PLANE_PEERS, N_BAND, 8, LANES),
            small(N_BAND, N_BAND, BANDS_DEV, LANES),
            pltpu.SemaphoreType.DMA(()),
            pltpu.SemaphoreType.DMA((CELL_PARTS,)),
            sems(2), sems(PIECES), sems(PIECES), sems(PIECES), sems(PIECES),
            sems(PLANE_PEERS - 1), sems(1), sems(3), sems(PLANE_PEERS - 1),
        ],
        compiler_params=pltpu.CompilerParams(
            collective_id=1, has_side_effects=True, vmem_limit_bytes=48 * 2**20
        ),
        name="finish",
    )(cells, table)


def shards(
    wavefunctions, stiffness, cell_scale, cell_potential, connectivity, lower_face, upper_face
):
    node_count = wavefunctions.shape[1]
    face_count = lower_face.shape[0]
    space_count = lax.axis_size("space")
    owned_count = node_count * space_count - face_count * (space_count - 1)

    index, keys, scale, potential, stiff = make_layout(connectivity, cell_scale, cell_potential, stiffness)
    cells, table = filter_cells(index, keys, wavefunctions, stiff, scale, potential)
    return finish(cells, table, owned_count)[:, :node_count]


def solution(mesh):
    placed = (
        P("band", "space"),
        P(),
        P("space"),
        P("space"),
        P(None, "space"),
        P("space"),
        P("space"),
    )
    return jax.shard_map(
        shards, mesh=mesh, in_specs=placed, out_specs=P("band", "space"), check_vma=False
    )
```
